32 devices in a mesh: dp: 8 (over z, x), mp: 4 (over y, core).
Axes of the slice: x: 2, y: 2, z: 4, core: 2. Of those that a mesh axis runs over, the one named last changes fastest.
Arguments:
- x_in: bfloat16 [1024, 1024], P('dp', 'mp'), may hold values from -90 to 90
- gain: float32 [1024], replicated, may hold values from 0.25 to 1.75
- w_in: bfloat16 [1024, 4096], P('mp'), may hold values from -0.5 to 0.5
- w_out: bfloat16 [1024, 4096], P('mp'), may hold values from -0.1875 to 0.1875
- grad_out: bfloat16 [1024, 1024], P('dp', 'mp'), may hold values from -6 to 6
- block_cols: int32 [4, 256], P('mp'), may hold values from 0 to 127, as said below
- slots: int32 [4, 256], P('mp'), may hold values from 0 to 511, as said below
Outputs:
- branch: bfloat16 [1024, 1024], P('dp', 'mp')
- grad_normed: bfloat16 [1024, 1024], P('dp', 'mp')
- owned_grad: float32 [4, 512, 4096], P('mp', 'dp')
The draws below stay inside these ranges and needn't reach their ends.
Inputs may be any that keep to these rules, and one draw needn't show every extreme that they name: Within one row of block_cols, the 16 entries k with the same k // 16 are distinct. The entries of one row of slots are distinct; slot s lies on index s // 64 of dp. In each row every index of dp holds at most 64 slots that are named, and some index holds exactly 64.
All inputs are finite; a program needn't handle non-finite values.
Results may differ from the reference program's by a relative error of at most 0.0062.
Values may be sent and summed in bfloat16 or wider, within the bound.
No kernel may reach another device: no remote copies, remote signals or barrier semaphores. Data moves between devices by JAX's collectives and lax.ppermute only.
A program may use at most 128 MiB of HBM per device.

```python
import math
import jax
import jax.numpy as jnp
from jax import lax

D = 1024
FF = 32768
BLK = 64
DENS = 8
TOK_DEV = 128
TOKENS = 1024
NRB = 16
NCB = 128
KB = 256
KR = 16
CAP = 64
N_DP = 8
N_MP = 4


def draw_x_in(key, part):
    key_base, key_cols, key_rows = jax.random.split(key, 3)
    column = jnp.arange(D, dtype=jnp.float32)
    rising = 1.0 + 2.0 * column / (D - 1)
    base = jax.random.truncated_normal(key_base, -4.0, 4.0, (TOKENS, D), jnp.float32)
    col_scale = jnp.exp(jax.random.uniform(key_cols, (1, D), jnp.float32, -1.2, 1.2))
    row_scale = jnp.exp(jax.random.uniform(key_rows, (TOKENS, 1), jnp.float32, -0.7, 0.7))
    return (base * col_scale * rising * row_scale).astype(jnp.bfloat16)


def draw_block_cols(key, part):

    def one_shard(shard_key):
        key_hot, key_score = jax.random.split(shard_key)
        hot = (jax.random.permutation(key_hot, NCB) < NCB // 8).astype(jnp.int32)
        scores = jax.random.randint(key_score, (NRB, NCB), 0, 65536) + hot[None, :] * 32768
        scores = scores * NCB + jnp.arange(NCB, dtype=jnp.int32)[None, :]
        chosen = lax.top_k(scores, KR)[1]
        return chosen.reshape(KB).astype(jnp.int32)
    return jax.vmap(one_shard)(jax.random.split(jax.random.fold_in(key, 11), N_MP))


def draw_slots(key, part):

    def one_shard(shard_key):
        key_busy, key_rest, key_order = jax.random.split(shard_key, 3)
        busy = jax.random.randint(key_busy, (), 0, N_DP)
        rest = jax.random.permutation(key_rest, (N_DP - 1) * CAP)[:KB - CAP]
        owner = rest // CAP
        owner = owner + (owner >= busy).astype(jnp.int32)
        placed = owner * CAP + rest % CAP
        full = busy * CAP + jnp.arange(CAP, dtype=jnp.int32)
        every = jnp.concatenate([full.astype(jnp.int32), placed.astype(jnp.int32)])
        order = jax.random.permutation(key_order, KB)
        return every[order].astype(jnp.int32)
    return jax.vmap(one_shard)(jax.random.split(jax.random.fold_in(key, 23), N_MP))


def steps_of(rng, extent, shards, low, high):
    level, own = 1.0, jax.random.fold_in(rng, 6)
    for position, blocks in shards:
        draws = jnp.exp(jax.random.uniform(jax.random.fold_in(own, position), (blocks,), jnp.float32, low / len(shards), high / len(shards)))
        level = level * jnp.repeat(draws, extent[position] // blocks).reshape([-1 if axis == position else 1 for axis in range(len(extent))])
    return level


def noise(key, dims, deviation, reach, shards=(), kind=jnp.bfloat16):
    result = jax.random.normal(key, dims, jnp.float32) * deviation
    if len(shards) > 0:
        result = steps_of(key, dims, shards, -0.22, 0.18) * result
    return jnp.clip(result, min=-reach, max=reach).astype(kind)


def setup_inputs(seed: int = 0) -> dict:
    key_list = jax.random.split(jax.random.key(seed), 8)
    return {
        "x_in": draw_x_in(jax.random.fold_in(key_list[7], 71), 0),
        "gain": jnp.clip(1.0 + 0.15 * jax.random.normal(key_list[1], (D,), jnp.float32), 0.25, 1.75),
        "w_in": noise(key_list[2], (N_MP * KB, BLK * BLK), (D // DENS) ** -0.5, 0.5, ((0, 4),)),
        "w_out": noise(key_list[3], (N_MP * KB, BLK * BLK), (FF // N_MP // DENS) ** -0.5, 0.1875, ((0, 4),)),
        "grad_out": noise(key_list[4], (TOKENS, D), 1.0, 6.0, ((0, 8), (1, 4))),
        "block_cols": draw_block_cols(jax.random.fold_in(key_list[7], 71), 0),
        "slots": draw_slots(jax.random.fold_in(key_list[7], 71), 0),
    }


norm_eps = 1e-06
tanh_coef = 0.7978845608028654

def gelu_value(pre_act):
    cubic = pre_act * pre_act * pre_act
    slope_arg = jnp.tanh(tanh_coef * (pre_act + 0.044715 * cubic))
    return 0.5 * pre_act * (1.0 + slope_arg)

def gelu_slope(pre_act):
    cubic = pre_act * pre_act * pre_act
    slope_arg = jnp.tanh(tanh_coef * (pre_act + 0.044715 * cubic))
    inner = tanh_coef * (1.0 + 0.134145 * pre_act * pre_act)
    return 0.5 * (1.0 + slope_arg) + 0.5 * pre_act * (1.0 - slope_arg * slope_arg) * inner

def reference(x_in, gain, w_in, w_out, grad_out, block_cols, slots):
    in_all = w_in.astype(jnp.float32).reshape(N_MP, NRB, KR, BLK, BLK)
    out_all = w_out.astype(jnp.float32).reshape(N_MP, NRB, KR, BLK, BLK)
    weight_scale = 1.0 / math.sqrt(TOKENS)

    def step(totals, inputs):
        x_block, grad_block = inputs
        x_float = x_block.astype(jnp.float32)
        inv_rms = lax.rsqrt(lax.optimization_barrier(jnp.mean(x_float * x_float, axis=-1, keepdims=True)) + norm_eps)
        normed = (x_float * inv_rms * gain).astype(jnp.bfloat16)
        normed_rows = normed.astype(jnp.float32).reshape(TOK_DEV, NRB, BLK)
        grad_rows = grad_block.astype(jnp.float32).reshape(TOK_DEV, NRB, BLK)
        branch = jnp.zeros((TOK_DEV, NRB, BLK), jnp.float32)
        normed_grad = jnp.zeros((TOK_DEV, NRB, BLK), jnp.float32)
        pieces = []
        for shard in range(N_MP):
            col_ids = block_cols[shard].astype(jnp.int32)
            in_blocks = in_all[shard]
            out_blocks = out_all[shard]
            pre_parts = jnp.einsum('trb,rkbc->rktc', normed_rows, in_blocks)
            pre_act = jax.ops.segment_sum(pre_parts.reshape(KB, TOK_DEV, BLK), col_ids, num_segments=NCB)
            activation = gelu_value(pre_act).astype(jnp.bfloat16)
            act_blocks = jnp.take(activation, col_ids, axis=0).astype(jnp.float32).reshape(NRB, KR, TOK_DEV, BLK)
            branch = branch + jnp.einsum('rktc,rkcb->trb', act_blocks, out_blocks)
            act_parts = jnp.einsum('trb,rkcb->rktc', grad_rows, out_blocks)
            grad_act = jax.ops.segment_sum(act_parts.reshape(KB, TOK_DEV, BLK), col_ids, num_segments=NCB)
            grad_pre = (grad_act * gelu_slope(pre_act)).astype(jnp.bfloat16)
            pre_blocks = jnp.take(grad_pre, col_ids, axis=0).astype(jnp.float32).reshape(NRB, KR, TOK_DEV, BLK)
            normed_grad = normed_grad + jnp.einsum('rktc,rkbc->trb', pre_blocks, in_blocks)
            pieces.append(jnp.einsum('trb,rktc->rkcb', normed_rows, pre_blocks).reshape(KB, BLK * BLK))
        totals = totals + jnp.stack(pieces) * weight_scale
        return (totals, (branch.reshape(TOK_DEV, D).astype(jnp.bfloat16), normed_grad.reshape(TOK_DEV, D).astype(jnp.bfloat16)))
    start_totals = jnp.zeros((N_MP, KB, BLK * BLK), jnp.float32)
    inputs = (x_in.reshape(N_DP, TOK_DEV, D), grad_out.reshape(N_DP, TOK_DEV, D))
    totals, outputs = lax.scan(step, start_totals, inputs)
    branch, grad_normed = outputs
    shard_ids = jnp.arange(N_MP, dtype=jnp.int32)[:, None]
    owned_grad = jnp.zeros((N_MP, N_DP * CAP, BLK * BLK), jnp.float32).at[shard_ids, slots.astype(jnp.int32)].set(totals)
    return (branch.reshape(TOKENS, D), grad_normed.reshape(TOKENS, D), owned_grad)
```

```python
import functools
import math

import jax
import jax.numpy as jnp
from jax import lax
from jax.experimental import pallas as pl
from jax.experimental.pallas import tpu as pltpu
from jax.sharding import PartitionSpec as P

FF = 32768
BLK = 64
HALF = BLK // 2
GROUP = 4


norm_eps = 1e-06
tanh_coef = 0.7978845608028654

F32 = jnp.float32
BF16 = jnp.bfloat16
MIB = 1024 * 1024


def gelu_value(pre_act):
    cubic = pre_act * pre_act * pre_act
    slope_arg = jnp.tanh(tanh_coef * (pre_act + 0.044715 * cubic))
    return 0.5 * pre_act * (1.0 + slope_arg)


def gelu_slope(pre_act):
    cubic = pre_act * pre_act * pre_act
    slope_arg = jnp.tanh(tanh_coef * (pre_act + 0.044715 * cubic))
    inner = tanh_coef * (1.0 + 0.134145 * pre_act * pre_act)
    return 0.5 * (1.0 + slope_arg) + 0.5 * pre_act * (1.0 - slope_arg * slope_arg) * inner


def gelu_both(v):
    square = v * v
    th = jnp.tanh(v * (tanh_coef + (tanh_coef * 0.044715) * square))
    gate = 0.5 + 0.5 * th
    inner = 2.0 * tanh_coef + (2.0 * tanh_coef * 0.134145) * square
    return v * gate, gate + v * (gate - gate * gate) * inner


def dot(a, b, dims=((1,), (0,))):
    return lax.dot_general(a, b, (dims, ((), ())), preferred_element_type=F32)


def iota(shape, axis):
    return lax.broadcasted_iota(jnp.int32, shape, axis)


def even_first(width):
    row, col = iota((width, width), 0), iota((width, width), 1)
    inside = row & (BLK - 1)
    target = (row - inside) + (inside & 1) * HALF + (inside >> 1)
    return jnp.where(col == target, 1.0, 0.0).astype(BF16)


def plan_kernel(cap, col_blocks, cols_ref, slots_ref, out_ref):
    kept = cols_ref.shape[1]
    me = lax.axis_index("dp")
    cols, slots = cols_ref[...], slots_ref[...]
    owner = lax.div(slots, jnp.int32(cap))
    eq = cols == iota((col_blocks, kept), 0)
    own = jnp.max(jnp.where(eq & (owner == me), 1.0, 0.0), axis=1, keepdims=True)
    peer = jnp.max(jnp.where(eq & (owner == (me ^ 1)), 1.0, 0.0), axis=1, keepdims=True)
    rank = jnp.where(peer > 0, jnp.where(own > 0, 1.0, 0.0), jnp.where(own > 0, 2.0, 3.0))
    key_c = rank * col_blocks + iota((col_blocks, 1), 0).astype(F32)
    eye = iota((col_blocks, col_blocks), 0) == iota((col_blocks, col_blocks), 1)
    key_r = jnp.sum(jnp.where(eye, key_c, 0.0), axis=0, keepdims=True)
    pos = jnp.sum(jnp.where(key_r < key_c, 1.0, 0.0), axis=1, keepdims=True)
    posk_r = jnp.sum(jnp.where(eq, pos, 0.0), axis=0, keepdims=True)
    eye_k = iota((kept, kept), 0) == iota((kept, kept), 1)

    def turn(row):
        return jnp.sum(jnp.where(eye_k, row, 0.0), axis=1, keepdims=True)

    k_r = iota((1, kept), 1).astype(F32)
    k_c = iota((kept, 1), 0).astype(F32)
    posk_c = turn(posk_r)
    slot_c = turn(slots.astype(F32))
    place = jnp.sum(
        jnp.where(posk_r * kept + k_r < posk_c * kept + k_c, 1.0, 0.0), axis=1, keepdims=True
    )
    hit = place == iota((kept, kept), 1).astype(F32)

    def pick(column):
        return jnp.sum(jnp.where(hit, column, 0.0), axis=0, keepdims=True)

    starts = jnp.sum(
        jnp.where(posk_c < GROUP * iota((kept, kept), 1).astype(F32), 1.0, 0.0),
        axis=0,
        keepdims=True,
    )

    def count(flags):
        return jnp.sum(jnp.where(flags, 1.0, 0.0), axis=0, keepdims=True)

    rows = [
        pick(k_c),
        pick(posk_c),
        pick(slot_c),
        starts,
        count(rank < 1),
        count(rank < 2),
        count(rank < 3),
        jnp.full((1, 1), 1, F32) * me.astype(F32),
    ]
    for index, row in enumerate(rows):
        out_ref[index : index + 1, :] = jnp.broadcast_to(row, (1, kept)).astype(jnp.int32)


def dense_kernel(per_row, plan, win_ref, wout_ref, din_ref, dout_ref, pin, pout):
    g = pl.program_id(0)
    lanes = 2 * BLK
    piece = 512

    @pl.when(g == 0)
    def _():
        row, col = iota((lanes, lanes), 0), iota((lanes, lanes), 1)
        swap = jnp.where(((col + BLK) & (lanes - 1)) == row, 1.0, 0.0).astype(BF16)
        same = jnp.where(col == row, 1.0, 0.0).astype(BF16)
        perm = even_first(lanes)
        perm_swap = dot(perm, swap).astype(BF16)
        left = jnp.concatenate([perm, perm_swap], axis=1)
        right = jnp.concatenate([same, swap], axis=1)

        def step(i, carry):
            at = pl.ds(pl.multiple_of(i * piece, piece), piece)
            pin[at, :] = dot(win_ref[at, :], left).astype(BF16)
            pout[at, :] = dot(wout_ref[at, :], right).astype(BF16)
            return carry

        lax.fori_loop(0, win_ref.shape[0] // piece, step, 0)

    din_ref[...] = jnp.zeros_like(din_ref)
    dout_ref[...] = jnp.zeros_like(dout_ref)
    side = iota((HALF, lanes), 1) // BLK
    masks = [jnp.where(side == h, 1.0, 0.0) for h in (0, 1)]

    def place(i, carry):
        k = plan[0, i]
        p = plan[1, i] - g * GROUP
        r = lax.div(k, jnp.int32(per_row))
        src = pl.ds(pl.multiple_of(k * HALF, HALF), HALF)
        for ref, parts, blk_row, blk_col in ((din_ref, pin, r, p), (dout_ref, pout, p, r)):
            h = blk_col & 1
            at_lane = pl.ds(pl.multiple_of((blk_col >> 1) * lanes, lanes), lanes)
            keep = jnp.where(h == 0, masks[0], masks[1]).astype(BF16)
            straight, swapped = parts[src, :lanes], parts[src, lanes:]
            for a in (0, 1):
                value = jnp.where(h == a, straight, swapped)
                at_row = pl.ds(pl.multiple_of(blk_row * BLK + a * HALF, HALF), HALF)
                ref[0, at_row, at_lane] = ref[0, at_row, at_lane] + value * keep
        return carry

    lax.fori_loop(plan[3, g], plan[3, g + 1], place, 0)


def load_tokens(pieces, tok, gain_ref, perm, n_s, np_s, g_s, base):
    mine = lax.axis_index("mp")
    width = pieces[0][0].shape[1]
    values, total = [], 0.0
    for ref, first in pieces:
        value = ref[first : first + tok, :].astype(F32)
        values.append(value)
        total = total + jnp.sum(value * value, axis=-1, keepdims=True)
    inv_rms = lax.rsqrt(total / (width * len(pieces)) + norm_eps)
    for q, (ref, first) in enumerate(pieces):
        at = pl.ds(pl.multiple_of((mine ^ q) * width, width), width)
        normed = (values[q] * inv_rms * gain_ref[:, at]).astype(BF16)
        rows = slice(base, base + tok)
        if n_s is not None:
            n_s[rows, at] = normed
        np_s[rows, at] = dot(normed, perm).astype(BF16)
        g_s[rows, at] = ref[first + tok : first + 2 * tok, :]


def local_kernel(gain_ref, s0, s1, s2, s3, din_ref, dout_ref, o0, o1, o2, o3, np_s, g_s, acc_b, acc_n):
    g = pl.program_id(0)
    width = s0.shape[1]
    tok = s0.shape[0] // 2

    @pl.when(g == 0)
    def _():
        pieces = [(ref, 0) for ref in (s0, s1, s2, s3)]
        load_tokens(pieces, tok, gain_ref, even_first(width), None, np_s, g_s, 0)
        acc_b[...] = jnp.zeros_like(acc_b)
        acc_n[...] = jnp.zeros_like(acc_n)

    w_in, w_out = din_ref[0], dout_ref[0]
    pre_act = dot(np_s[...], w_in)
    grad_act = dot(g_s[...], w_out, ((1,), (1,)))
    value, slope = gelu_both(pre_act)
    acc_b[...] += dot(value.astype(BF16), w_out)
    acc_n[...] += dot((grad_act * slope).astype(BF16), w_in, ((1,), (1,)))

    @pl.when(g == pl.num_programs(0) - 1)
    def _():
        mine = lax.axis_index("mp")
        perm = even_first(width)
        for q, out in enumerate((o0, o1, o2, o3)):
            at = pl.ds(pl.multiple_of((mine ^ q) * width, width), width)
            out[:tok, :] = acc_b[:, at].astype(BF16)
            out[tok:, :] = dot(acc_n[:, at].astype(BF16), perm, ((1,), (1,))).astype(BF16)


def group_range(plan, for_peer):
    if for_peer:
        return 0, (plan[5, 0] + GROUP - 1) // GROUP
    return plan[4, 0] // GROUP, (plan[6, 0] + GROUP - 1) // GROUP


def block_kernel(
    for_peer, per_row, cap, scale, plan, gain_ref, s0, s1, s2, s3, z0, z1, z2, z3, din_ref, dout_ref,
    out_ref, n_s, np_s, g_s, big
):
    i = pl.program_id(0)
    width = s0.shape[1]
    tok = s0.shape[0] // 2
    lanes = 2 * BLK
    first, last = group_range(plan, for_peer)

    @pl.when(i == 0)
    def _():
        perm = even_first(width)
        load_tokens([(ref, 0) for ref in (s0, s1, s2, s3)], tok, gain_ref, perm, n_s, np_s, g_s, 0)
        for j in range(z0.shape[0] // (2 * tok)):
            pieces = [(ref, 2 * tok * j) for ref in (z0, z1, z2, z3)]
            load_tokens(pieces, tok, gain_ref, perm, n_s, np_s, g_s, (j + 1) * tok)
        out_ref[...] = jnp.zeros_like(out_ref)

    g = first + i

    @pl.when(g < last)
    def _():
        w_in, w_out = din_ref[0], dout_ref[0]
        pre_act = dot(np_s[...], w_in)
        grad_act = dot(g_s[...], w_out, ((1,), (1,)))
        _, slope = gelu_both(pre_act)
        grad_pre = (grad_act * slope).astype(BF16)
        big[...] = dot(grad_pre, n_s[...], ((0,), (0,))) * scale
        target = plan[7, 0] ^ 1 if for_peer else plan[7, 0]
        left = iota((HALF, lanes), 1) < BLK

        def take(e, carry):
            slot = plan[2, e] - target * cap

            @pl.when((slot >= 0) & (slot < cap))
            def _():
                k = plan[0, e]
                r = lax.div(k, jnp.int32(per_row))
                row = (plan[1, e] - g * GROUP) * BLK
                at_lane = pl.ds(pl.multiple_of((r >> 1) * lanes, lanes), lanes)
                top = big[pl.ds(pl.multiple_of(row, BLK), HALF), at_lane]
                low = big[pl.ds(pl.multiple_of(row + HALF, HALF), HALF), at_lane]
                odd = (r & 1) == 1
                top = jnp.where(odd, pltpu.roll(top, BLK, 1), top)
                low = jnp.where(odd, low, pltpu.roll(low, BLK, 1))
                out_ref[slot] = jnp.where(left, top, low).astype(out_ref.dtype)

            return carry

        lax.fori_loop(plan[3, g], plan[3, g + 1], take, 0)


def fast_body(x_in, gain, w_in, w_out, grad_out, block_cols, slots):
    dp_count, mp_count = lax.axis_size("dp"), lax.axis_size("mp")
    tok, width = x_in.shape
    feat = width * mp_count
    kept = w_in.shape[0]
    row_blocks = feat // BLK
    per_row = kept // row_blocks
    hidden = FF // mp_count
    col_blocks = hidden // BLK
    groups = col_blocks // GROUP
    wide = GROUP * BLK
    lanes = 2 * BLK
    cap = 2 * kept // dp_count
    scale = 1.0 / math.sqrt(tok * dp_count)
    across_x = [(i, i ^ 1) for i in range(dp_count)]
    near = [[(i, i ^ q) for i in range(mp_count)] for q in range(mp_count)]
    z_count = dp_count // 2
    along_z = [
        [(((z + j) % z_count) * 2 + x, z * 2 + x) for z in range(z_count) for x in range(2)]
        for j in range(z_count)
    ]

    own = jnp.concatenate([x_in, grad_out], axis=0)
    gathered = [own] + [lax.ppermute(own, "mp", near[q]) for q in range(1, mp_count)]
    column = jnp.concatenate(
        [lax.ppermute(own, "dp", along_z[j]) for j in range(1, z_count)], axis=0
    )
    column_y = lax.ppermute(column, "mp", near[2])
    columns = [
        column,
        lax.ppermute(column, "mp", near[1]),
        column_y,
        lax.ppermute(column_y, "mp", near[1]),
    ]
    gain_row = gain.reshape(1, feat)

    plan = pl.pallas_call(
        functools.partial(plan_kernel, cap, col_blocks),
        out_shape=jax.ShapeDtypeStruct((8, kept), jnp.int32),
        cost_estimate=pl.CostEstimate(flops=4_000_000, bytes_accessed=16384, transcendentals=0),
        name="plan",
    )(block_cols, slots)

    in_flat = w_in.reshape(kept * HALF, lanes)
    out_flat = w_out.reshape(kept * HALF, lanes)
    whole = pl.BlockSpec(memory_space=pltpu.VMEM)
    dense_in, dense_out = pl.pallas_call(
        functools.partial(dense_kernel, per_row),
        out_shape=(
            jax.ShapeDtypeStruct((groups, feat, wide), BF16),
            jax.ShapeDtypeStruct((groups, wide, feat), BF16),
        ),
        grid_spec=pltpu.PrefetchScalarGridSpec(
            num_scalar_prefetch=1,
            grid=(groups,),
            in_specs=[whole, whole],
            out_specs=[
                pl.BlockSpec((1, feat, wide), lambda g, plan: (g, 0, 0)),
                pl.BlockSpec((1, wide, feat), lambda g, plan: (g, 0, 0)),
            ],
            scratch_shapes=[pltpu.VMEM((kept * HALF, 2 * lanes), BF16)] * 2,
        ),
        compiler_params=pltpu.CompilerParams(vmem_limit_bytes=40 * MIB),
        cost_estimate=pl.CostEstimate(
            flops=4 * kept * HALF * lanes * 2 * lanes,
            bytes_accessed=4 * hidden * feat + 4 * kept * HALF * lanes,
            transcendentals=0,
        ),
        name="dense",
    )(plan, in_flat, out_flat)

    parts = pl.pallas_call(
        local_kernel,
        out_shape=[jax.ShapeDtypeStruct((2 * tok, width), BF16)] * mp_count,
        grid_spec=pltpu.PrefetchScalarGridSpec(
            num_scalar_prefetch=0,
            grid=(groups,),
            in_specs=[whole] * 5
            + [
                pl.BlockSpec((1, feat, wide), lambda g: (g, 0, 0)),
                pl.BlockSpec((1, wide, feat), lambda g: (g, 0, 0)),
            ],
            out_specs=[whole] * mp_count,
            scratch_shapes=[
                pltpu.VMEM((tok, feat), BF16),
                pltpu.VMEM((tok, feat), BF16),
                pltpu.VMEM((tok, feat), F32),
                pltpu.VMEM((tok, feat), F32),
            ],
        ),
        compiler_params=pltpu.CompilerParams(vmem_limit_bytes=40 * MIB),
        cost_estimate=pl.CostEstimate(
            flops=8 * tok * feat * hidden,
            bytes_accessed=4 * hidden * feat,
            transcendentals=tok * hidden,
        ),
        name="local",
    )(gain_row, *gathered, dense_in, dense_out)

    rows = tok * z_count
    steps = cap // GROUP + 1

    def blocks(for_peer):
        def index(i, plan):
            first, last = group_range(plan, for_peer)
            return (jnp.maximum(jnp.minimum(first + i, last - 1), 0), 0, 0)

        return pl.pallas_call(
            functools.partial(block_kernel, for_peer, per_row, cap, scale),
            out_shape=jax.ShapeDtypeStruct((cap, HALF, lanes), BF16 if for_peer else F32),
            grid_spec=pltpu.PrefetchScalarGridSpec(
                num_scalar_prefetch=1,
                grid=(steps,),
                in_specs=[whole] * 9
                + [pl.BlockSpec((1, feat, wide), index), pl.BlockSpec((1, wide, feat), index)],
                out_specs=whole,
                scratch_shapes=[
                    pltpu.VMEM((rows, feat), BF16),
                    pltpu.VMEM((rows, feat), BF16),
                    pltpu.VMEM((rows, feat), BF16),
                    pltpu.VMEM((wide, feat), F32),
                ],
            ),
            compiler_params=pltpu.CompilerParams(vmem_limit_bytes=40 * MIB),
            cost_estimate=pl.CostEstimate(
                flops=6 * rows * feat * wide * steps // 2,
                bytes_accessed=2 * hidden * feat,
                transcendentals=rows * wide * steps // 2,
            ),
            name="blocks_peer" if for_peer else "blocks_own",
        )(plan, gain_row, *gathered, *columns, dense_in, dense_out)

    arrived = lax.ppermute(blocks(True), "dp", across_x)
    summed = [parts[0]] + [lax.ppermute(parts[q], "mp", near[q]) for q in range(1, mp_count)]
    total = sum(part.astype(F32) for part in summed)
    branch, grad_normed = total[:tok].astype(BF16), total[tok:].astype(BF16)
    owned_grad = (blocks(False) + arrived.astype(F32)).reshape(cap, BLK * BLK)
    return (branch, grad_normed, owned_grad[None])


def sum_sources(received):
    return jnp.sum(received, axis=0)


def body(x_in, gain, w_in, w_out, grad_out, block_cols, slots):
    whole_x, whole_grad = (
        lax.all_gather(x_in, "mp", axis=1, tiled=True),
        lax.all_gather(grad_out, "mp", axis=1, tiled=True),
    )
    tok_rows = whole_x.shape[0]
    feat_width = whole_x.shape[1]
    row_blocks = feat_width // BLK
    kept_count = w_in.shape[0]
    per_row = kept_count // row_blocks
    col_blocks = FF // lax.axis_size("mp") // BLK
    col_ids = block_cols[0]
    slot_ids = slots[0]
    x_float = whole_x.astype(jnp.float32)
    inv_rms = lax.rsqrt(jnp.mean(x_float * x_float, axis=-1, keepdims=True) + norm_eps)
    normed = (x_float * inv_rms * gain).astype(jnp.bfloat16)
    normed_cols = normed.reshape(tok_rows, row_blocks, BLK).transpose(1, 2, 0)
    grad_cols = whole_grad.reshape(tok_rows, row_blocks, BLK).transpose(1, 2, 0)
    in_blocks = w_in.reshape(row_blocks, per_row, BLK, BLK)
    out_blocks = w_out.reshape(row_blocks, per_row, BLK, BLK)
    col_onehot = (col_ids[None, :] == jnp.arange(col_blocks, dtype=jnp.int32)[:, None]).astype(
        jnp.float32
    )
    pre_parts = jnp.einsum(
        "rkbc,rbt->rkct", in_blocks, normed_cols, preferred_element_type=jnp.float32
    )
    pre_act = jnp.dot(
        col_onehot,
        pre_parts.reshape(kept_count, BLK * tok_rows),
        precision=lax.Precision.HIGHEST,
        preferred_element_type=jnp.float32,
    )
    pre_act = pre_act.reshape(col_blocks, BLK, tok_rows)
    activation = gelu_value(pre_act).astype(jnp.bfloat16)
    act_blocks = jnp.take(activation, col_ids, axis=0).reshape(row_blocks, per_row, BLK, tok_rows)
    branch_cols = jnp.einsum(
        "rkcb,rkct->rbt", out_blocks, act_blocks, preferred_element_type=jnp.float32
    )
    branch_part = branch_cols.transpose(2, 0, 1).reshape(tok_rows, feat_width)
    branch = lax.psum_scatter(branch_part, "mp", scatter_dimension=1, tiled=True).astype(
        jnp.bfloat16
    )
    act_parts = jnp.einsum(
        "rkcb,rbt->rkct", out_blocks, grad_cols, preferred_element_type=jnp.float32
    )
    grad_act = jnp.dot(
        col_onehot,
        act_parts.reshape(kept_count, BLK * tok_rows),
        precision=lax.Precision.HIGHEST,
        preferred_element_type=jnp.float32,
    )
    grad_act = grad_act.reshape(col_blocks, BLK, tok_rows)
    grad_pre = (grad_act * gelu_slope(pre_act)).astype(jnp.bfloat16)
    pre_blocks = jnp.take(grad_pre, col_ids, axis=0).reshape(row_blocks, per_row, BLK, tok_rows)
    dp_count = lax.axis_size("dp")
    weight_scale = 1.0 / math.sqrt(tok_rows * dp_count)
    block_terms = jnp.einsum(
        "rkct,rbt->rkcb", pre_blocks, normed_cols, preferred_element_type=jnp.float32
    )
    block_partial = (block_terms * weight_scale).reshape(kept_count, BLK * BLK)
    capacity = 2 * kept_count // dp_count
    outgoing = (
        jnp.zeros((dp_count * capacity, BLK * BLK), jnp.float32).at[slot_ids].set(block_partial)
    )
    outgoing = outgoing.reshape(dp_count, capacity, BLK * BLK)
    owned_grad = sum_sources(
        lax.all_to_all(
            outgoing.astype(jnp.bfloat16), "dp", split_axis=0, concat_axis=0, tiled=True
        ).astype(outgoing.dtype)
    )
    normed_part = jnp.einsum(
        "rkbc,rkct->rbt", in_blocks, pre_blocks, preferred_element_type=jnp.float32
    )
    normed_part = normed_part.transpose(2, 0, 1).reshape(tok_rows, feat_width)
    grad_normed = lax.psum_scatter(normed_part, "mp", scatter_dimension=1, tiled=True).astype(
        jnp.bfloat16
    )
    return (branch, grad_normed, owned_grad[None])


def solution(mesh):
    placed = (
        P("dp", "mp"),
        P(),
        P("mp", None),
        P("mp", None),
        P("dp", "mp"),
        P("mp", None),
        P("mp", None),
    )
    fits = mesh.shape["dp"] == 8 and mesh.shape["mp"] == 4
    return jax.shard_map(
        fast_body if fits else body,
        mesh=mesh,
        in_specs=placed,
        out_specs=(P("dp", "mp"), P("dp", "mp"), P("mp", "dp", None)),
        check_vma=False,
    )
```

```python
import functools
import math

import jax
import jax.numpy as jnp
from jax import lax
from jax.experimental import pallas as pl
from jax.experimental.pallas import tpu as pltpu
from jax.sharding import PartitionSpec as P

FF = 32768
BLK = 64
HALF = BLK // 2
GROUP = 4


norm_eps = 1e-06
tanh_coef = 0.7978845608028654

F32 = jnp.float32
BF16 = jnp.bfloat16
MIB = 1024 * 1024


def gelu_value(pre_act):
    cubic = pre_act * pre_act * pre_act
    slope_arg = jnp.tanh(tanh_coef * (pre_act + 0.044715 * cubic))
    return 0.5 * pre_act * (1.0 + slope_arg)


def gelu_slope(pre_act):
    cubic = pre_act * pre_act * pre_act
    slope_arg = jnp.tanh(tanh_coef * (pre_act + 0.044715 * cubic))
    inner = tanh_coef * (1.0 + 0.134145 * pre_act * pre_act)
    return 0.5 * (1.0 + slope_arg) + 0.5 * pre_act * (1.0 - slope_arg * slope_arg) * inner


def gelu_both(v):
    square = v * v
    th = jnp.tanh(v * (tanh_coef + (tanh_coef * 0.044715) * square))
    gate = 0.5 + 0.5 * th
    inner = 2.0 * tanh_coef + (2.0 * tanh_coef * 0.134145) * square
    return v * gate, gate + v * (gate - gate * gate) * inner


def dot(a, b, dims=((1,), (0,))):
    return lax.dot_general(a, b, (dims, ((), ())), preferred_element_type=F32)


def iota(shape, axis):
    return lax.broadcasted_iota(jnp.int32, shape, axis)


def even_first(width):
    row, col = iota((width, width), 0), iota((width, width), 1)
    inside = row & (BLK - 1)
    target = (row - inside) + (inside & 1) * HALF + (inside >> 1)
    return jnp.where(col == target, 1.0, 0.0).astype(BF16)


def plan_kernel(cap, col_blocks, cols_ref, slots_ref, out_ref):
    kept = cols_ref.shape[1]
    me = lax.axis_index("dp")
    cols, slots = cols_ref[...], slots_ref[...]
    owner = lax.div(slots, jnp.int32(cap))
    eq = cols == iota((col_blocks, kept), 0)
    own = jnp.where(owner == me, 1.0, 0.0)
    peer = jnp.where(owner == (me ^ 1), 1.0, 0.0)
    needed = jnp.max(jnp.where(eq, own + peer, 0.0), axis=1, keepdims=True)

    def listed(flags_r, flags_c):
        size = flags_r.shape[1]
        before = iota((size, size), 1) < iota((size, size), 0)
        place = jnp.sum(jnp.where(before, flags_r, 0.0), axis=1, keepdims=True)
        hit = (place == iota((size, kept), 1).astype(F32)) & (flags_c > 0)
        index = iota((size, 1), 0).astype(F32)
        row = jnp.sum(jnp.where(hit, index, 0.0), axis=0, keepdims=True)
        return row, jnp.sum(flags_r, axis=1, keepdims=True)

    def to_column(row):
        size = row.shape[1]
        eye = iota((size, size), 0) == iota((size, size), 1)
        return jnp.sum(jnp.where(eye, row, 0.0), axis=1, keepdims=True)

    def to_row(column):
        size = column.shape[0]
        eye = iota((size, size), 0) == iota((size, size), 1)
        return jnp.sum(jnp.where(eye, column, 0.0), axis=0, keepdims=True)

    peer_list, peer_count = listed(peer, to_column(peer))
    own_list, own_count = listed(own, to_column(own))
    need_list, need_count = listed(to_row(needed), needed)
    rows = [
        cols.astype(F32),
        (slots - owner * cap).astype(F32),
        peer_list,
        own_list,
        need_list,
        peer_count,
        own_count,
        need_count,
    ]
    for index, row in enumerate(rows):
        out_ref[index : index + 1, :] = jnp.broadcast_to(row, (1, kept)).astype(jnp.int32)


def prepare_kernel(win_ref, wout_ref, a_in, b_in, p_out, a_out, order):
    per_row, length = win_ref.shape
    lanes = 2 * BLK
    rows = per_row * HALF

    @pl.when(pl.program_id(0) == 0)
    def _():
        row, col = iota((rows, rows), 0), iota((rows, rows), 1)
        source = (row & (HALF - 1)) * per_row + lax.div(row, jnp.int32(HALF))
        order[...] = jnp.where(col == source, 1.0, 0.0).astype(BF16)

    row, col = iota((lanes, lanes), 0), iota((lanes, lanes), 1)
    swap = jnp.where(((col + BLK) & (lanes - 1)) == row, 1.0, 0.0).astype(BF16)
    perm = even_first(lanes)
    both = jnp.concatenate([perm, dot(perm, swap).astype(BF16)], axis=1)

    def by_block(ref):
        stacked = jnp.concatenate(
            [ref[:, j * lanes : (j + 1) * lanes] for j in range(length // lanes)], axis=0
        )
        return dot(order[...], stacked).astype(BF16)

    kept_in = dot(by_block(win_ref), both).astype(BF16)
    kept_out = by_block(wout_ref)
    p_out[0] = kept_out
    left = iota((HALF, lanes), 1) < BLK
    for pair in range(per_row // 2):
        first = kept_in[2 * pair * HALF : (2 * pair + 1) * HALF].astype(F32)
        second = kept_in[(2 * pair + 1) * HALF : (2 * pair + 2) * HALF].astype(F32)
        at = slice(pair * lanes, (pair + 1) * lanes)
        b_in[0, :HALF, at] = jnp.where(left, first[:, :lanes], second[:, lanes:]).astype(BF16)
        b_in[0, HALF:, at] = jnp.where(left, first[:, lanes:], second[:, :lanes]).astype(BF16)
    for quad in range(per_row // GROUP):
        rows_of = slice(quad * lanes, (quad + 1) * lanes)
        turned = kept_in[rows_of, :lanes].T
        a_in[0, quad * BLK : (quad + 1) * BLK, :lanes] = turned[:BLK]
        a_in[0, quad * BLK : (quad + 1) * BLK, lanes:] = turned[BLK:]
        turned = kept_out[rows_of].T
        a_out[0, :, rows_of] = turned[:BLK]
        a_out[0, :, rows + quad * lanes : rows + (quad + 1) * lanes] = turned[BLK:]


def load_tokens(pieces, tok, gain_ref, perm, n_s, nt_s, gt_s, base):
    mine = lax.axis_index("mp")
    width = pieces[0][0].shape[1]
    values, total = [], 0.0
    for ref, first in pieces:
        value = ref[first : first + tok, :].astype(F32)
        values.append(value)
        total = total + jnp.sum(value * value, axis=-1, keepdims=True)
    inv_rms = lax.rsqrt(total / (width * len(pieces)) + norm_eps)
    for q, (ref, first) in enumerate(pieces):
        at = pl.ds(pl.multiple_of((mine ^ q) * width, width), width)
        normed = (values[q] * inv_rms * gain_ref[:, at]).astype(BF16)
        n_s[base : base + tok, at] = normed
        nt_s[at, :] = dot(normed, perm).astype(BF16).T
        gt_s[at, :] = ref[first + tok : first + 2 * tok, :].T


def expand(plan, a_in, p_out, nt_s, gt_s, acc_v, acc_a):
    row_blocks = a_in.shape[0]
    tok = nt_s.shape[1]
    per_row = p_out.shape[1] // HALF
    acc_v[...] = jnp.zeros_like(acc_v)
    acc_a[...] = jnp.zeros_like(acc_a)
    gap = jnp.zeros((HALF, tok), BF16)
    gap2 = jnp.zeros((BLK, tok), BF16)

    def step(r, carry):
        at = pl.ds(pl.multiple_of(r * BLK, BLK), BLK)
        normed, cot = nt_s[at, :], gt_s[at, :]
        spread = []
        for a in (0, 1):
            part = normed[a * HALF : (a + 1) * HALF]
            for u in range(GROUP):
                spread.append(
                    jnp.concatenate([part if v == u else gap for v in range(GROUP)], axis=1)
                )
        terms_v = dot(a_in[r], jnp.concatenate(spread, axis=0))
        cots = jnp.concatenate(
            [jnp.concatenate([cot, gap2], axis=1), jnp.concatenate([gap2, cot], axis=1)], axis=0
        )
        terms_a = dot(p_out[r], cots)
        for quad in range(per_row // GROUP):
            new = []
            for u in range(GROUP):
                k = quad * GROUP + u
                c = plan[0, r * per_row + k]
                v = acc_v[c] + terms_v[quad * BLK : (quad + 1) * BLK, u * tok : (u + 1) * tok]
                rows = terms_a[k * HALF : (k + 1) * HALF]
                a = acc_a[c] + jnp.concatenate([rows[:, :tok], rows[:, tok:]], axis=0)
                new.append((c, v, a))
            for c, v, a in new:
                acc_v[c] = v
                acc_a[c] = a
        return carry

    lax.fori_loop(0, row_blocks, step, 0)


def local_kernel(
    plan, gain_ref, s0, s1, s2, s3, a_in, b_in, p_out, a_out, o0, o1, o2, o3, gp_ref, n_ref,
    nt_s, gt_s, acc_v, acc_a, act_s, br_s, gn_s
):
    width = s0.shape[1]
    tok = s0.shape[0] // 2
    row_blocks, per_row = a_in.shape[0], p_out.shape[1] // HALF
    col_blocks = acc_v.shape[0]
    perm = even_first(width)
    load_tokens([(ref, 0) for ref in (s0, s1, s2, s3)], tok, gain_ref, perm, n_ref, nt_s, gt_s, 0)
    expand(plan, a_in, p_out, nt_s, gt_s, acc_v, acc_a)

    def bend(c, carry):
        value, slope = gelu_both(acc_v[c])
        act_s[c] = value.astype(BF16)
        gp_ref[c] = (acc_a[c] * slope).astype(BF16)
        return carry

    lax.fori_loop(0, col_blocks, bend, 0, unroll=2)

    def contract(r, carry):
        at = pl.ds(pl.multiple_of(r * BLK, BLK), BLK)
        ids = [plan[0, r * per_row + k] for k in range(per_row)]
        acts = [act_s[c, a * HALF : (a + 1) * HALF, :] for a in (0, 1) for c in ids]
        br_s[at, :] = dot(a_out[r], jnp.concatenate(acts, axis=0)).astype(BF16)
        grads = [gp_ref[c] for c in ids]
        gn_s[at, :] = dot(b_in[r], jnp.concatenate(grads, axis=0)).astype(BF16)
        return carry

    lax.fori_loop(0, row_blocks, contract, 0)
    mine = lax.axis_index("mp")
    for q, out in enumerate((o0, o1, o2, o3)):
        at = pl.ds(pl.multiple_of((mine ^ q) * width, width), width)
        out[:tok, :] = br_s[at, :].T
        out[tok:, :] = dot(gn_s[at, :].T, perm, ((1,), (1,))).astype(BF16)


def block_kernel(
    scale, plan, gain_ref, z0, z1, z2, z3, a_in, p_out, gp_own, n_own, peer_ref, own_ref,
    n_s, nt_s, gt_s, acc_v, acc_a, gp_s
):
    tok = n_own.shape[0]
    per_row = p_out.shape[1] // HALF
    lanes = 2 * BLK
    perm = even_first(z0.shape[1])
    n_s[:tok, :] = n_own[...]

    def keep(i, carry):
        c = plan[4, i]
        gp_s[c, :, :tok] = gp_own[c]
        return carry

    lax.fori_loop(0, plan[7, 0], keep, 0)
    for j in range(z0.shape[0] // (2 * tok)):
        pieces = [(ref, 2 * tok * j) for ref in (z0, z1, z2, z3)]
        load_tokens(pieces, tok, gain_ref, perm, n_s, nt_s, gt_s, (j + 1) * tok)
        expand(plan, a_in, p_out, nt_s, gt_s, acc_v, acc_a)

        def bend(i, carry):
            c = plan[4, i]
            _, slope = gelu_both(acc_v[c])
            gp_s[c, :, (j + 1) * tok : (j + 2) * tok] = (acc_a[c] * slope).astype(BF16)
            return carry

        lax.fori_loop(0, plan[7, 0], bend, 0)

    left = iota((HALF, lanes), 1) < BLK
    for out_ref, list_row, count_row in ((peer_ref, 2, 5), (own_ref, 3, 6)):
        out_ref[...] = jnp.zeros_like(out_ref)
        count = plan[count_row, 0]

        def outer(i, carry):
            done = []
            for u in range(GROUP):
                k = plan[list_row, jnp.minimum(i * GROUP + u, count - 1)]
                r = lax.div(k, jnp.int32(per_row))
                at_lane = pl.ds(pl.multiple_of((r >> 1) * lanes, lanes), lanes)
                block = dot(gp_s[plan[0, k]], n_s[:, at_lane]) * scale
                odd = (r & 1) == 1
                top, low = block[:HALF], block[HALF:]
                top = jnp.where(odd, pltpu.roll(top, BLK, 1), top)
                low = jnp.where(odd, low, pltpu.roll(low, BLK, 1))
                done.append((plan[1, k], jnp.where(left, top, low).astype(out_ref.dtype)))
            for slot, value in done:
                out_ref[slot] = value
            return carry

        lax.fori_loop(0, (count + GROUP - 1) // GROUP, outer, 0)


def fast_body(x_in, gain, w_in, w_out, grad_out, block_cols, slots):
    dp_count, mp_count = lax.axis_size("dp"), lax.axis_size("mp")
    tok, width = x_in.shape
    feat = width * mp_count
    kept = w_in.shape[0]
    row_blocks = feat // BLK
    per_row = kept // row_blocks
    hidden = FF // mp_count
    col_blocks = hidden // BLK
    lanes = 2 * BLK
    cap = 2 * kept // dp_count
    scale = 1.0 / math.sqrt(tok * dp_count)
    across_x = [(i, i ^ 1) for i in range(dp_count)]
    near = [[(i, i ^ q) for i in range(mp_count)] for q in range(mp_count)]
    z_count = dp_count // 2
    along_z = [
        [(((z + j) % z_count) * 2 + x, z * 2 + x) for z in range(z_count) for x in range(2)]
        for j in range(z_count)
    ]

    own = jnp.concatenate([x_in, grad_out], axis=0)
    gathered = [own] + [lax.ppermute(own, "mp", near[q]) for q in range(1, mp_count)]
    column = jnp.concatenate(
        [lax.ppermute(own, "dp", along_z[j]) for j in range(1, z_count)], axis=0
    )
    column_y = lax.ppermute(column, "mp", near[2])
    columns = [
        column,
        lax.ppermute(column, "mp", near[1]),
        column_y,
        lax.ppermute(column_y, "mp", near[1]),
    ]
    gain_row = gain.reshape(1, feat)
    whole = pl.BlockSpec(memory_space=pltpu.VMEM)
    mm = 2 * tok * kept * BLK * BLK

    plan = pl.pallas_call(
        functools.partial(plan_kernel, cap, col_blocks),
        out_shape=jax.ShapeDtypeStruct((8, kept), jnp.int32),
        cost_estimate=pl.CostEstimate(flops=4_000_000, bytes_accessed=16384, transcendentals=0),
        name="plan",
    )(block_cols, slots)

    shapes = [
        (per_row // GROUP * BLK, 2 * lanes),
        (BLK, per_row * BLK),
        (per_row * HALF, lanes),
        (BLK, per_row * BLK),
    ]
    a_in, b_in, p_out, a_out = pl.pallas_call(
        prepare_kernel,
        out_shape=[jax.ShapeDtypeStruct((row_blocks, *shape), BF16) for shape in shapes],
        grid=(row_blocks,),
        in_specs=[pl.BlockSpec((per_row, BLK * BLK), lambda r: (r, 0))] * 2,
        out_specs=[pl.BlockSpec((1, *shape), lambda r: (r, 0, 0)) for shape in shapes],
        scratch_shapes=[pltpu.VMEM((per_row * HALF, per_row * HALF), BF16)],
        compiler_params=pltpu.CompilerParams(vmem_limit_bytes=24 * MIB),
        cost_estimate=pl.CostEstimate(
            flops=8 * mm, bytes_accessed=12 * kept * BLK * BLK, transcendentals=0
        ),
        name="prepare",
    )(w_in, w_out)

    hidden_f32 = pltpu.VMEM((col_blocks, BLK, tok), F32)
    turned = pltpu.VMEM((feat, tok), BF16)
    *parts, gp_own, n_own = pl.pallas_call(
        local_kernel,
        out_shape=[jax.ShapeDtypeStruct((2 * tok, width), BF16)] * mp_count
        + [
            jax.ShapeDtypeStruct((col_blocks, BLK, tok), BF16),
            jax.ShapeDtypeStruct((tok, feat), BF16),
        ],
        grid_spec=pltpu.PrefetchScalarGridSpec(
            num_scalar_prefetch=1,
            grid=(),
            in_specs=[whole] * 9,
            out_specs=[whole] * (mp_count + 2),
            scratch_shapes=[
                turned,
                turned,
                hidden_f32,
                hidden_f32,
                pltpu.VMEM((col_blocks, BLK, tok), BF16),
                turned,
                turned,
            ],
        ),
        compiler_params=pltpu.CompilerParams(vmem_limit_bytes=32 * MIB),
        cost_estimate=pl.CostEstimate(
            flops=16 * mm,
            bytes_accessed=10 * kept * BLK * BLK,
            transcendentals=tok * hidden,
        ),
        name="local",
    )(plan, gain_row, *gathered, a_in, b_in, p_out, a_out)

    rows = tok * z_count
    for_peer, for_own = pl.pallas_call(
        functools.partial(block_kernel, scale),
        out_shape=[
            jax.ShapeDtypeStruct((cap, HALF, lanes), BF16),
            jax.ShapeDtypeStruct((cap, HALF, lanes), F32),
        ],
        grid_spec=pltpu.PrefetchScalarGridSpec(
            num_scalar_prefetch=1,
            grid=(),
            in_specs=[whole] * 9,
            out_specs=[whole] * 2,
            scratch_shapes=[
                pltpu.VMEM((rows, feat), BF16),
                turned,
                turned,
                hidden_f32,
                hidden_f32,
                pltpu.VMEM((col_blocks, BLK, rows), BF16),
            ],
        ),
        compiler_params=pltpu.CompilerParams(vmem_limit_bytes=40 * MIB),
        cost_estimate=pl.CostEstimate(
            flops=24 * mm,
            bytes_accessed=6 * kept * BLK * BLK,
            transcendentals=tok * hidden,
        ),
        name="blocks",
    )(plan, gain_row, *columns, a_in, p_out, gp_own, n_own)

    arrived = lax.ppermute(for_peer, "dp", across_x)
    summed = [parts[0]] + [lax.ppermute(parts[q], "mp", near[q]) for q in range(1, mp_count)]
    total = sum(part.astype(F32) for part in summed)
    branch, grad_normed = total[:tok].astype(BF16), total[tok:].astype(BF16)
    owned_grad = (for_own + arrived.astype(F32)).reshape(cap, BLK * BLK)
    return (branch, grad_normed, owned_grad[None])


def sum_sources(received):
    return jnp.sum(received, axis=0)


def body(x_in, gain, w_in, w_out, grad_out, block_cols, slots):
    whole_x, whole_grad = (
        lax.all_gather(x_in, "mp", axis=1, tiled=True),
        lax.all_gather(grad_out, "mp", axis=1, tiled=True),
    )
    tok_rows = whole_x.shape[0]
    feat_width = whole_x.shape[1]
    row_blocks = feat_width // BLK
    kept_count = w_in.shape[0]
    per_row = kept_count // row_blocks
    col_blocks = FF // lax.axis_size("mp") // BLK
    col_ids = block_cols[0]
    slot_ids = slots[0]
    x_float = whole_x.astype(jnp.float32)
    inv_rms = lax.rsqrt(jnp.mean(x_float * x_float, axis=-1, keepdims=True) + norm_eps)
    normed = (x_float * inv_rms * gain).astype(jnp.bfloat16)
    normed_cols = normed.reshape(tok_rows, row_blocks, BLK).transpose(1, 2, 0)
    grad_cols = whole_grad.reshape(tok_rows, row_blocks, BLK).transpose(1, 2, 0)
    in_blocks = w_in.reshape(row_blocks, per_row, BLK, BLK)
    out_blocks = w_out.reshape(row_blocks, per_row, BLK, BLK)
    col_onehot = (col_ids[None, :] == jnp.arange(col_blocks, dtype=jnp.int32)[:, None]).astype(
        jnp.float32
    )
    pre_parts = jnp.einsum(
        "rkbc,rbt->rkct", in_blocks, normed_cols, preferred_element_type=jnp.float32
    )
    pre_act = jnp.dot(
        col_onehot,
        pre_parts.reshape(kept_count, BLK * tok_rows),
        precision=lax.Precision.HIGHEST,
        preferred_element_type=jnp.float32,
    )
    pre_act = pre_act.reshape(col_blocks, BLK, tok_rows)
    activation = gelu_value(pre_act).astype(jnp.bfloat16)
    act_blocks = jnp.take(activation, col_ids, axis=0).reshape(row_blocks, per_row, BLK, tok_rows)
    branch_cols = jnp.einsum(
        "rkcb,rkct->rbt", out_blocks, act_blocks, preferred_element_type=jnp.float32
    )
    branch_part = branch_cols.transpose(2, 0, 1).reshape(tok_rows, feat_width)
    branch = lax.psum_scatter(branch_part, "mp", scatter_dimension=1, tiled=True).astype(
        jnp.bfloat16
    )
    act_parts = jnp.einsum(
        "rkcb,rbt->rkct", out_blocks, grad_cols, preferred_element_type=jnp.float32
    )
    grad_act = jnp.dot(
        col_onehot,
        act_parts.reshape(kept_count, BLK * tok_rows),
        precision=lax.Precision.HIGHEST,
        preferred_element_type=jnp.float32,
    )
    grad_act = grad_act.reshape(col_blocks, BLK, tok_rows)
    grad_pre = (grad_act * gelu_slope(pre_act)).astype(jnp.bfloat16)
    pre_blocks = jnp.take(grad_pre, col_ids, axis=0).reshape(row_blocks, per_row, BLK, tok_rows)
    dp_count = lax.axis_size("dp")
    weight_scale = 1.0 / math.sqrt(tok_rows * dp_count)
    block_terms = jnp.einsum(
        "rkct,rbt->rkcb", pre_blocks, normed_cols, preferred_element_type=jnp.float32
    )
    block_partial = (block_terms * weight_scale).reshape(kept_count, BLK * BLK)
    capacity = 2 * kept_count // dp_count
    outgoing = (
        jnp.zeros((dp_count * capacity, BLK * BLK), jnp.float32).at[slot_ids].set(block_partial)
    )
    outgoing = outgoing.reshape(dp_count, capacity, BLK * BLK)
    owned_grad = sum_sources(
        lax.all_to_all(
            outgoing.astype(jnp.bfloat16), "dp", split_axis=0, concat_axis=0, tiled=True
        ).astype(outgoing.dtype)
    )
    normed_part = jnp.einsum(
        "rkbc,rkct->rbt", in_blocks, pre_blocks, preferred_element_type=jnp.float32
    )
    normed_part = normed_part.transpose(2, 0, 1).reshape(tok_rows, feat_width)
    grad_normed = lax.psum_scatter(normed_part, "mp", scatter_dimension=1, tiled=True).astype(
        jnp.bfloat16
    )
    return (branch, grad_normed, owned_grad[None])


def solution(mesh):
    placed = (
        P("dp", "mp"),
        P(),
        P("mp", None),
        P("mp", None),
        P("dp", "mp"),
        P("mp", None),
        P("mp", None),
    )
    fits = mesh.shape["dp"] == 8 and mesh.shape["mp"] == 4
    return jax.shard_map(
        fast_body if fits else body,
        mesh=mesh,
        in_specs=placed,
        out_specs=(P("dp", "mp"), P("dp", "mp"), P("mp", "dp", None)),
        check_vma=False,
    )
```

```python
import functools
import math

import jax
import jax.numpy as jnp
from jax import lax
from jax.experimental import pallas as pl
from jax.experimental.pallas import tpu as pltpu
from jax.sharding import PartitionSpec as P

FF = 32768
BLK = 64
HALF = BLK // 2
GROUP = 4
FIRST = 1024
BATCH = 16


norm_eps = 1e-06
tanh_coef = 0.7978845608028654

F32 = jnp.float32
BF16 = jnp.bfloat16
MIB = 1024 * 1024


def gelu_value(pre_act):
    cubic = pre_act * pre_act * pre_act
    slope_arg = jnp.tanh(tanh_coef * (pre_act + 0.044715 * cubic))
    return 0.5 * pre_act * (1.0 + slope_arg)


def gelu_slope(pre_act):
    cubic = pre_act * pre_act * pre_act
    slope_arg = jnp.tanh(tanh_coef * (pre_act + 0.044715 * cubic))
    inner = tanh_coef * (1.0 + 0.134145 * pre_act * pre_act)
    return 0.5 * (1.0 + slope_arg) + 0.5 * pre_act * (1.0 - slope_arg * slope_arg) * inner


def gelu_both(v):
    square = v * v
    th = jnp.tanh(v * (tanh_coef + (tanh_coef * 0.044715) * square))
    gate = 0.5 + 0.5 * th
    inner = 2.0 * tanh_coef + (2.0 * tanh_coef * 0.134145) * square
    return v * gate, gate + v * (gate - gate * gate) * inner


def dot(a, b, dims=((1,), (0,))):
    return lax.dot_general(a, b, (dims, ((), ())), preferred_element_type=F32)


def iota(shape, axis):
    return lax.broadcasted_iota(jnp.int32, shape, axis)


def even_first(width):
    row, col = iota((width, width), 0), iota((width, width), 1)
    inside = row & (BLK - 1)
    target = (row - inside) + (inside & 1) * HALF + (inside >> 1)
    return jnp.where(col == target, 1.0, 0.0).astype(BF16)


def plan_kernel(cap, col_blocks, row_blocks, cols_ref, slots_ref, x_ref, grad_ref, out_ref, both_ref):
    kept = cols_ref.shape[1]
    per_row = kept // row_blocks
    me = lax.axis_index("dp")
    tok = x_ref.shape[0]
    both_ref[:tok, :] = x_ref[...]
    both_ref[tok:, :] = grad_ref[...]
    cols, slots = cols_ref[...], slots_ref[...]
    owner = lax.div(slots, jnp.int32(cap))
    own = jnp.where(owner == me, 1.0, 0.0)
    peer = jnp.where(owner == (me ^ 1), 1.0, 0.0)
    flag = own + peer
    needed = jnp.max(jnp.where(cols == iota((col_blocks, kept), 0), flag, 0.0), axis=1, keepdims=True)

    def to_column(row):
        size = row.shape[1]
        eye = iota((size, size), 0) == iota((size, size), 1)
        return jnp.sum(jnp.where(eye, row, 0.0), axis=1, keepdims=True)

    def to_row(column):
        size = column.shape[0]
        eye = iota((size, size), 0) == iota((size, size), 1)
        return jnp.sum(jnp.where(eye, column, 0.0), axis=0, keepdims=True)

    def listed(flags_r, flags_c):
        size = flags_r.shape[1]
        before = iota((size, size), 1) < iota((size, size), 0)
        place = jnp.sum(jnp.where(before, flags_r, 0.0), axis=1, keepdims=True)
        hit = (place == iota((size, kept), 1).astype(F32)) & (flags_c > 0)
        index = iota((size, 1), 0).astype(F32)
        return jnp.sum(jnp.where(hit, index, 0.0), axis=0, keepdims=True)

    cols_r = cols.astype(F32)
    cols_c = to_column(cols_r)
    earlier = iota((kept, kept), 1) < iota((kept, kept), 0)
    seen = jnp.max(jnp.where(earlier & (cols_r == cols_c), 1.0, 0.0), axis=1, keepdims=True)
    flag_c = to_column(flag)
    pair_end = iota((kept, kept), 0) < 2 * per_row * iota((kept, kept), 1)
    rows = [
        cols_r + FIRST * (1.0 - to_row(seen)),
        (slots - owner * cap).astype(F32) + cap * own,
        listed(flag, flag_c),
        jnp.sum(jnp.where(pair_end, flag_c, 0.0), axis=0, keepdims=True),
        listed(to_row(needed), needed),
        jnp.sum(needed, axis=0, keepdims=True),
    ]
    for index, row in enumerate(rows):
        out_ref[index : index + 1, :] = jnp.broadcast_to(row, (1, kept)).astype(jnp.int32)
    out_ref[len(rows) :, :] = jnp.zeros((out_ref.shape[0] - len(rows), kept), jnp.int32)


def prepare_kernel(win_ref, wout_ref, a_in, b_in, p_out, a_out, order, both):
    count = a_in.shape[0]
    per_row, length = win_ref.shape[0] // count, win_ref.shape[1]
    lanes = 2 * BLK
    rows = per_row * HALF

    @pl.when(pl.program_id(0) == 0)
    def _():
        row, col = iota((rows, rows), 0), iota((rows, rows), 1)
        source = (row & (HALF - 1)) * per_row + lax.div(row, jnp.int32(HALF))
        order[...] = jnp.where(col == source, 1.0, 0.0).astype(BF16)
        row, col = iota((lanes, lanes), 0), iota((lanes, lanes), 1)
        swap = jnp.where(((col + BLK) & (lanes - 1)) == row, 1.0, 0.0).astype(BF16)
        perm = even_first(lanes)
        both[:, :lanes] = perm
        both[:, lanes:] = dot(perm, swap).astype(BF16)

    def by_block(ref):
        stacked = [
            jnp.concatenate(
                [
                    ref[n * per_row : (n + 1) * per_row, j * lanes : (j + 1) * lanes]
                    for j in range(length // lanes)
                ],
                axis=0,
            )
            for n in range(count)
        ]
        return dot(order[...], jnp.concatenate(stacked, axis=1)).astype(BF16)

    ordered_in, ordered_out = by_block(win_ref), by_block(wout_ref)
    left = iota((HALF, lanes), 1) < BLK
    for n in range(count):
        of_n = slice(n * lanes, (n + 1) * lanes)
        kept_in = dot(ordered_in[:, of_n], both[...])
        kept_out = ordered_out[:, of_n]
        p_out[n] = kept_out
        for pair in range(per_row // 2):
            first = kept_in[2 * pair * HALF : (2 * pair + 1) * HALF]
            second = kept_in[(2 * pair + 1) * HALF : (2 * pair + 2) * HALF]
            at = slice(pair * lanes, (pair + 1) * lanes)
            b_in[n, :HALF, at] = jnp.where(left, first[:, :lanes], second[:, lanes:]).astype(BF16)
            b_in[n, HALF:, at] = jnp.where(left, first[:, lanes:], second[:, :lanes]).astype(BF16)
        for quad in range(per_row // GROUP):
            rows_of = slice(quad * lanes, (quad + 1) * lanes)
            turned = kept_in[rows_of, :lanes].astype(BF16).T
            a_in[n, quad * BLK : (quad + 1) * BLK, :lanes] = turned[:BLK]
            a_in[n, quad * BLK : (quad + 1) * BLK, lanes:] = turned[BLK:]
            turned = kept_out[rows_of].T
            a_out[n, :, rows_of] = turned[:BLK]
            a_out[n, :, rows + quad * lanes : rows + (quad + 1) * lanes] = turned[BLK:]


def load_tokens(pieces, tok, gain_ref, perm, n_s, nt_s, gt_s, base):
    mine = lax.axis_index("mp")
    width = pieces[0][0].shape[1]
    values, total = [], 0.0
    for ref, first in pieces:
        value = ref[first : first + tok, :].astype(F32)
        values.append(value)
        total = total + jnp.sum(value * value, axis=-1, keepdims=True)
    inv_rms = lax.rsqrt(total / (width * len(pieces)) + norm_eps)
    for q, (ref, first) in enumerate(pieces):
        at = pl.ds(pl.multiple_of((mine ^ q) * width, width), width)
        normed = (values[q] * inv_rms * gain_ref[:, at]).astype(BF16)
        n_s[base : base + tok, at] = normed
        nt_s[at, :] = dot(normed, perm).astype(BF16).T
        gt_s[at, :] = ref[first + tok : first + 2 * tok, :].T


def expand(plan, a_in, p_out, nt_s, gt_s, acc_v, acc_a):
    row_blocks = a_in.shape[0]
    tok = nt_s.shape[1]
    per_row = p_out.shape[1] // HALF
    gap = jnp.zeros((HALF, tok), BF16)
    gap2 = jnp.zeros((BLK, tok), BF16)

    def step(r, carry):
        at = pl.ds(pl.multiple_of(r * BLK, BLK), BLK)
        normed, cot = nt_s[at, :], gt_s[at, :]
        spread = []
        for a in (0, 1):
            part = normed[a * HALF : (a + 1) * HALF]
            for u in range(GROUP):
                spread.append(
                    jnp.concatenate([part if v == u else gap for v in range(GROUP)], axis=1)
                )
        terms_v = dot(a_in[r], jnp.concatenate(spread, axis=0))
        cots = jnp.concatenate(
            [jnp.concatenate([cot, gap2], axis=1), jnp.concatenate([gap2, cot], axis=1)], axis=0
        )
        terms_a = dot(p_out[r], cots)
        for quad in range(per_row // GROUP):
            new = []
            for u in range(GROUP):
                k = quad * GROUP + u
                code = plan[0, r * per_row + k]
                c, first = code & (FIRST - 1), code >= FIRST
                v = terms_v[quad * BLK : (quad + 1) * BLK, u * tok : (u + 1) * tok]
                rows = terms_a[k * HALF : (k + 1) * HALF]
                a = jnp.concatenate([rows[:, :tok], rows[:, tok:]], axis=0)
                v = jnp.where(first, v, acc_v[c] + v)
                a = jnp.where(first, a, acc_a[c] + a)
                new.append((c, v, a))
            for c, v, a in new:
                acc_v[c] = v
                acc_a[c] = a
        return carry

    lax.fori_loop(0, row_blocks, step, 0, unroll=4)


def local_kernel(
    plan, gain_ref, s0, s1, s2, s3, a_in, b_in, p_out, a_out, o0, o1, o2, o3, gp_ref, n_ref,
    nt_s, gt_s, acc_v, acc_a, act_s, br_s, gn_s
):
    width = s0.shape[1]
    tok = s0.shape[0] // 2
    row_blocks, per_row = a_in.shape[0], p_out.shape[1] // HALF
    col_blocks = acc_v.shape[0]
    perm = even_first(width)
    load_tokens([(ref, 0) for ref in (s0, s1, s2, s3)], tok, gain_ref, perm, n_ref, nt_s, gt_s, 0)
    expand(plan, a_in, p_out, nt_s, gt_s, acc_v, acc_a)

    def bend(c, carry):
        value, slope = gelu_both(acc_v[c])
        act_s[c] = value.astype(BF16)
        gp_ref[c] = (acc_a[c] * slope).astype(BF16)
        return carry

    lax.fori_loop(0, col_blocks, bend, 0, unroll=4)

    def contract(r, carry):
        at = pl.ds(pl.multiple_of(r * BLK, BLK), BLK)
        ids = [plan[0, r * per_row + k] & (FIRST - 1) for k in range(per_row)]
        acts = [act_s[c, a * HALF : (a + 1) * HALF, :] for a in (0, 1) for c in ids]
        br_s[at, :] = dot(a_out[r], jnp.concatenate(acts, axis=0)).astype(BF16)
        grads = [gp_ref[c] for c in ids]
        gn_s[at, :] = dot(b_in[r], jnp.concatenate(grads, axis=0)).astype(BF16)
        return carry

    lax.fori_loop(0, row_blocks, contract, 0, unroll=4)
    mine = lax.axis_index("mp")
    for q, out in enumerate((o0, o1, o2, o3)):
        at = pl.ds(pl.multiple_of((mine ^ q) * width, width), width)
        out[:tok, :] = br_s[at, :].T
        out[tok:, :] = dot(gn_s[at, :].T, perm, ((1,), (1,))).astype(BF16)


def block_kernel(
    scale, plan, gain_ref, z0, z1, z2, z3, a_in, p_out, gp_own, n_own, peer_ref, own_ref,
    n_s, nt_s, gt_s, acc_v, acc_a, gp_s, found
):
    tok = n_own.shape[0]
    per_row = p_out.shape[1] // HALF
    lanes = 2 * BLK
    perm = even_first(z0.shape[1])
    n_s[:tok, :] = n_own[...]

    def keep(i, carry):
        c = plan[4, i]
        gp_s[c, :, :tok] = gp_own[c]
        return carry

    lax.fori_loop(0, plan[5, 0], keep, 0)
    for j in range(z0.shape[0] // (2 * tok)):
        pieces = [(ref, 2 * tok * j) for ref in (z0, z1, z2, z3)]
        load_tokens(pieces, tok, gain_ref, perm, n_s, nt_s, gt_s, (j + 1) * tok)
        expand(plan, a_in, p_out, nt_s, gt_s, acc_v, acc_a)

        def bend(i, carry):
            c = plan[4, i]
            _, slope = gelu_both(acc_v[c])
            gp_s[c, :, (j + 1) * tok : (j + 2) * tok] = (acc_a[c] * slope).astype(BF16)
            return carry

        lax.fori_loop(0, plan[5, 0], bend, 0)

    left = iota((HALF, lanes), 1) < BLK
    cap = own_ref.shape[0]
    found[...] = jnp.zeros_like(found)

    def form(pair, first):
        end = plan[3, pair + 1]
        at_lane = pl.ds(pl.multiple_of(pair * lanes, lanes), lanes)
        ids = [
            plan[2, jnp.maximum(jnp.minimum(first + u, end - 1), 0)] for u in range(BATCH)
        ]
        grads = jnp.concatenate([gp_s[plan[0, k] & (FIRST - 1)] for k in ids], axis=0)
        blocks = dot(grads, n_s[:, at_lane]) * scale
        done = []
        for u, k in enumerate(ids):
            odd = (lax.div(k, jnp.int32(per_row)) & 1) == 1
            top = blocks[u * BLK : u * BLK + HALF]
            low = blocks[u * BLK + HALF : (u + 1) * BLK]
            top = jnp.where(odd, pltpu.roll(top, BLK, 1), top)
            low = jnp.where(odd, low, pltpu.roll(low, BLK, 1))
            slot = jnp.where(first < end, plan[1, k], 2 * cap)
            done.append((slot, jnp.where(left, top, low)))
        for slot, value in done:
            found[slot] = value

    pairs = p_out.shape[0] // 2

    def begin(pair, carry):
        form(pair, plan[3, pair])
        return carry

    lax.fori_loop(0, pairs, begin, 0, unroll=2)

    def finish(pair, carry):
        @pl.when(plan[3, pair + 1] - plan[3, pair] > BATCH)
        def _():
            form(pair, plan[3, pair] + BATCH)

        return carry

    lax.fori_loop(0, pairs, finish, 0)
    peer_ref[...] = found[:cap].astype(peer_ref.dtype)
    own_ref[...] = found[cap : 2 * cap]


def fast_body(x_in, gain, w_in, w_out, grad_out, block_cols, slots):
    dp_count, mp_count = lax.axis_size("dp"), lax.axis_size("mp")
    tok, width = x_in.shape
    feat = width * mp_count
    kept = w_in.shape[0]
    row_blocks = feat // BLK
    per_row = kept // row_blocks
    hidden = FF // mp_count
    col_blocks = hidden // BLK
    lanes = 2 * BLK
    cap = 2 * kept // dp_count
    scale = 1.0 / math.sqrt(tok * dp_count)
    across_x = [(i, i ^ 1) for i in range(dp_count)]
    near = [[(i, i ^ q) for i in range(mp_count)] for q in range(mp_count)]
    z_count = dp_count // 2
    along_z = [[(i, i ^ (2 * j)) for i in range(dp_count)] for j in (1, 3, 2)]

    whole = pl.BlockSpec(memory_space=pltpu.VMEM)
    mm = 2 * tok * kept * BLK * BLK

    plan, own = pl.pallas_call(
        functools.partial(plan_kernel, cap, col_blocks, row_blocks),
        out_shape=[
            jax.ShapeDtypeStruct((8, kept), jnp.int32),
            jax.ShapeDtypeStruct((2 * tok, width), BF16),
        ],
        cost_estimate=pl.CostEstimate(flops=4_000_000, bytes_accessed=16384, transcendentals=0),
        name="plan",
    )(block_cols, slots, x_in, grad_out)

    pieces = [lax.ppermute(own, "dp", hop) for hop in along_z]
    gathered = [own] + [lax.ppermute(own, "mp", near[q]) for q in range(1, mp_count)]
    gain_row = gain.reshape(1, feat)

    step = min(4, row_blocks)
    shapes = [
        (per_row // GROUP * BLK, 2 * lanes),
        (BLK, per_row * BLK),
        (per_row * HALF, lanes),
        (BLK, per_row * BLK),
    ]
    a_in, b_in, p_out, a_out = pl.pallas_call(
        prepare_kernel,
        out_shape=[jax.ShapeDtypeStruct((row_blocks, *shape), BF16) for shape in shapes],
        grid=(row_blocks // step,),
        in_specs=[pl.BlockSpec((step * per_row, BLK * BLK), lambda r: (r, 0))] * 2,
        out_specs=[pl.BlockSpec((step, *shape), lambda r: (r, 0, 0)) for shape in shapes],
        scratch_shapes=[
            pltpu.VMEM((per_row * HALF, per_row * HALF), BF16),
            pltpu.VMEM((lanes, 2 * lanes), BF16),
        ],
        compiler_params=pltpu.CompilerParams(vmem_limit_bytes=24 * MIB),
        cost_estimate=pl.CostEstimate(
            flops=8 * mm, bytes_accessed=12 * kept * BLK * BLK, transcendentals=0
        ),
        name="prepare",
    )(
        pltpu.with_memory_space_constraint(w_in, pltpu.HBM),
        pltpu.with_memory_space_constraint(w_out, pltpu.HBM),
    )

    pieces, gathered, p_out = lax.optimization_barrier((pieces, gathered, p_out))
    column = jnp.concatenate(pieces, axis=0)
    column_c = lax.ppermute(column, "mp", near[1])
    column_y = lax.ppermute(column, "mp", near[2])

    hidden_f32 = pltpu.VMEM((col_blocks, BLK, tok), F32)
    turned = pltpu.VMEM((feat, tok), BF16)
    *parts, gp_own, n_own = pl.pallas_call(
        local_kernel,
        out_shape=[jax.ShapeDtypeStruct((2 * tok, width), BF16)] * mp_count
        + [
            jax.ShapeDtypeStruct((col_blocks, BLK, tok), BF16),
            jax.ShapeDtypeStruct((tok, feat), BF16),
        ],
        grid_spec=pltpu.PrefetchScalarGridSpec(
            num_scalar_prefetch=1,
            grid=(),
            in_specs=[whole] * 9,
            out_specs=[whole] * (mp_count + 2),
            scratch_shapes=[
                turned,
                turned,
                hidden_f32,
                hidden_f32,
                pltpu.VMEM((col_blocks, BLK, tok), BF16),
                turned,
                turned,
            ],
        ),
        compiler_params=pltpu.CompilerParams(vmem_limit_bytes=32 * MIB),
        cost_estimate=pl.CostEstimate(
            flops=16 * mm,
            bytes_accessed=10 * kept * BLK * BLK,
            transcendentals=tok * hidden,
        ),
        name="local",
    )(plan, gain_row, *gathered, a_in, b_in, p_out, a_out)

    column_y, n_own = lax.optimization_barrier((column_y, n_own))
    columns = [column, column_c, column_y, lax.ppermute(column_y, "mp", near[1])]
    rows = tok * z_count
    for_peer, for_own = pl.pallas_call(
        functools.partial(block_kernel, scale),
        out_shape=[
            jax.ShapeDtypeStruct((cap, HALF, lanes), BF16),
            jax.ShapeDtypeStruct((cap, HALF, lanes), F32),
        ],
        grid_spec=pltpu.PrefetchScalarGridSpec(
            num_scalar_prefetch=1,
            grid=(),
            in_specs=[whole] * 9,
            out_specs=[whole] * 2,
            scratch_shapes=[
                pltpu.VMEM((rows, feat), BF16),
                turned,
                turned,
                hidden_f32,
                hidden_f32,
                pltpu.VMEM((col_blocks, BLK, rows), BF16),
                pltpu.VMEM((2 * cap + 1, HALF, lanes), F32),
            ],
        ),
        compiler_params=pltpu.CompilerParams(vmem_limit_bytes=40 * MIB),
        cost_estimate=pl.CostEstimate(
            flops=24 * mm,
            bytes_accessed=6 * kept * BLK * BLK,
            transcendentals=tok * hidden,
        ),
        name="blocks",
    )(plan, gain_row, *columns, a_in, p_out, gp_own, n_own)

    arrived = lax.ppermute(for_peer, "dp", across_x)
    summed = [parts[0]] + [lax.ppermute(parts[q], "mp", near[q]) for q in range(1, mp_count)]
    total = sum(part.astype(F32) for part in summed)
    branch, grad_normed = total[:tok].astype(BF16), total[tok:].astype(BF16)
    owned_grad = (for_own + arrived.astype(F32)).reshape(cap, BLK * BLK)
    return (branch, grad_normed, owned_grad[None])


def sum_sources(received):
    return jnp.sum(received, axis=0)


def body(x_in, gain, w_in, w_out, grad_out, block_cols, slots):
    whole_x, whole_grad = (
        lax.all_gather(x_in, "mp", axis=1, tiled=True),
        lax.all_gather(grad_out, "mp", axis=1, tiled=True),
    )
    tok_rows = whole_x.shape[0]
    feat_width = whole_x.shape[1]
    row_blocks = feat_width // BLK
    kept_count = w_in.shape[0]
    per_row = kept_count // row_blocks
    col_blocks = FF // lax.axis_size("mp") // BLK
    col_ids = block_cols[0]
    slot_ids = slots[0]
    x_float = whole_x.astype(jnp.float32)
    inv_rms = lax.rsqrt(jnp.mean(x_float * x_float, axis=-1, keepdims=True) + norm_eps)
    normed = (x_float * inv_rms * gain).astype(jnp.bfloat16)
    normed_cols = normed.reshape(tok_rows, row_blocks, BLK).transpose(1, 2, 0)
    grad_cols = whole_grad.reshape(tok_rows, row_blocks, BLK).transpose(1, 2, 0)
    in_blocks = w_in.reshape(row_blocks, per_row, BLK, BLK)
    out_blocks = w_out.reshape(row_blocks, per_row, BLK, BLK)
    col_onehot = (col_ids[None, :] == jnp.arange(col_blocks, dtype=jnp.int32)[:, None]).astype(
        jnp.float32
    )
    pre_parts = jnp.einsum(
        "rkbc,rbt->rkct", in_blocks, normed_cols, preferred_element_type=jnp.float32
    )
    pre_act = jnp.dot(
        col_onehot,
        pre_parts.reshape(kept_count, BLK * tok_rows),
        precision=lax.Precision.HIGHEST,
        preferred_element_type=jnp.float32,
    )
    pre_act = pre_act.reshape(col_blocks, BLK, tok_rows)
    activation = gelu_value(pre_act).astype(jnp.bfloat16)
    act_blocks = jnp.take(activation, col_ids, axis=0).reshape(row_blocks, per_row, BLK, tok_rows)
    branch_cols = jnp.einsum(
        "rkcb,rkct->rbt", out_blocks, act_blocks, preferred_element_type=jnp.float32
    )
    branch_part = branch_cols.transpose(2, 0, 1).reshape(tok_rows, feat_width)
    branch = lax.psum_scatter(branch_part, "mp", scatter_dimension=1, tiled=True).astype(
        jnp.bfloat16
    )
    act_parts = jnp.einsum(
        "rkcb,rbt->rkct", out_blocks, grad_cols, preferred_element_type=jnp.float32
    )
    grad_act = jnp.dot(
        col_onehot,
        act_parts.reshape(kept_count, BLK * tok_rows),
        precision=lax.Precision.HIGHEST,
        preferred_element_type=jnp.float32,
    )
    grad_act = grad_act.reshape(col_blocks, BLK, tok_rows)
    grad_pre = (grad_act * gelu_slope(pre_act)).astype(jnp.bfloat16)
    pre_blocks = jnp.take(grad_pre, col_ids, axis=0).reshape(row_blocks, per_row, BLK, tok_rows)
    dp_count = lax.axis_size("dp")
    weight_scale = 1.0 / math.sqrt(tok_rows * dp_count)
    block_terms = jnp.einsum(
        "rkct,rbt->rkcb", pre_blocks, normed_cols, preferred_element_type=jnp.float32
    )
    block_partial = (block_terms * weight_scale).reshape(kept_count, BLK * BLK)
    capacity = 2 * kept_count // dp_count
    outgoing = (
        jnp.zeros((dp_count * capacity, BLK * BLK), jnp.float32).at[slot_ids].set(block_partial)
    )
    outgoing = outgoing.reshape(dp_count, capacity, BLK * BLK)
    owned_grad = sum_sources(
        lax.all_to_all(
            outgoing.astype(jnp.bfloat16), "dp", split_axis=0, concat_axis=0, tiled=True
        ).astype(outgoing.dtype)
    )
    normed_part = jnp.einsum(
        "rkbc,rkct->rbt", in_blocks, pre_blocks, preferred_element_type=jnp.float32
    )
    normed_part = normed_part.transpose(2, 0, 1).reshape(tok_rows, feat_width)
    grad_normed = lax.psum_scatter(normed_part, "mp", scatter_dimension=1, tiled=True).astype(
        jnp.bfloat16
    )
    return (branch, grad_normed, owned_grad[None])


def solution(mesh):
    placed = (
        P("dp", "mp"),
        P(),
        P("mp", None),
        P("mp", None),
        P("dp", "mp"),
        P("mp", None),
        P("mp", None),
    )
    fits = mesh.shape["dp"] == 8 and mesh.shape["mp"] == 4
    return jax.shard_map(
        fast_body if fits else body,
        mesh=mesh,
        in_specs=placed,
        out_specs=(P("dp", "mp"), P("dp", "mp"), P("mp", "dp", None)),
        check_vma=False,
    )
```

```python
import functools
import math

import jax
import jax.numpy as jnp
from jax import lax
from jax.experimental import pallas as pl
from jax.experimental.pallas import tpu as pltpu
from jax.sharding import PartitionSpec as P

FF = 32768
BLK = 64
HALF = BLK // 2
GROUP = 4
FIRST = 1024
BATCH = 12


norm_eps = 1e-06
tanh_coef = 0.7978845608028654

F32 = jnp.float32
BF16 = jnp.bfloat16
MIB = 1024 * 1024


def gelu_value(pre_act):
    cubic = pre_act * pre_act * pre_act
    slope_arg = jnp.tanh(tanh_coef * (pre_act + 0.044715 * cubic))
    return 0.5 * pre_act * (1.0 + slope_arg)


def gelu_slope(pre_act):
    cubic = pre_act * pre_act * pre_act
    slope_arg = jnp.tanh(tanh_coef * (pre_act + 0.044715 * cubic))
    inner = tanh_coef * (1.0 + 0.134145 * pre_act * pre_act)
    return 0.5 * (1.0 + slope_arg) + 0.5 * pre_act * (1.0 - slope_arg * slope_arg) * inner


def gelu_both(v):
    square = v * v
    th = jnp.tanh(v * (tanh_coef + (tanh_coef * 0.044715) * square))
    gate = 0.5 + 0.5 * th
    inner = 2.0 * tanh_coef + (2.0 * tanh_coef * 0.134145) * square
    return v * gate, gate + v * (gate - gate * gate) * inner


def dot(a, b, dims=((1,), (0,))):
    return lax.dot_general(a, b, (dims, ((), ())), preferred_element_type=F32)


def iota(shape, axis):
    return lax.broadcasted_iota(jnp.int32, shape, axis)


def even_first(width):
    row, col = iota((width, width), 0), iota((width, width), 1)
    inside = row & (BLK - 1)
    target = (row - inside) + (inside & 1) * HALF + (inside >> 1)
    return jnp.where(col == target, 1.0, 0.0).astype(BF16)


def stack_kernel(x_ref, grad_ref, both_ref):
    tok = x_ref.shape[0]
    both_ref[:tok, :] = x_ref[...]
    both_ref[tok:, :] = grad_ref[...]


def plan_kernel(cap, col_blocks, row_blocks, cols_ref, slots_ref, out_ref):
    kept = cols_ref.shape[1]
    per_row = kept // row_blocks
    me = lax.axis_index("dp")
    cols, slots = cols_ref[...], slots_ref[...]
    owner = lax.div(slots, jnp.int32(cap))
    own = jnp.where(owner == me, 1.0, 0.0)
    peer = jnp.where(owner == (me ^ 1), 1.0, 0.0)
    needed = jnp.max(
        jnp.where(cols == iota((col_blocks, kept), 0), own + peer, 0.0), axis=1, keepdims=True
    )

    def to_column(row):
        size = row.shape[1]
        eye = iota((size, size), 0) == iota((size, size), 1)
        return jnp.sum(jnp.where(eye, row, 0.0), axis=1, keepdims=True)

    def to_row(column):
        size = column.shape[0]
        eye = iota((size, size), 0) == iota((size, size), 1)
        return jnp.sum(jnp.where(eye, column, 0.0), axis=0, keepdims=True)

    def listed(flags_r, flags_c):
        size = flags_r.shape[1]
        before = iota((size, size), 1) < iota((size, size), 0)
        place = jnp.sum(jnp.where(before, flags_r, 0.0), axis=1, keepdims=True)
        hit = (place == iota((size, kept), 1).astype(F32)) & (flags_c > 0)
        index = iota((size, 1), 0).astype(F32)
        return jnp.sum(jnp.where(hit, index, 0.0), axis=0, keepdims=True)

    cols_r = cols.astype(F32)
    cols_c = to_column(cols_r)
    earlier = iota((kept, kept), 1) < iota((kept, kept), 0)
    seen = jnp.max(jnp.where(earlier & (cols_r == cols_c), 1.0, 0.0), axis=1, keepdims=True)
    peer_c, own_c = to_column(peer), to_column(own)
    pair_end = iota((kept, kept), 0) < 2 * per_row * iota((kept, kept), 1)

    def starts(flags_c):
        return jnp.sum(jnp.where(pair_end, flags_c, 0.0), axis=0, keepdims=True)

    rows = [
        cols_r + FIRST * (1.0 - to_row(seen)),
        (slots - owner * cap).astype(F32),
        listed(peer, peer_c),
        starts(peer_c),
        listed(to_row(needed), needed),
        jnp.sum(needed, axis=0, keepdims=True),
        listed(own, own_c),
        starts(own_c),
    ]
    for index, row in enumerate(rows):
        out_ref[index : index + 1, :] = jnp.broadcast_to(row, (1, kept)).astype(jnp.int32)


def prepare_kernel(plan_ref, win_ref, wout_ref, a_in, b_in, p_out, a_out, order, both):
    count = a_in.shape[0]
    per_row, length = win_ref.shape[0] // count, win_ref.shape[1]
    lanes = 2 * BLK
    rows = per_row * HALF

    @pl.when(pl.program_id(0) == 0)
    def _():
        row, col = iota((rows, rows), 0), iota((rows, rows), 1)
        source = (row & (HALF - 1)) * per_row + lax.div(row, jnp.int32(HALF))
        order[...] = jnp.where(col == source, 1.0, 0.0).astype(BF16)
        row, col = iota((lanes, lanes), 0), iota((lanes, lanes), 1)
        swap = jnp.where(((col + BLK) & (lanes - 1)) == row, 1.0, 0.0).astype(BF16)
        perm = even_first(lanes)
        both[:, :lanes] = perm
        both[:, lanes:] = dot(perm, swap).astype(BF16)

    def by_block(ref):
        stacked = [
            jnp.concatenate(
                [
                    ref[n * per_row : (n + 1) * per_row, j * lanes : (j + 1) * lanes]
                    for j in range(length // lanes)
                ],
                axis=0,
            )
            for n in range(count)
        ]
        return dot(order[...], jnp.concatenate(stacked, axis=1)).astype(BF16)

    ordered_in, ordered_out = by_block(win_ref), by_block(wout_ref)
    left = iota((HALF, lanes), 1) < BLK
    for n in range(count):
        of_n = slice(n * lanes, (n + 1) * lanes)
        kept_in = dot(ordered_in[:, of_n], both[...])
        kept_out = ordered_out[:, of_n]
        p_out[n] = kept_out
        for pair in range(per_row // 2):
            first = kept_in[2 * pair * HALF : (2 * pair + 1) * HALF]
            second = kept_in[(2 * pair + 1) * HALF : (2 * pair + 2) * HALF]
            at = slice(pair * lanes, (pair + 1) * lanes)
            b_in[n, :HALF, at] = jnp.where(left, first[:, :lanes], second[:, lanes:]).astype(BF16)
            b_in[n, HALF:, at] = jnp.where(left, first[:, lanes:], second[:, :lanes]).astype(BF16)
        for quad in range(per_row // GROUP):
            rows_of = slice(quad * lanes, (quad + 1) * lanes)
            turned = kept_in[rows_of, :lanes].astype(BF16).T
            a_in[n, quad * BLK : (quad + 1) * BLK, :lanes] = turned[:BLK]
            a_in[n, quad * BLK : (quad + 1) * BLK, lanes:] = turned[BLK:]
            turned = kept_out[rows_of].T
            a_out[n, :, rows_of] = turned[:BLK]
            a_out[n, :, rows + quad * lanes : rows + (quad + 1) * lanes] = turned[BLK:]


def load_tokens(pieces, tok, gain_ref, perm, n_s, nt_s, gt_s, base):
    mine = lax.axis_index("mp")
    width = pieces[0][0].shape[1]
    values, total = [], 0.0
    for ref, first in pieces:
        value = ref[first : first + tok, :].astype(F32)
        values.append(value)
        total = total + jnp.sum(value * value, axis=-1, keepdims=True)
    inv_rms = lax.rsqrt(total / (width * len(pieces)) + norm_eps)
    for q, (ref, first) in enumerate(pieces):
        at = pl.ds(pl.multiple_of((mine ^ q) * width, width), width)
        normed = (values[q] * inv_rms * gain_ref[:, at]).astype(BF16)
        n_s[base : base + tok, at] = normed
        nt_s[at, :] = dot(normed, perm).astype(BF16).T
        gt_s[at, :] = ref[first + tok : first + 2 * tok, :].T


def expand(plan, a_in, p_out, nt_s, gt_s, acc_v, acc_a):
    row_blocks = a_in.shape[0]
    tok = nt_s.shape[1]
    per_row = p_out.shape[1] // HALF
    gap = jnp.zeros((HALF, tok), BF16)
    gap2 = jnp.zeros((BLK, tok), BF16)

    def step(r, carry):
        at = pl.ds(pl.multiple_of(r * BLK, BLK), BLK)
        normed, cot = nt_s[at, :], gt_s[at, :]
        spread = []
        for a in (0, 1):
            part = normed[a * HALF : (a + 1) * HALF]
            for u in range(GROUP):
                spread.append(
                    jnp.concatenate([part if v == u else gap for v in range(GROUP)], axis=1)
                )
        terms_v = dot(a_in[r], jnp.concatenate(spread, axis=0))
        cots = jnp.concatenate(
            [jnp.concatenate([cot, gap2], axis=1), jnp.concatenate([gap2, cot], axis=1)], axis=0
        )
        terms_a = dot(p_out[r], cots)
        for quad in range(per_row // GROUP):
            new = []
            for u in range(GROUP):
                k = quad * GROUP + u
                code = plan[0, r * per_row + k]
                c, first = code & (FIRST - 1), code >= FIRST
                v = terms_v[quad * BLK : (quad + 1) * BLK, u * tok : (u + 1) * tok]
                rows = terms_a[k * HALF : (k + 1) * HALF]
                a = jnp.concatenate([rows[:, :tok], rows[:, tok:]], axis=0)
                v = jnp.where(first, v, acc_v[c] + v)
                a = jnp.where(first, a, acc_a[c] + a)
                new.append((c, v, a))
            for c, v, a in new:
                acc_v[c] = v
                acc_a[c] = a
        return carry

    lax.fori_loop(0, row_blocks, step, 0, unroll=8)


def local_kernel(
    plan, gain_ref, s0, s1, s2, s3, a_in, p_out, act_ref, gp_ref, n_ref, nt_s, gt_s, acc_v, acc_a
):
    tok = n_ref.shape[0]
    perm = even_first(s0.shape[1])
    load_tokens([(ref, 0) for ref in (s0, s1, s2, s3)], tok, gain_ref, perm, n_ref, nt_s, gt_s, 0)
    expand(plan, a_in, p_out, nt_s, gt_s, acc_v, acc_a)

    def bend(c, carry):
        value, slope = gelu_both(acc_v[c])
        act_ref[c] = value.astype(BF16)
        gp_ref[c] = (acc_a[c] * slope).astype(BF16)
        return carry

    lax.fori_loop(0, gp_ref.shape[0], bend, 0, unroll=4)


def contract_kernel(plan, act_ref, gp_ref, b_in, a_out, o0, o1, o2, o3, br_s, gn_s):
    tok, width = o0.shape[0] // 2, o0.shape[1]
    row_blocks, per_row = b_in.shape[0], b_in.shape[2] // BLK
    perm = even_first(width)

    def contract(r, carry):
        at = pl.ds(pl.multiple_of(r * BLK, BLK), BLK)
        ids = [plan[0, r * per_row + k] & (FIRST - 1) for k in range(per_row)]
        acts = [act_ref[c, a * HALF : (a + 1) * HALF, :] for a in (0, 1) for c in ids]
        br_s[at, :] = dot(a_out[r], jnp.concatenate(acts, axis=0)).astype(BF16)
        grads = [gp_ref[c] for c in ids]
        gn_s[at, :] = dot(b_in[r], jnp.concatenate(grads, axis=0)).astype(BF16)
        return carry

    lax.fori_loop(0, row_blocks, contract, 0, unroll=4)
    mine = lax.axis_index("mp")
    for q, out in enumerate((o0, o1, o2, o3)):
        at = pl.ds(pl.multiple_of((mine ^ q) * width, width), width)
        out[:tok, :] = br_s[at, :].T
        out[tok:, :] = dot(gn_s[at, :].T, perm, ((1,), (1,))).astype(BF16)


def chunk_kernel(
    plan, gain_ref, s0, s1, s2, s3, a_in, p_out, gp_ref, n_ref, nt_s, gt_s, acc_v, acc_a
):
    chunks = gp_ref.shape[0]
    tok = n_ref.shape[0] // chunks
    perm = even_first(s0.shape[1])
    count = plan[5, 0]
    for j in range(chunks):
        pieces = [(ref, 2 * tok * j) for ref in (s0, s1, s2, s3)]
        load_tokens(pieces, tok, gain_ref, perm, n_ref, nt_s, gt_s, j * tok)
        expand(plan, a_in, p_out, nt_s, gt_s, acc_v, acc_a)

        def bend(i, carry):
            for u in range(GROUP):
                c = plan[4, jnp.minimum(i * GROUP + u, count - 1)]
                _, slope = gelu_both(acc_v[c])
                gp_ref[j, c] = (acc_a[c] * slope).astype(BF16)
            return carry

        lax.fori_loop(0, (count + GROUP - 1) // GROUP, bend, 0)


def block_kernel(
    list_row, scale, plan, gp0, gp1, gp2, n0, n1, n2, p_out, out_ref, found
):
    per_row = p_out.shape[1] // HALF
    lanes = 2 * BLK
    pairs = p_out.shape[0] // 2
    cap = out_ref.shape[0]
    left = iota((HALF, lanes), 1) < BLK
    found[...] = jnp.zeros_like(found)

    def form(pair, first):
        end = plan[list_row + 1, pair + 1]
        at_lane = pl.ds(pl.multiple_of(pair * lanes, lanes), lanes)
        ids = [
            plan[list_row, jnp.maximum(jnp.minimum(first + u, end - 1), 0)] for u in range(BATCH)
        ]
        grads = []
        for k in ids:
            c = plan[0, k] & (FIRST - 1)
            chunks = [gp0[c]] + [ref[j, c] for ref in (gp1, gp2) for j in range(ref.shape[0])]
            grads.append(jnp.concatenate(chunks, axis=1))
        normed = jnp.concatenate([ref[:, at_lane] for ref in (n0, n1, n2)], axis=0)
        blocks = dot(jnp.concatenate(grads, axis=0), normed) * scale
        done = []
        for u, k in enumerate(ids):
            odd = (lax.div(k, jnp.int32(per_row)) & 1) == 1
            top = blocks[u * BLK : u * BLK + HALF]
            low = blocks[u * BLK + HALF : (u + 1) * BLK]
            top = jnp.where(odd, pltpu.roll(top, BLK, 1), top)
            low = jnp.where(odd, low, pltpu.roll(low, BLK, 1))
            slot = jnp.where(first < end, plan[1, k], cap)
            done.append((slot, jnp.where(left, top, low)))
        for slot, value in done:
            found[slot] = value

    def begin(pair, carry):
        form(pair, plan[list_row + 1, pair])
        return carry

    lax.fori_loop(0, pairs, begin, 0, unroll=8)

    def finish(pair, carry):
        begin, end = plan[list_row + 1, pair], plan[list_row + 1, pair + 1]

        def more(i, carry):
            form(pair, begin + i * BATCH)
            return carry

        return lax.fori_loop(1, (end - begin + BATCH - 1) // BATCH, more, carry)

    lax.fori_loop(0, pairs, finish, 0)
    out_ref[...] = found[:cap].astype(out_ref.dtype)


def finish_kernel(own_ref, arrived_ref, s0, s1, s2, s3, branch_ref, normed_ref, out_ref):
    lanes = own_ref.shape[2]
    rows = 8
    for first in range(0, own_ref.shape[0], rows):
        at = slice(first, first + rows)
        blocks = own_ref[at] + arrived_ref[at].astype(F32)
        turned = jnp.swapaxes(blocks, 0, 1)
        for j in range(turned.shape[0]):
            out_ref[at, j * lanes : (j + 1) * lanes] = turned[j]

    @pl.when(pl.program_id(0) == 0)
    def _():
        tok = branch_ref.shape[0]
        for out, base in ((branch_ref, 0), (normed_ref, tok)):
            total = sum(ref[base : base + tok, :].astype(F32) for ref in (s0, s1, s2, s3))
            out[...] = total.astype(BF16)


def fast_body(x_in, gain, w_in, w_out, grad_out, block_cols, slots):
    dp_count, mp_count = lax.axis_size("dp"), lax.axis_size("mp")
    tok, width = x_in.shape
    feat = width * mp_count
    kept = w_in.shape[0]
    row_blocks = feat // BLK
    per_row = kept // row_blocks
    hidden = FF // mp_count
    col_blocks = hidden // BLK
    lanes = 2 * BLK
    cap = 2 * kept // dp_count
    scale = 1.0 / math.sqrt(tok * dp_count)
    across_x = [(i, i ^ 1) for i in range(dp_count)]
    near = [[(i, i ^ q) for i in range(mp_count)] for q in range(mp_count)]
    z_count = dp_count // 2
    along_z = [[(i, i ^ (2 * j)) for i in range(dp_count)] for j in (1, 3, 2)]

    whole = pl.BlockSpec(memory_space=pltpu.VMEM)
    mm = 2 * tok * kept * BLK * BLK

    own = pl.pallas_call(
        stack_kernel,
        out_shape=jax.ShapeDtypeStruct((2 * tok, width), BF16),
        cost_estimate=pl.CostEstimate(flops=0, bytes_accessed=8 * tok * width, transcendentals=0),
        name="stack",
    )(x_in, grad_out)
    pieces = [lax.ppermute(own, "dp", along_z[0])]
    gathered = [own] + [lax.ppermute(own, "mp", near[q]) for q in range(1, mp_count)]
    gathered[1], own_late = lax.optimization_barrier((gathered[1], own))
    pieces += [lax.ppermute(own_late, "dp", hop) for hop in along_z[1:]]
    pieces[0], cols_late, slots_late = lax.optimization_barrier((pieces[0], block_cols, slots))
    plan = pl.pallas_call(
        functools.partial(plan_kernel, cap, col_blocks, row_blocks),
        out_shape=jax.ShapeDtypeStruct((8, kept), jnp.int32),
        cost_estimate=pl.CostEstimate(flops=4_000_000, bytes_accessed=16384, transcendentals=0),
        name="plan",
    )(cols_late, slots_late)
    near_piece = [pieces[0]] + [lax.ppermute(pieces[0], "mp", near[q]) for q in (1, 2)]
    gain_row = gain.reshape(1, feat)

    step = min(4, row_blocks)
    shapes = [
        (per_row // GROUP * BLK, 2 * lanes),
        (BLK, per_row * BLK),
        (per_row * HALF, lanes),
        (BLK, per_row * BLK),
    ]
    a_in, b_in, p_out, a_out = pl.pallas_call(
        prepare_kernel,
        out_shape=[jax.ShapeDtypeStruct((row_blocks, *shape), BF16) for shape in shapes],
        grid=(row_blocks // step,),
        in_specs=[pl.BlockSpec(memory_space=pltpu.SMEM)]
        + [pl.BlockSpec((step * per_row, BLK * BLK), lambda r: (r, 0))] * 2,
        out_specs=[pl.BlockSpec((step, *shape), lambda r: (r, 0, 0)) for shape in shapes],
        scratch_shapes=[
            pltpu.VMEM((per_row * HALF, per_row * HALF), BF16),
            pltpu.VMEM((lanes, 2 * lanes), BF16),
        ],
        compiler_params=pltpu.CompilerParams(vmem_limit_bytes=24 * MIB),
        cost_estimate=pl.CostEstimate(
            flops=8 * mm, bytes_accessed=12 * kept * BLK * BLK, transcendentals=0
        ),
        name="prepare",
    )(
        plan,
        pltpu.with_memory_space_constraint(w_in, pltpu.HBM),
        pltpu.with_memory_space_constraint(w_out, pltpu.HBM),
    )

    late, near_piece, gathered, p_out = lax.optimization_barrier(
        (pieces[1:], near_piece, gathered, p_out)
    )
    column = jnp.concatenate(late, axis=0)
    far_pieces = [column] + [lax.ppermute(column, "mp", near[q]) for q in (1, 2)]
    near_piece.append(lax.ppermute(near_piece[2], "mp", near[1]))

    hidden_f32 = pltpu.VMEM((col_blocks, BLK, tok), F32)
    turned = pltpu.VMEM((feat, tok), BF16)

    def hidden_bf16(*chunks):
        return jax.ShapeDtypeStruct((*chunks, col_blocks, BLK, tok), BF16)

    def flat(chunks):
        return jax.ShapeDtypeStruct((chunks * tok, feat), BF16)

    def call(kernel, out_shape, scratch, limit, flops, transcendentals, *args):
        return pl.pallas_call(
            kernel,
            out_shape=out_shape,
            grid_spec=pltpu.PrefetchScalarGridSpec(
                num_scalar_prefetch=1,
                grid=(),
                in_specs=[whole] * (len(args) - 1),
                out_specs=[whole] * len(out_shape),
                scratch_shapes=scratch,
            ),
            compiler_params=pltpu.CompilerParams(vmem_limit_bytes=limit * MIB),
            cost_estimate=pl.CostEstimate(
                flops=flops, bytes_accessed=flops // (4 * tok), transcendentals=transcendentals
            ),
            name=(kernel.func if isinstance(kernel, functools.partial) else kernel).__name__,
        )(*args)

    scratch = [turned, turned, hidden_f32, hidden_f32]
    act, gp_own, n_own = call(
        local_kernel, [hidden_bf16(), hidden_bf16(), flat(1)], scratch, 32, 8 * mm, tok * hidden,
        plan, gain_row, *gathered, a_in, p_out,
    )
    far_pieces[2], n_own = lax.optimization_barrier((far_pieces[2], n_own))
    far_pieces.append(lax.ppermute(far_pieces[2], "mp", near[1]))
    gp_near, n_near = call(
        chunk_kernel, [hidden_bf16(1), flat(1)], scratch, 32, 8 * mm, tok * hidden // 2,
        plan, gain_row, *near_piece, a_in, p_out,
    )
    gp_far, n_far = call(
        chunk_kernel, [hidden_bf16(z_count - 2), flat(z_count - 2)], scratch, 32, 16 * mm, tok * hidden,
        plan, gain_row, *far_pieces, a_in, p_out,
    )

    def blocks(list_row, dtype, flops, plan):
        return call(
            functools.partial(block_kernel, list_row, scale),
            [jax.ShapeDtypeStruct((cap, HALF, lanes), dtype)],
            [pltpu.VMEM((cap + 1, HALF, lanes), F32)],
            16, flops, 0,
            plan, gp_own, gp_near, gp_far, n_own, n_near, n_far, p_out,
        )[0]

    for_peer = blocks(2, BF16, 2 * mm, plan)
    for_peer, plan_later, act = lax.optimization_barrier((for_peer, plan, act))
    arrived = lax.ppermute(for_peer, "dp", across_x)
    parts = call(
        contract_kernel,
        [jax.ShapeDtypeStruct((2 * tok, width), BF16)] * mp_count,
        [turned, turned],
        16, 0, 0,
        plan_later, act, gp_own, b_in, a_out,
    )
    for_own = blocks(6, F32, 0, plan_later)
    summed = [parts[0]] + [lax.ppermute(parts[q], "mp", near[q]) for q in range(1, mp_count)]
    steps = 4
    own_rows = pl.BlockSpec((cap // steps, HALF, lanes), lambda i: (i, 0, 0))
    token_rows = pl.BlockSpec((2 * tok, width), lambda i: (0, 0))
    result = pl.BlockSpec((tok, width), lambda i: (0, 0))
    branch, grad_normed, owned_grad = pl.pallas_call(
        finish_kernel,
        out_shape=[
            jax.ShapeDtypeStruct((tok, width), BF16),
            jax.ShapeDtypeStruct((tok, width), BF16),
            jax.ShapeDtypeStruct((cap, BLK * BLK), F32),
        ],
        grid=(steps,),
        in_specs=[own_rows] * 2 + [token_rows] * mp_count,
        out_specs=[result, result, pl.BlockSpec((cap // steps, BLK * BLK), lambda i: (i, 0))],
        compiler_params=pltpu.CompilerParams(vmem_limit_bytes=16 * MIB),
        cost_estimate=pl.CostEstimate(flops=0, bytes_accessed=0, transcendentals=0),
        name="finish",
    )(for_own, arrived, *summed)
    return (branch, grad_normed, owned_grad[None])


def sum_sources(received):
    return jnp.sum(received, axis=0)


def body(x_in, gain, w_in, w_out, grad_out, block_cols, slots):
    whole_x, whole_grad = (
        lax.all_gather(x_in, "mp", axis=1, tiled=True),
        lax.all_gather(grad_out, "mp", axis=1, tiled=True),
    )
    tok_rows = whole_x.shape[0]
    feat_width = whole_x.shape[1]
    row_blocks = feat_width // BLK
    kept_count = w_in.shape[0]
    per_row = kept_count // row_blocks
    col_blocks = FF // lax.axis_size("mp") // BLK
    col_ids = block_cols[0]
    slot_ids = slots[0]
    x_float = whole_x.astype(jnp.float32)
    inv_rms = lax.rsqrt(jnp.mean(x_float * x_float, axis=-1, keepdims=True) + norm_eps)
    normed = (x_float * inv_rms * gain).astype(jnp.bfloat16)
    normed_cols = normed.reshape(tok_rows, row_blocks, BLK).transpose(1, 2, 0)
    grad_cols = whole_grad.reshape(tok_rows, row_blocks, BLK).transpose(1, 2, 0)
    in_blocks = w_in.reshape(row_blocks, per_row, BLK, BLK)
    out_blocks = w_out.reshape(row_blocks, per_row, BLK, BLK)
    col_onehot = (col_ids[None, :] == jnp.arange(col_blocks, dtype=jnp.int32)[:, None]).astype(
        jnp.float32
    )
    pre_parts = jnp.einsum(
        "rkbc,rbt->rkct", in_blocks, normed_cols, preferred_element_type=jnp.float32
    )
    pre_act = jnp.dot(
        col_onehot,
        pre_parts.reshape(kept_count, BLK * tok_rows),
        precision=lax.Precision.HIGHEST,
        preferred_element_type=jnp.float32,
    )
    pre_act = pre_act.reshape(col_blocks, BLK, tok_rows)
    activation = gelu_value(pre_act).astype(jnp.bfloat16)
    act_blocks = jnp.take(activation, col_ids, axis=0).reshape(row_blocks, per_row, BLK, tok_rows)
    branch_cols = jnp.einsum(
        "rkcb,rkct->rbt", out_blocks, act_blocks, preferred_element_type=jnp.float32
    )
    branch_part = branch_cols.transpose(2, 0, 1).reshape(tok_rows, feat_width)
    branch = lax.psum_scatter(branch_part, "mp", scatter_dimension=1, tiled=True).astype(
        jnp.bfloat16
    )
    act_parts = jnp.einsum(
        "rkcb,rbt->rkct", out_blocks, grad_cols, preferred_element_type=jnp.float32
    )
    grad_act = jnp.dot(
        col_onehot,
        act_parts.reshape(kept_count, BLK * tok_rows),
        precision=lax.Precision.HIGHEST,
        preferred_element_type=jnp.float32,
    )
    grad_act = grad_act.reshape(col_blocks, BLK, tok_rows)
    grad_pre = (grad_act * gelu_slope(pre_act)).astype(jnp.bfloat16)
    pre_blocks = jnp.take(grad_pre, col_ids, axis=0).reshape(row_blocks, per_row, BLK, tok_rows)
    dp_count = lax.axis_size("dp")
    weight_scale = 1.0 / math.sqrt(tok_rows * dp_count)
    block_terms = jnp.einsum(
        "rkct,rbt->rkcb", pre_blocks, normed_cols, preferred_element_type=jnp.float32
    )
    block_partial = (block_terms * weight_scale).reshape(kept_count, BLK * BLK)
    capacity = 2 * kept_count // dp_count
    outgoing = (
        jnp.zeros((dp_count * capacity, BLK * BLK), jnp.float32).at[slot_ids].set(block_partial)
    )
    outgoing = outgoing.reshape(dp_count, capacity, BLK * BLK)
    owned_grad = sum_sources(
        lax.all_to_all(
            outgoing.astype(jnp.bfloat16), "dp", split_axis=0, concat_axis=0, tiled=True
        ).astype(outgoing.dtype)
    )
    normed_part = jnp.einsum(
        "rkbc,rkct->rbt", in_blocks, pre_blocks, preferred_element_type=jnp.float32
    )
    normed_part = normed_part.transpose(2, 0, 1).reshape(tok_rows, feat_width)
    grad_normed = lax.psum_scatter(normed_part, "mp", scatter_dimension=1, tiled=True).astype(
        jnp.bfloat16
    )
    return (branch, grad_normed, owned_grad[None])


def solution(mesh):
    placed = (
        P("dp", "mp"),
        P(),
        P("mp", None),
        P("mp", None),
        P("dp", "mp"),
        P("mp", None),
        P("mp", None),
    )
    fits = mesh.shape["dp"] == 8 and mesh.shape["mp"] == 4
    return jax.shard_map(
        fast_body if fits else body,
        mesh=mesh,
        in_specs=placed,
        out_specs=(P("dp", "mp"), P("dp", "mp"), P("mp", "dp", None)),
        check_vma=False,
    )
```

```python
import functools
import math

import jax
import jax.numpy as jnp
from jax import lax
from jax.experimental import pallas as pl
from jax.experimental.pallas import tpu as pltpu
from jax.sharding import PartitionSpec as P

FF = 32768
BLK = 64
HALF = BLK // 2
GROUP = 4
FIRST = 1024
BATCH = 12
BEND = 8


norm_eps = 1e-06
tanh_coef = 0.7978845608028654

F32 = jnp.float32
BF16 = jnp.bfloat16
MIB = 1024 * 1024


def gelu_value(pre_act):
    cubic = pre_act * pre_act * pre_act
    slope_arg = jnp.tanh(tanh_coef * (pre_act + 0.044715 * cubic))
    return 0.5 * pre_act * (1.0 + slope_arg)


def gelu_slope(pre_act):
    cubic = pre_act * pre_act * pre_act
    slope_arg = jnp.tanh(tanh_coef * (pre_act + 0.044715 * cubic))
    inner = tanh_coef * (1.0 + 0.134145 * pre_act * pre_act)
    return 0.5 * (1.0 + slope_arg) + 0.5 * pre_act * (1.0 - slope_arg * slope_arg) * inner


def gelu_both(v):
    square = v * v
    th = jnp.tanh(v * (tanh_coef + (tanh_coef * 0.044715) * square))
    gate = 0.5 + 0.5 * th
    inner = 2.0 * tanh_coef + (2.0 * tanh_coef * 0.134145) * square
    return v * gate, gate + v * (gate - gate * gate) * inner


def dot(a, b, dims=((1,), (0,))):
    return lax.dot_general(a, b, (dims, ((), ())), preferred_element_type=F32)


def iota(shape, axis):
    return lax.broadcasted_iota(jnp.int32, shape, axis)


def even_first(width):
    row, col = iota((width, width), 0), iota((width, width), 1)
    inside = row & (BLK - 1)
    target = (row - inside) + (inside & 1) * HALF + (inside >> 1)
    return jnp.where(col == target, 1.0, 0.0).astype(BF16)


def stack_kernel(x_ref, grad_ref, both_ref):
    tok = x_ref.shape[0]
    both_ref[:tok, :] = x_ref[...]
    both_ref[tok:, :] = grad_ref[...]


def plan_kernel(cap, col_blocks, row_blocks, cols_ref, slots_ref, out_ref):
    kept = cols_ref.shape[1]
    per_row = kept // row_blocks
    me = lax.axis_index("dp")
    cols, slots = cols_ref[...], slots_ref[...]
    owner = lax.div(slots, jnp.int32(cap))
    own = jnp.where(owner == me, 1.0, 0.0)
    peer = jnp.where(owner == (me ^ 1), 1.0, 0.0)
    needed = jnp.max(
        jnp.where(cols == iota((col_blocks, kept), 0), own + peer, 0.0), axis=1, keepdims=True
    )

    def to_column(row):
        size = row.shape[1]
        eye = iota((size, size), 0) == iota((size, size), 1)
        return jnp.sum(jnp.where(eye, row, 0.0), axis=1, keepdims=True)

    def to_row(column):
        size = column.shape[0]
        eye = iota((size, size), 0) == iota((size, size), 1)
        return jnp.sum(jnp.where(eye, column, 0.0), axis=0, keepdims=True)

    def listed(flags_r, flags_c):
        size = flags_r.shape[1]
        before = iota((size, size), 1) < iota((size, size), 0)
        place = jnp.sum(jnp.where(before, flags_r, 0.0), axis=1, keepdims=True)
        hit = (place == iota((size, kept), 1).astype(F32)) & (flags_c > 0)
        index = iota((size, 1), 0).astype(F32)
        return jnp.sum(jnp.where(hit, index, 0.0), axis=0, keepdims=True)

    cols_r = cols.astype(F32)
    cols_c = to_column(cols_r)
    earlier = iota((kept, kept), 1) < iota((kept, kept), 0)
    seen = jnp.max(jnp.where(earlier & (cols_r == cols_c), 1.0, 0.0), axis=1, keepdims=True)
    peer_c, own_c = to_column(peer), to_column(own)
    pair_end = iota((kept, kept), 0) < 2 * per_row * iota((kept, kept), 1)

    def starts(flags_c):
        return jnp.sum(jnp.where(pair_end, flags_c, 0.0), axis=0, keepdims=True)

    rows = [
        cols_r + FIRST * (1.0 - to_row(seen)),
        (slots - owner * cap).astype(F32),
        listed(peer, peer_c),
        starts(peer_c),
        listed(to_row(needed), needed),
        jnp.sum(needed, axis=0, keepdims=True),
        listed(own, own_c),
        starts(own_c),
    ]
    for index, row in enumerate(rows):
        out_ref[index : index + 1, :] = jnp.broadcast_to(row, (1, kept)).astype(jnp.int32)


def prepare_kernel(plan_ref, win_ref, wout_ref, a_in, b_in, p_out, a_out, order, both):
    count = a_in.shape[0]
    per_row, length = win_ref.shape[0] // count, win_ref.shape[1]
    lanes = 2 * BLK
    rows = per_row * HALF

    @pl.when(pl.program_id(0) == 0)
    def _():
        row, col = iota((rows, rows), 0), iota((rows, rows), 1)
        source = (row & (HALF - 1)) * per_row + lax.div(row, jnp.int32(HALF))
        order[...] = jnp.where(col == source, 1.0, 0.0).astype(BF16)
        row, col = iota((lanes, lanes), 0), iota((lanes, lanes), 1)
        swap = jnp.where(((col + BLK) & (lanes - 1)) == row, 1.0, 0.0).astype(BF16)
        perm = even_first(lanes)
        both[:, :lanes] = perm
        both[:, lanes:] = dot(perm, swap).astype(BF16)

    def by_block(ref):
        stacked = [
            jnp.concatenate(
                [
                    ref[n * per_row : (n + 1) * per_row, j * lanes : (j + 1) * lanes]
                    for j in range(length // lanes)
                ],
                axis=0,
            )
            for n in range(count)
        ]
        return dot(order[...], jnp.concatenate(stacked, axis=1)).astype(BF16)

    ordered_in, ordered_out = by_block(win_ref), by_block(wout_ref)
    left = iota((HALF, lanes), 1) < BLK
    left2 = iota((BLK, lanes), 1) < BLK
    for n in range(count):
        of_n = slice(n * lanes, (n + 1) * lanes)
        kept_in = dot(ordered_in[:, of_n], both[...])
        kept_out = ordered_out[:, of_n]
        p_out[n] = kept_out
        for pair in range(per_row // 2):
            first = kept_in[2 * pair * HALF : (2 * pair + 1) * HALF]
            second = kept_in[(2 * pair + 1) * HALF : (2 * pair + 2) * HALF]
            at = slice(pair * lanes, (pair + 1) * lanes)
            b_in[n, :HALF, at] = jnp.where(left, first[:, :lanes], second[:, lanes:]).astype(BF16)
            b_in[n, HALF:, at] = jnp.where(left, first[:, lanes:], second[:, :lanes]).astype(BF16)
        for quad in range(per_row // GROUP):
            rows_of = slice(quad * lanes, (quad + 1) * lanes)
            straight, swapped = kept_in[rows_of, :lanes], kept_in[rows_of, lanes:]
            pairs = jnp.concatenate(
                [
                    jnp.where(left2, straight[:BLK], swapped[BLK:]),
                    jnp.where(left2, swapped[:BLK], straight[BLK:]),
                ],
                axis=0,
            )
            a_in[n, rows_of, :] = pairs.astype(BF16).T
            turned = kept_out[rows_of].T
            a_out[n, :, rows_of] = turned[:BLK]
            a_out[n, :, rows + quad * lanes : rows + (quad + 1) * lanes] = turned[BLK:]


def load_tokens(pieces, tok, gain_ref, perm, n_s, nt_s, gt_s, base):
    mine = lax.axis_index("mp")
    width = pieces[0][0].shape[1]
    values, total = [], 0.0
    for ref, first in pieces:
        value = ref[first : first + tok, :].astype(F32)
        values.append(value)
        total = total + jnp.sum(value * value, axis=-1, keepdims=True)
    inv_rms = lax.rsqrt(total / (width * len(pieces)) + norm_eps)
    for q, (ref, first) in enumerate(pieces):
        at = pl.ds(pl.multiple_of((mine ^ q) * width, width), width)
        normed = (values[q] * inv_rms * gain_ref[:, at]).astype(BF16)
        n_s[base : base + tok, at] = normed
        nt_s[at, :] = dot(normed, perm).astype(BF16).T
        gt_s[at, :] = ref[first + tok : first + 2 * tok, :].T


def expand(plan, a_in, p_out, nt_s, gt_s, acc_v, acc_a):
    row_blocks = a_in.shape[0]
    tok = nt_s.shape[1]
    per_row = p_out.shape[1] // HALF
    gap = jnp.zeros((HALF, tok), BF16)
    gap2 = jnp.zeros((BLK, tok), BF16)

    def step(r, carry):
        at = pl.ds(pl.multiple_of(r * BLK, BLK), BLK)
        normed, cot = nt_s[at, :], gt_s[at, :]
        spread = []
        for a in (0, 1):
            part = normed[a * HALF : (a + 1) * HALF]
            spread.append(jnp.concatenate([part, gap], axis=1))
            spread.append(jnp.concatenate([gap, part], axis=1))
        terms_v = dot(a_in[r], jnp.concatenate(spread, axis=0))
        cots = jnp.concatenate(
            [jnp.concatenate([cot, gap2], axis=1), jnp.concatenate([gap2, cot], axis=1)], axis=0
        )
        terms_a = dot(p_out[r], cots)
        for quad in range(per_row // GROUP):
            new = []
            for u in range(GROUP):
                k = quad * GROUP + u
                code = plan[0, r * per_row + k]
                c, first = code & (FIRST - 1), code >= FIRST
                rows = terms_v[(k // 2) * BLK : (k // 2 + 1) * BLK]
                v = rows[:, (k % 2) * tok : (k % 2 + 1) * tok]
                rows = terms_a[k * HALF : (k + 1) * HALF]
                a = jnp.concatenate([rows[:, :tok], rows[:, tok:]], axis=0)
                v = jnp.where(first, v, acc_v[c] + v)
                a = jnp.where(first, a, acc_a[c] + a)
                new.append((c, v, a))
            for c, v, a in new:
                acc_v[c] = v
                acc_a[c] = a
        return carry

    lax.fori_loop(0, row_blocks, step, 0, unroll=16)


def local_kernel(
    plan, gain_ref, s0, s1, s2, s3, a_in, p_out, act_ref, gp_ref, n_ref, nt_s, gt_s, acc_v, acc_a
):
    tok = n_ref.shape[0]
    perm = even_first(s0.shape[1])
    load_tokens([(ref, 0) for ref in (s0, s1, s2, s3)], tok, gain_ref, perm, n_ref, nt_s, gt_s, 0)
    expand(plan, a_in, p_out, nt_s, gt_s, acc_v, acc_a)

    def bend(c, carry):
        value, slope = gelu_both(acc_v[c])
        act_ref[c] = value.astype(BF16)
        gp_ref[c] = (acc_a[c] * slope).astype(BF16)
        return carry

    lax.fori_loop(0, gp_ref.shape[0], bend, 0, unroll=4)


def contract_kernel(plan, act_ref, gp_ref, b_in, a_out, o0, o1, o2, o3, br_s, gn_s):
    tok, width = o0.shape[0] // 2, o0.shape[1]
    row_blocks, per_row = b_in.shape[0], b_in.shape[2] // BLK
    perm = even_first(width)

    def contract(r, carry):
        at = pl.ds(pl.multiple_of(r * BLK, BLK), BLK)
        ids = [plan[0, r * per_row + k] & (FIRST - 1) for k in range(per_row)]
        acts = [act_ref[c, a * HALF : (a + 1) * HALF, :] for a in (0, 1) for c in ids]
        br_s[at, :] = dot(a_out[r], jnp.concatenate(acts, axis=0)).astype(BF16)
        grads = [gp_ref[c] for c in ids]
        gn_s[at, :] = dot(b_in[r], jnp.concatenate(grads, axis=0)).astype(BF16)
        return carry

    lax.fori_loop(0, row_blocks, contract, 0, unroll=8)
    mine = lax.axis_index("mp")
    for q, out in enumerate((o0, o1, o2, o3)):
        at = pl.ds(pl.multiple_of((mine ^ q) * width, width), width)
        out[:tok, :] = br_s[at, :].T
        out[tok:, :] = dot(gn_s[at, :].T, perm, ((1,), (1,))).astype(BF16)


def chunk_kernel(
    plan, gain_ref, s0, s1, s2, s3, a_in, p_out, gp_ref, n_ref, nt_s, gt_s, acc_v, acc_a
):
    chunks = gp_ref.shape[0]
    tok = n_ref.shape[0] // chunks
    perm = even_first(s0.shape[1])
    count = plan[5, 0]
    for j in range(chunks):
        pieces = [(ref, 2 * tok * j) for ref in (s0, s1, s2, s3)]
        load_tokens(pieces, tok, gain_ref, perm, n_ref, nt_s, gt_s, j * tok)
        expand(plan, a_in, p_out, nt_s, gt_s, acc_v, acc_a)

        def bend(i, carry):
            for u in range(BEND):
                c = plan[4, jnp.minimum(i * BEND + u, count - 1)]
                _, slope = gelu_both(acc_v[c])
                gp_ref[j, c] = (acc_a[c] * slope).astype(BF16)
            return carry

        lax.fori_loop(0, (count + BEND - 1) // BEND, bend, 0)


def block_kernel(
    list_row, scale, plan, gp0, gp1, gp2, n0, n1, n2, p_out, out_ref, found
):
    per_row = p_out.shape[1] // HALF
    lanes = 2 * BLK
    pairs = p_out.shape[0] // 2
    cap = out_ref.shape[0]
    left = iota((HALF, lanes), 1) < BLK
    found[...] = jnp.zeros_like(found)

    def form(pair, first):
        end = plan[list_row + 1, pair + 1]
        at_lane = pl.ds(pl.multiple_of(pair * lanes, lanes), lanes)
        ids = [
            plan[list_row, jnp.maximum(jnp.minimum(first + u, end - 1), 0)] for u in range(BATCH)
        ]
        grads = []
        for k in ids:
            c = plan[0, k] & (FIRST - 1)
            chunks = [gp0[c]] + [ref[j, c] for ref in (gp1, gp2) for j in range(ref.shape[0])]
            grads.append(jnp.concatenate(chunks, axis=1))
        normed = jnp.concatenate([ref[:, at_lane] for ref in (n0, n1, n2)], axis=0)
        blocks = dot(jnp.concatenate(grads, axis=0), normed) * scale
        done = []
        for u, k in enumerate(ids):
            odd = (lax.div(k, jnp.int32(per_row)) & 1) == 1
            top = blocks[u * BLK : u * BLK + HALF]
            low = blocks[u * BLK + HALF : (u + 1) * BLK]
            top = jnp.where(odd, pltpu.roll(top, BLK, 1), top)
            low = jnp.where(odd, low, pltpu.roll(low, BLK, 1))
            slot = jnp.where(first < end, plan[1, k], cap)
            done.append((slot, jnp.where(left, top, low)))
        for slot, value in done:
            found[slot] = value

    def begin(pair, carry):
        form(pair, plan[list_row + 1, pair])
        return carry

    lax.fori_loop(0, pairs, begin, 0, unroll=8)

    def finish(pair, carry):
        begin, end = plan[list_row + 1, pair], plan[list_row + 1, pair + 1]

        def more(i, carry):
            form(pair, begin + i * BATCH)
            return carry

        return lax.fori_loop(1, (end - begin + BATCH - 1) // BATCH, more, carry)

    lax.fori_loop(0, pairs, finish, 0)
    out_ref[...] = found[:cap].astype(out_ref.dtype)


def finish_kernel(own_ref, arrived_ref, s0, s1, s2, s3, branch_ref, normed_ref, out_ref):
    lanes = own_ref.shape[2]
    rows = 8
    for first in range(0, own_ref.shape[0], rows):
        at = slice(first, first + rows)
        blocks = own_ref[at] + arrived_ref[at].astype(F32)
        turned = jnp.swapaxes(blocks, 0, 1)
        for j in range(turned.shape[0]):
            out_ref[at, j * lanes : (j + 1) * lanes] = turned[j]

    @pl.when(pl.program_id(0) == 0)
    def _():
        tok = branch_ref.shape[0]
        for out, base in ((branch_ref, 0), (normed_ref, tok)):
            total = sum(ref[base : base + tok, :].astype(F32) for ref in (s0, s1, s2, s3))
            out[...] = total.astype(BF16)


def fast_body(x_in, gain, w_in, w_out, grad_out, block_cols, slots):
    dp_count, mp_count = lax.axis_size("dp"), lax.axis_size("mp")
    tok, width = x_in.shape
    feat = width * mp_count
    kept = w_in.shape[0]
    row_blocks = feat // BLK
    per_row = kept // row_blocks
    hidden = FF // mp_count
    col_blocks = hidden // BLK
    lanes = 2 * BLK
    cap = 2 * kept // dp_count
    scale = 1.0 / math.sqrt(tok * dp_count)
    across_x = [(i, i ^ 1) for i in range(dp_count)]
    near = [[(i, i ^ q) for i in range(mp_count)] for q in range(mp_count)]
    z_count = dp_count // 2
    along_z = [[(i, i ^ (2 * j)) for i in range(dp_count)] for j in (1, 3, 2)]

    whole = pl.BlockSpec(memory_space=pltpu.VMEM)
    mm = 2 * tok * kept * BLK * BLK

    own = pl.pallas_call(
        stack_kernel,
        out_shape=jax.ShapeDtypeStruct((2 * tok, width), BF16),
        cost_estimate=pl.CostEstimate(flops=0, bytes_accessed=8 * tok * width, transcendentals=0),
        name="stack",
    )(x_in, grad_out)
    pieces = [lax.ppermute(own, "dp", along_z[0])]
    gathered = [own] + [lax.ppermute(own, "mp", near[q]) for q in range(1, mp_count)]
    gathered[1], own_late = lax.optimization_barrier((gathered[1], own))
    pieces += [lax.ppermute(own_late, "dp", hop) for hop in along_z[1:]]
    pieces[0], cols_late, slots_late = lax.optimization_barrier((pieces[0], block_cols, slots))
    plan = pl.pallas_call(
        functools.partial(plan_kernel, cap, col_blocks, row_blocks),
        out_shape=jax.ShapeDtypeStruct((8, kept), jnp.int32),
        cost_estimate=pl.CostEstimate(flops=4_000_000, bytes_accessed=16384, transcendentals=0),
        name="plan",
    )(cols_late, slots_late)
    near_piece = [pieces[0]] + [lax.ppermute(pieces[0], "mp", near[q]) for q in (1, 2)]
    gain_row = gain.reshape(1, feat)

    step = min(4, row_blocks)
    shapes = [
        (per_row // 2 * BLK, lanes),
        (BLK, per_row * BLK),
        (per_row * HALF, lanes),
        (BLK, per_row * BLK),
    ]
    a_in, b_in, p_out, a_out = pl.pallas_call(
        prepare_kernel,
        out_shape=[jax.ShapeDtypeStruct((row_blocks, *shape), BF16) for shape in shapes],
        grid=(row_blocks // step,),
        in_specs=[pl.BlockSpec(memory_space=pltpu.SMEM)]
        + [pl.BlockSpec((step * per_row, BLK * BLK), lambda r: (r, 0))] * 2,
        out_specs=[pl.BlockSpec((step, *shape), lambda r: (r, 0, 0)) for shape in shapes],
        scratch_shapes=[
            pltpu.VMEM((per_row * HALF, per_row * HALF), BF16),
            pltpu.VMEM((lanes, 2 * lanes), BF16),
        ],
        compiler_params=pltpu.CompilerParams(vmem_limit_bytes=24 * MIB),
        cost_estimate=pl.CostEstimate(
            flops=8 * mm, bytes_accessed=12 * kept * BLK * BLK, transcendentals=0
        ),
        name="prepare",
    )(
        plan,
        pltpu.with_memory_space_constraint(w_in, pltpu.HBM),
        pltpu.with_memory_space_constraint(w_out, pltpu.HBM),
    )

    late, near_piece, gathered, p_out = lax.optimization_barrier(
        (pieces[1:], near_piece, gathered, p_out)
    )
    column = jnp.concatenate(late, axis=0)
    far_pieces = [column] + [lax.ppermute(column, "mp", near[q]) for q in (1, 2)]
    near_piece.append(lax.ppermute(near_piece[2], "mp", near[1]))

    hidden_f32 = pltpu.VMEM((col_blocks, BLK, tok), F32)
    turned = pltpu.VMEM((feat, tok), BF16)

    def hidden_bf16(*chunks):
        return jax.ShapeDtypeStruct((*chunks, col_blocks, BLK, tok), BF16)

    def flat(chunks):
        return jax.ShapeDtypeStruct((chunks * tok, feat), BF16)

    def call(kernel, out_shape, scratch, limit, flops, transcendentals, *args):
        return pl.pallas_call(
            kernel,
            out_shape=out_shape,
            grid_spec=pltpu.PrefetchScalarGridSpec(
                num_scalar_prefetch=1,
                grid=(),
                in_specs=[whole] * (len(args) - 1),
                out_specs=[whole] * len(out_shape),
                scratch_shapes=scratch,
            ),
            compiler_params=pltpu.CompilerParams(vmem_limit_bytes=limit * MIB),
            cost_estimate=pl.CostEstimate(
                flops=flops, bytes_accessed=flops // (4 * tok), transcendentals=transcendentals
            ),
            name=(kernel.func if isinstance(kernel, functools.partial) else kernel).__name__,
        )(*args)

    scratch = [turned, turned, hidden_f32, hidden_f32]
    act, gp_own, n_own = call(
        local_kernel, [hidden_bf16(), hidden_bf16(), flat(1)], scratch, 32, 8 * mm, tok * hidden,
        plan, gain_row, *gathered, a_in, p_out,
    )
    far_pieces[2], n_own = lax.optimization_barrier((far_pieces[2], n_own))
    far_pieces.append(lax.ppermute(far_pieces[2], "mp", near[1]))
    gp_near, n_near = call(
        chunk_kernel, [hidden_bf16(1), flat(1)], scratch, 32, 8 * mm, tok * hidden // 2,
        plan, gain_row, *near_piece, a_in, p_out,
    )
    gp_far, n_far = call(
        chunk_kernel, [hidden_bf16(z_count - 2), flat(z_count - 2)], scratch, 32, 16 * mm, tok * hidden,
        plan, gain_row, *far_pieces, a_in, p_out,
    )

    def blocks(list_row, dtype, flops, plan):
        return call(
            functools.partial(block_kernel, list_row, scale),
            [jax.ShapeDtypeStruct((cap, HALF, lanes), dtype)],
            [pltpu.VMEM((cap + 1, HALF, lanes), F32)],
            16, flops, 0,
            plan, gp_own, gp_near, gp_far, n_own, n_near, n_far, p_out,
        )[0]

    for_peer = blocks(2, BF16, 2 * mm, plan)
    for_peer, plan_later, act = lax.optimization_barrier((for_peer, plan, act))
    arrived = lax.ppermute(for_peer, "dp", across_x)
    parts = call(
        contract_kernel,
        [jax.ShapeDtypeStruct((2 * tok, width), BF16)] * mp_count,
        [turned, turned],
        16, 0, 0,
        plan_later, act, gp_own, b_in, a_out,
    )
    for_own = blocks(6, F32, 0, plan_later)
    summed = [parts[0]] + [lax.ppermute(parts[q], "mp", near[q]) for q in range(1, mp_count)]
    steps = 4
    own_rows = pl.BlockSpec((cap // steps, HALF, lanes), lambda i: (i, 0, 0))
    token_rows = pl.BlockSpec((2 * tok, width), lambda i: (0, 0))
    result = pl.BlockSpec((tok, width), lambda i: (0, 0))
    branch, grad_normed, owned_grad = pl.pallas_call(
        finish_kernel,
        out_shape=[
            jax.ShapeDtypeStruct((tok, width), BF16),
            jax.ShapeDtypeStruct((tok, width), BF16),
            jax.ShapeDtypeStruct((cap, BLK * BLK), F32),
        ],
        grid=(steps,),
        in_specs=[own_rows] * 2 + [token_rows] * mp_count,
        out_specs=[result, result, pl.BlockSpec((cap // steps, BLK * BLK), lambda i: (i, 0))],
        compiler_params=pltpu.CompilerParams(vmem_limit_bytes=16 * MIB),
        cost_estimate=pl.CostEstimate(flops=0, bytes_accessed=0, transcendentals=0),
        name="finish",
    )(for_own, arrived, *summed)
    return (branch, grad_normed, owned_grad[None])


def sum_sources(received):
    return jnp.sum(received, axis=0)


def body(x_in, gain, w_in, w_out, grad_out, block_cols, slots):
    whole_x, whole_grad = (
        lax.all_gather(x_in, "mp", axis=1, tiled=True),
        lax.all_gather(grad_out, "mp", axis=1, tiled=True),
    )
    tok_rows = whole_x.shape[0]
    feat_width = whole_x.shape[1]
    row_blocks = feat_width // BLK
    kept_count = w_in.shape[0]
    per_row = kept_count // row_blocks
    col_blocks = FF // lax.axis_size("mp") // BLK
    col_ids = block_cols[0]
    slot_ids = slots[0]
    x_float = whole_x.astype(jnp.float32)
    inv_rms = lax.rsqrt(jnp.mean(x_float * x_float, axis=-1, keepdims=True) + norm_eps)
    normed = (x_float * inv_rms * gain).astype(jnp.bfloat16)
    normed_cols = normed.reshape(tok_rows, row_blocks, BLK).transpose(1, 2, 0)
    grad_cols = whole_grad.reshape(tok_rows, row_blocks, BLK).transpose(1, 2, 0)
    in_blocks = w_in.reshape(row_blocks, per_row, BLK, BLK)
    out_blocks = w_out.reshape(row_blocks, per_row, BLK, BLK)
    col_onehot = (col_ids[None, :] == jnp.arange(col_blocks, dtype=jnp.int32)[:, None]).astype(
        jnp.float32
    )
    pre_parts = jnp.einsum(
        "rkbc,rbt->rkct", in_blocks, normed_cols, preferred_element_type=jnp.float32
    )
    pre_act = jnp.dot(
        col_onehot,
        pre_parts.reshape(kept_count, BLK * tok_rows),
        precision=lax.Precision.HIGHEST,
        preferred_element_type=jnp.float32,
    )
    pre_act = pre_act.reshape(col_blocks, BLK, tok_rows)
    activation = gelu_value(pre_act).astype(jnp.bfloat16)
    act_blocks = jnp.take(activation, col_ids, axis=0).reshape(row_blocks, per_row, BLK, tok_rows)
    branch_cols = jnp.einsum(
        "rkcb,rkct->rbt", out_blocks, act_blocks, preferred_element_type=jnp.float32
    )
    branch_part = branch_cols.transpose(2, 0, 1).reshape(tok_rows, feat_width)
    branch = lax.psum_scatter(branch_part, "mp", scatter_dimension=1, tiled=True).astype(
        jnp.bfloat16
    )
    act_parts = jnp.einsum(
        "rkcb,rbt->rkct", out_blocks, grad_cols, preferred_element_type=jnp.float32
    )
    grad_act = jnp.dot(
        col_onehot,
        act_parts.reshape(kept_count, BLK * tok_rows),
        precision=lax.Precision.HIGHEST,
        preferred_element_type=jnp.float32,
    )
    grad_act = grad_act.reshape(col_blocks, BLK, tok_rows)
    grad_pre = (grad_act * gelu_slope(pre_act)).astype(jnp.bfloat16)
    pre_blocks = jnp.take(grad_pre, col_ids, axis=0).reshape(row_blocks, per_row, BLK, tok_rows)
    dp_count = lax.axis_size("dp")
    weight_scale = 1.0 / math.sqrt(tok_rows * dp_count)
    block_terms = jnp.einsum(
        "rkct,rbt->rkcb", pre_blocks, normed_cols, preferred_element_type=jnp.float32
    )
    block_partial = (block_terms * weight_scale).reshape(kept_count, BLK * BLK)
    capacity = 2 * kept_count // dp_count
    outgoing = (
        jnp.zeros((dp_count * capacity, BLK * BLK), jnp.float32).at[slot_ids].set(block_partial)
    )
    outgoing = outgoing.reshape(dp_count, capacity, BLK * BLK)
    owned_grad = sum_sources(
        lax.all_to_all(
            outgoing.astype(jnp.bfloat16), "dp", split_axis=0, concat_axis=0, tiled=True
        ).astype(outgoing.dtype)
    )
    normed_part = jnp.einsum(
        "rkbc,rkct->rbt", in_blocks, pre_blocks, preferred_element_type=jnp.float32
    )
    normed_part = normed_part.transpose(2, 0, 1).reshape(tok_rows, feat_width)
    grad_normed = lax.psum_scatter(normed_part, "mp", scatter_dimension=1, tiled=True).astype(
        jnp.bfloat16
    )
    return (branch, grad_normed, owned_grad[None])


def solution(mesh):
    placed = (
        P("dp", "mp"),
        P(),
        P("mp", None),
        P("mp", None),
        P("dp", "mp"),
        P("mp", None),
        P("mp", None),
    )
    fits = mesh.shape["dp"] == 8 and mesh.shape["mp"] == 4
    return jax.shard_map(
        fast_body if fits else body,
        mesh=mesh,
        in_specs=placed,
        out_specs=(P("dp", "mp"), P("dp", "mp"), P("mp", "dp", None)),
        check_vma=False,
    )
```

```python
import functools
import math

import jax
import jax.numpy as jnp
from jax import lax
from jax.experimental import pallas as pl
from jax.experimental.pallas import tpu as pltpu
from jax.sharding import PartitionSpec as P

FF = 32768
BLK = 64
HALF = BLK // 2
GROUP = 4
FIRST = 1024
BATCH = 12
BEND = 8


norm_eps = 1e-06
tanh_coef = 0.7978845608028654

F32 = jnp.float32
BF16 = jnp.bfloat16
MIB = 1024 * 1024


def gelu_value(pre_act):
    cubic = pre_act * pre_act * pre_act
    slope_arg = jnp.tanh(tanh_coef * (pre_act + 0.044715 * cubic))
    return 0.5 * pre_act * (1.0 + slope_arg)


def gelu_slope(pre_act):
    cubic = pre_act * pre_act * pre_act
    slope_arg = jnp.tanh(tanh_coef * (pre_act + 0.044715 * cubic))
    inner = tanh_coef * (1.0 + 0.134145 * pre_act * pre_act)
    return 0.5 * (1.0 + slope_arg) + 0.5 * pre_act * (1.0 - slope_arg * slope_arg) * inner


def gelu_both(v):
    square = v * v
    th = jnp.tanh(v * (tanh_coef + (tanh_coef * 0.044715) * square))
    gate = 0.5 + 0.5 * th
    inner = 2.0 * tanh_coef + (2.0 * tanh_coef * 0.134145) * square
    return v * gate, gate + v * (gate - gate * gate) * inner


def dot(a, b, dims=((1,), (0,))):
    return lax.dot_general(a, b, (dims, ((), ())), preferred_element_type=F32)


def iota(shape, axis):
    return lax.broadcasted_iota(jnp.int32, shape, axis)


def even_first(width):
    row, col = iota((width, width), 0), iota((width, width), 1)
    inside = row & (BLK - 1)
    target = (row - inside) + (inside & 1) * HALF + (inside >> 1)
    return jnp.where(col == target, 1.0, 0.0).astype(BF16)


def stack_kernel(x_ref, grad_ref, both_ref):
    tok = x_ref.shape[0]
    both_ref[:tok, :] = x_ref[...]
    both_ref[tok:, :] = grad_ref[...]


def plan_kernel(cap, col_blocks, row_blocks, cols_ref, slots_ref, out_ref):
    kept = cols_ref.shape[1]
    per_row = kept // row_blocks
    me = lax.axis_index("dp")
    cols, slots = cols_ref[...], slots_ref[...]
    owner = lax.div(slots, jnp.int32(cap))
    own = jnp.where(owner == me, 1.0, 0.0)
    peer = jnp.where(owner == (me ^ 1), 1.0, 0.0)
    needed = jnp.max(
        jnp.where(cols == iota((col_blocks, kept), 0), own + peer, 0.0), axis=1, keepdims=True
    )

    def to_column(row):
        size = row.shape[1]
        eye = iota((size, size), 0) == iota((size, size), 1)
        return jnp.sum(jnp.where(eye, row, 0.0), axis=1, keepdims=True)

    def to_row(column):
        size = column.shape[0]
        eye = iota((size, size), 0) == iota((size, size), 1)
        return jnp.sum(jnp.where(eye, column, 0.0), axis=0, keepdims=True)

    def listed(flags_r, flags_c):
        size = flags_r.shape[1]
        before = iota((size, size), 1) < iota((size, size), 0)
        place = jnp.sum(jnp.where(before, flags_r, 0.0), axis=1, keepdims=True)
        hit = (place == iota((size, kept), 1).astype(F32)) & (flags_c > 0)
        index = iota((size, 1), 0).astype(F32)
        return jnp.sum(jnp.where(hit, index, 0.0), axis=0, keepdims=True)

    cols_r = cols.astype(F32)
    cols_c = to_column(cols_r)
    earlier = iota((kept, kept), 1) < iota((kept, kept), 0)
    seen = jnp.max(jnp.where(earlier & (cols_r == cols_c), 1.0, 0.0), axis=1, keepdims=True)
    peer_c, own_c = to_column(peer), to_column(own)
    pair_end = iota((kept, kept), 0) < 2 * per_row * iota((kept, kept), 1)

    def starts(flags_c):
        return jnp.sum(jnp.where(pair_end, flags_c, 0.0), axis=0, keepdims=True)

    rows = [
        cols_r + FIRST * (1.0 - to_row(seen)),
        (slots - owner * cap).astype(F32),
        listed(peer, peer_c),
        starts(peer_c),
        listed(to_row(needed), needed),
        jnp.sum(needed, axis=0, keepdims=True),
        listed(own, own_c),
        starts(own_c),
    ]
    for index, row in enumerate(rows):
        out_ref[index : index + 1, :] = jnp.broadcast_to(row, (1, kept)).astype(jnp.int32)


def prepare_kernel(plan_ref, win_ref, wout_ref, a_in, b_in, p_out, a_out, order, both):
    count = a_in.shape[0]
    per_row, length = win_ref.shape[0] // count, win_ref.shape[1]
    lanes = 2 * BLK
    rows = per_row * HALF

    @pl.when(pl.program_id(0) == 0)
    def _():
        row, col = iota((rows, rows), 0), iota((rows, rows), 1)
        source = (row & (HALF - 1)) * per_row + lax.div(row, jnp.int32(HALF))
        order[...] = jnp.where(col == source, 1.0, 0.0).astype(BF16)
        row, col = iota((lanes, lanes), 0), iota((lanes, lanes), 1)
        swap = jnp.where(((col + BLK) & (lanes - 1)) == row, 1.0, 0.0).astype(BF16)
        perm = even_first(lanes)
        both[:, :lanes] = perm
        both[:, lanes:] = dot(perm, swap).astype(BF16)

    def by_block(ref):
        stacked = [
            jnp.concatenate(
                [
                    ref[n * per_row : (n + 1) * per_row, j * lanes : (j + 1) * lanes]
                    for j in range(length // lanes)
                ],
                axis=0,
            )
            for n in range(count)
        ]
        return dot(order[...], jnp.concatenate(stacked, axis=1)).astype(BF16)

    ordered_in, ordered_out = by_block(win_ref), by_block(wout_ref)
    left = iota((HALF, lanes), 1) < BLK
    left2 = iota((BLK, lanes), 1) < BLK
    for n in range(count):
        of_n = slice(n * lanes, (n + 1) * lanes)
        kept_in = dot(ordered_in[:, of_n], both[...])
        kept_out = ordered_out[:, of_n]
        p_out[n] = kept_out
        for pair in range(per_row // 2):
            first = kept_in[2 * pair * HALF : (2 * pair + 1) * HALF]
            second = kept_in[(2 * pair + 1) * HALF : (2 * pair + 2) * HALF]
            at = slice(pair * lanes, (pair + 1) * lanes)
            b_in[n, :HALF, at] = jnp.where(left, first[:, :lanes], second[:, lanes:]).astype(BF16)
            b_in[n, HALF:, at] = jnp.where(left, first[:, lanes:], second[:, :lanes]).astype(BF16)
        for quad in range(per_row // GROUP):
            rows_of = slice(quad * lanes, (quad + 1) * lanes)
            straight, swapped = kept_in[rows_of, :lanes], kept_in[rows_of, lanes:]
            pairs = jnp.concatenate(
                [
                    jnp.where(left2, straight[:BLK], swapped[BLK:]),
                    jnp.where(left2, swapped[:BLK], straight[BLK:]),
                ],
                axis=0,
            )
            a_in[n, rows_of, :] = pairs.astype(BF16).T
            turned = kept_out[rows_of].T
            a_out[n, :, rows_of] = turned[:BLK]
            a_out[n, :, rows + quad * lanes : rows + (quad + 1) * lanes] = turned[BLK:]


def load_tokens(pieces, tok, gain_ref, perm, n_s, nt_s, gt_s, base):
    mine = lax.axis_index("mp")
    width = pieces[0][0].shape[1]
    values, total = [], 0.0
    for ref, first in pieces:
        value = ref[first : first + tok, :].astype(F32)
        values.append(value)
        total = total + jnp.sum(value * value, axis=-1, keepdims=True)
    inv_rms = lax.rsqrt(total / (width * len(pieces)) + norm_eps)
    for q, (ref, first) in enumerate(pieces):
        at = pl.ds(pl.multiple_of((mine ^ q) * width, width), width)
        normed = (values[q] * inv_rms * gain_ref[:, at]).astype(BF16)
        n_s[base : base + tok, at] = normed
        nt_s[at, :] = dot(normed, perm).astype(BF16).T
        gt_s[at, :] = ref[first + tok : first + 2 * tok, :].T


def expand(plan, a_in, p_out, nt_s, gt_s, acc_v, acc_a):
    row_blocks = a_in.shape[0]
    tok = nt_s.shape[1]
    per_row = p_out.shape[1] // HALF
    gap = jnp.zeros((HALF, tok), BF16)
    gap2 = jnp.zeros((BLK, tok), BF16)

    def step(r, carry):
        at = pl.ds(pl.multiple_of(r * BLK, BLK), BLK)
        normed, cot = nt_s[at, :], gt_s[at, :]
        spread = []
        for a in (0, 1):
            part = normed[a * HALF : (a + 1) * HALF]
            spread.append(jnp.concatenate([part, gap], axis=1))
            spread.append(jnp.concatenate([gap, part], axis=1))
        terms_v = dot(a_in[r], jnp.concatenate(spread, axis=0))
        cots = jnp.concatenate(
            [jnp.concatenate([cot, gap2], axis=1), jnp.concatenate([gap2, cot], axis=1)], axis=0
        )
        terms_a = dot(p_out[r], cots)
        for quad in range(per_row // GROUP):
            new = []
            for u in range(GROUP):
                k = quad * GROUP + u
                code = plan[0, r * per_row + k]
                c, first = code & (FIRST - 1), code >= FIRST
                rows = terms_v[(k // 2) * BLK : (k // 2 + 1) * BLK]
                v = rows[:, (k % 2) * tok : (k % 2 + 1) * tok]
                rows = terms_a[k * HALF : (k + 1) * HALF]
                a = jnp.concatenate([rows[:, :tok], rows[:, tok:]], axis=0)
                v = jnp.where(first, v, acc_v[c] + v)
                a = jnp.where(first, a, acc_a[c] + a)
                new.append((c, v, a))
            for c, v, a in new:
                acc_v[c] = v
                acc_a[c] = a
        return carry

    lax.fori_loop(0, row_blocks, step, 0, unroll=16)


def local_kernel(
    plan, gain_ref, s0, s1, s2, s3, a_in, p_out, act_ref, gp_ref, n_ref, nt_s, gt_s, acc_v, acc_a
):
    tok = n_ref.shape[0]
    perm = even_first(s0.shape[1])
    load_tokens([(ref, 0) for ref in (s0, s1, s2, s3)], tok, gain_ref, perm, n_ref, nt_s, gt_s, 0)
    expand(plan, a_in, p_out, nt_s, gt_s, acc_v, acc_a)

    def bend(c, carry):
        value, slope = gelu_both(acc_v[c])
        act_ref[c] = value.astype(BF16)
        gp_ref[c] = (acc_a[c] * slope).astype(BF16)
        return carry

    lax.fori_loop(0, gp_ref.shape[0], bend, 0, unroll=4)


def contract_kernel(plan, act_ref, gp_ref, b_in, a_out, o0, o1, o2, o3, br_s, gn_s):
    tok, width = o0.shape[0] // 2, o0.shape[1]
    row_blocks, per_row = b_in.shape[0], b_in.shape[2] // BLK
    perm = even_first(width)

    def contract(r, carry):
        at = pl.ds(pl.multiple_of(r * BLK, BLK), BLK)
        ids = [plan[0, r * per_row + k] & (FIRST - 1) for k in range(per_row)]
        acts = [act_ref[c, a * HALF : (a + 1) * HALF, :] for a in (0, 1) for c in ids]
        br_s[at, :] = dot(a_out[r], jnp.concatenate(acts, axis=0)).astype(BF16)
        grads = [gp_ref[c] for c in ids]
        gn_s[at, :] = dot(b_in[r], jnp.concatenate(grads, axis=0)).astype(BF16)
        return carry

    lax.fori_loop(0, row_blocks, contract, 0, unroll=8)
    mine = lax.axis_index("mp")
    for q, out in enumerate((o0, o1, o2, o3)):
        at = pl.ds(pl.multiple_of((mine ^ q) * width, width), width)
        out[:tok, :] = br_s[at, :].T
        out[tok:, :] = dot(gn_s[at, :].T, perm, ((1,), (1,))).astype(BF16)


def chunk_kernel(
    plan, gain_ref, s0, s1, s2, s3, a_in, p_out, gp_ref, n_ref, nt_s, gt_s, acc_v, acc_a
):
    chunks = gp_ref.shape[0]
    tok = n_ref.shape[0] // chunks
    perm = even_first(s0.shape[1])
    count = plan[5, 0]
    for j in range(chunks):
        pieces = [(ref, 2 * tok * j) for ref in (s0, s1, s2, s3)]
        load_tokens(pieces, tok, gain_ref, perm, n_ref, nt_s, gt_s, j * tok)
        expand(plan, a_in, p_out, nt_s, gt_s, acc_v, acc_a)

        def bend(i, carry):
            for u in range(BEND):
                c = plan[4, jnp.minimum(i * BEND + u, count - 1)]
                _, slope = gelu_both(acc_v[c])
                gp_ref[j, c] = (acc_a[c] * slope).astype(BF16)
            return carry

        lax.fori_loop(0, (count + BEND - 1) // BEND, bend, 0)


def block_kernel(
    list_row, scale, plan, gp0, gp1, gp2, n0, n1, n2, p_out, found
):
    per_row = p_out.shape[1] // HALF
    lanes = 2 * BLK
    pairs = p_out.shape[0] // 2
    cap = found.shape[0] - 1
    left = iota((HALF, lanes), 1) < BLK
    found[...] = jnp.zeros_like(found)

    def form(pair, first):
        end = plan[list_row + 1, pair + 1]
        at_lane = pl.ds(pl.multiple_of(pair * lanes, lanes), lanes)
        ids = [
            plan[list_row, jnp.maximum(jnp.minimum(first + u, end - 1), 0)] for u in range(BATCH)
        ]
        grads = []
        for k in ids:
            c = plan[0, k] & (FIRST - 1)
            chunks = [gp0[c]] + [ref[j, c] for ref in (gp1, gp2) for j in range(ref.shape[0])]
            grads.append(jnp.concatenate(chunks, axis=1))
        normed = jnp.concatenate([ref[:, at_lane] for ref in (n0, n1, n2)], axis=0)
        blocks = dot(jnp.concatenate(grads, axis=0), normed) * scale
        done = []
        for u, k in enumerate(ids):
            odd = (lax.div(k, jnp.int32(per_row)) & 1) == 1
            top = blocks[u * BLK : u * BLK + HALF]
            low = blocks[u * BLK + HALF : (u + 1) * BLK]
            top = jnp.where(odd, pltpu.roll(top, BLK, 1), top)
            low = jnp.where(odd, low, pltpu.roll(low, BLK, 1))
            slot = jnp.where(first < end, plan[1, k], cap)
            done.append((slot, jnp.where(left, top, low).astype(found.dtype)))
        for slot, value in done:
            found[slot] = value

    def begin(pair, carry):
        form(pair, plan[list_row + 1, pair])
        return carry

    lax.fori_loop(0, pairs, begin, 0, unroll=8)

    def finish(pair, carry):
        begin, end = plan[list_row + 1, pair], plan[list_row + 1, pair + 1]

        def more(i, carry):
            form(pair, begin + i * BATCH)
            return carry

        return lax.fori_loop(1, (end - begin + BATCH - 1) // BATCH, more, carry)

    lax.fori_loop(0, pairs, finish, 0)


def finish_kernel(own_ref, arrived_ref, s0, s1, s2, s3, branch_ref, normed_ref, out_ref):
    lanes = own_ref.shape[2]
    rows = 8
    for first in range(0, own_ref.shape[0], rows):
        at = slice(first, first + rows)
        blocks = own_ref[at] + arrived_ref[at].astype(F32)
        turned = jnp.swapaxes(blocks, 0, 1)
        for j in range(turned.shape[0]):
            out_ref[at, j * lanes : (j + 1) * lanes] = turned[j]

    @pl.when(pl.program_id(0) == 0)
    def _():
        tok = branch_ref.shape[0]
        for out, base in ((branch_ref, 0), (normed_ref, tok)):
            total = sum(ref[base : base + tok, :].astype(F32) for ref in (s0, s1, s2, s3))
            out[...] = total.astype(BF16)


def fast_body(x_in, gain, w_in, w_out, grad_out, block_cols, slots):
    dp_count, mp_count = lax.axis_size("dp"), lax.axis_size("mp")
    tok, width = x_in.shape
    feat = width * mp_count
    kept = w_in.shape[0]
    row_blocks = feat // BLK
    per_row = kept // row_blocks
    hidden = FF // mp_count
    col_blocks = hidden // BLK
    lanes = 2 * BLK
    cap = 2 * kept // dp_count
    scale = 1.0 / math.sqrt(tok * dp_count)
    across_x = [(i, i ^ 1) for i in range(dp_count)]
    near = [[(i, i ^ q) for i in range(mp_count)] for q in range(mp_count)]
    z_count = dp_count // 2
    along_z = [[(i, i ^ (2 * j)) for i in range(dp_count)] for j in (1, 3, 2)]

    whole = pl.BlockSpec(memory_space=pltpu.VMEM)
    mm = 2 * tok * kept * BLK * BLK

    own = pl.pallas_call(
        stack_kernel,
        out_shape=jax.ShapeDtypeStruct((2 * tok, width), BF16),
        cost_estimate=pl.CostEstimate(flops=0, bytes_accessed=8 * tok * width, transcendentals=0),
        name="stack",
    )(x_in, grad_out)
    pieces = [lax.ppermute(own, "dp", along_z[0])]
    over_core, own_late = lax.optimization_barrier((lax.ppermute(own, "mp", near[1]), own))
    over_y = lax.ppermute(own_late, "mp", near[2])
    gathered = [own, over_core, over_y, lax.ppermute(over_y, "mp", near[1])]
    pieces += [lax.ppermute(own_late, "dp", hop) for hop in along_z[1:]]
    pieces[0], cols_late, slots_late = lax.optimization_barrier((pieces[0], block_cols, slots))
    plan = pl.pallas_call(
        functools.partial(plan_kernel, cap, col_blocks, row_blocks),
        out_shape=jax.ShapeDtypeStruct((8, kept), jnp.int32),
        cost_estimate=pl.CostEstimate(flops=4_000_000, bytes_accessed=16384, transcendentals=0),
        name="plan",
    )(cols_late, slots_late)
    near_piece = [pieces[0]] + [lax.ppermute(pieces[0], "mp", near[q]) for q in (1, 2)]
    gain_row = gain.reshape(1, feat)

    step = min(4, row_blocks)
    shapes = [
        (per_row // 2 * BLK, lanes),
        (BLK, per_row * BLK),
        (per_row * HALF, lanes),
        (BLK, per_row * BLK),
    ]
    a_in, b_in, p_out, a_out = pl.pallas_call(
        prepare_kernel,
        out_shape=[jax.ShapeDtypeStruct((row_blocks, *shape), BF16) for shape in shapes],
        grid=(row_blocks // step,),
        in_specs=[pl.BlockSpec(memory_space=pltpu.SMEM)]
        + [pl.BlockSpec((step * per_row, BLK * BLK), lambda r: (r, 0))] * 2,
        out_specs=[pl.BlockSpec((step, *shape), lambda r: (r, 0, 0)) for shape in shapes],
        scratch_shapes=[
            pltpu.VMEM((per_row * HALF, per_row * HALF), BF16),
            pltpu.VMEM((lanes, 2 * lanes), BF16),
        ],
        compiler_params=pltpu.CompilerParams(vmem_limit_bytes=24 * MIB),
        cost_estimate=pl.CostEstimate(
            flops=8 * mm, bytes_accessed=12 * kept * BLK * BLK, transcendentals=0
        ),
        name="prepare",
    )(
        plan,
        pltpu.with_memory_space_constraint(w_in, pltpu.HBM),
        pltpu.with_memory_space_constraint(w_out, pltpu.HBM),
    )

    late, near_piece, gathered, p_out = lax.optimization_barrier(
        (pieces[1:], near_piece, gathered, p_out)
    )
    column = jnp.concatenate(late, axis=0)
    far_pieces = [column] + [lax.ppermute(column, "mp", near[q]) for q in (1, 2)]
    near_piece.append(lax.ppermute(near_piece[2], "mp", near[1]))

    hidden_f32 = pltpu.VMEM((col_blocks, BLK, tok), F32)
    turned = pltpu.VMEM((feat, tok), BF16)

    def hidden_bf16(*chunks):
        return jax.ShapeDtypeStruct((*chunks, col_blocks, BLK, tok), BF16)

    def flat(chunks):
        return jax.ShapeDtypeStruct((chunks * tok, feat), BF16)

    def call(kernel, out_shape, scratch, limit, flops, transcendentals, *args):
        return pl.pallas_call(
            kernel,
            out_shape=out_shape,
            grid_spec=pltpu.PrefetchScalarGridSpec(
                num_scalar_prefetch=1,
                grid=(),
                in_specs=[whole] * (len(args) - 1),
                out_specs=[whole] * len(out_shape),
                scratch_shapes=scratch,
            ),
            compiler_params=pltpu.CompilerParams(vmem_limit_bytes=limit * MIB),
            cost_estimate=pl.CostEstimate(
                flops=flops, bytes_accessed=flops // (4 * tok), transcendentals=transcendentals
            ),
            name=(kernel.func if isinstance(kernel, functools.partial) else kernel).__name__,
        )(*args)

    scratch = [turned, turned, hidden_f32, hidden_f32]
    act, gp_own, n_own = call(
        local_kernel, [hidden_bf16(), hidden_bf16(), flat(1)], scratch, 32, 8 * mm, tok * hidden,
        plan, gain_row, *gathered, a_in, p_out,
    )
    far_pieces[2], n_own = lax.optimization_barrier((far_pieces[2], n_own))
    far_pieces.append(lax.ppermute(far_pieces[2], "mp", near[1]))
    gp_near, n_near = call(
        chunk_kernel, [hidden_bf16(1), flat(1)], scratch, 32, 8 * mm, tok * hidden // 2,
        plan, gain_row, *near_piece, a_in, p_out,
    )
    gp_far, n_far = call(
        chunk_kernel, [hidden_bf16(z_count - 2), flat(z_count - 2)], scratch, 32, 16 * mm, tok * hidden,
        plan, gain_row, *far_pieces, a_in, p_out,
    )

    def blocks(list_row, dtype, flops, plan):
        return call(
            functools.partial(block_kernel, list_row, scale),
            [jax.ShapeDtypeStruct((cap + 1, HALF, lanes), dtype)],
            [],
            16, flops, 0,
            plan, gp_own, gp_near, gp_far, n_own, n_near, n_far, p_out,
        )[0]

    for_peer = blocks(2, BF16, 2 * mm, plan)
    for_peer, plan_later, act = lax.optimization_barrier((for_peer, plan, act))
    arrived = lax.ppermute(for_peer, "dp", across_x)
    parts = call(
        contract_kernel,
        [jax.ShapeDtypeStruct((2 * tok, width), BF16)] * mp_count,
        [turned, turned],
        16, 0, 0,
        plan_later, act, gp_own, b_in, a_out,
    )
    for_own = blocks(6, F32, 0, plan_later)
    summed = [parts[0]] + [lax.ppermute(parts[q], "mp", near[q]) for q in range(1, mp_count)]
    steps = 2
    own_rows = pl.BlockSpec((cap // steps, HALF, lanes), lambda i: (i, 0, 0))
    token_rows = pl.BlockSpec((2 * tok, width), lambda i: (0, 0))
    result = pl.BlockSpec((tok, width), lambda i: (0, 0))
    branch, grad_normed, owned_grad = pl.pallas_call(
        finish_kernel,
        out_shape=[
            jax.ShapeDtypeStruct((tok, width), BF16),
            jax.ShapeDtypeStruct((tok, width), BF16),
            jax.ShapeDtypeStruct((cap, BLK * BLK), F32),
        ],
        grid=(steps,),
        in_specs=[own_rows] * 2 + [token_rows] * mp_count,
        out_specs=[result, result, pl.BlockSpec((cap // steps, BLK * BLK), lambda i: (i, 0))],
        compiler_params=pltpu.CompilerParams(vmem_limit_bytes=16 * MIB),
        cost_estimate=pl.CostEstimate(flops=0, bytes_accessed=0, transcendentals=0),
        name="finish",
    )(for_own, arrived, *summed)
    return (branch, grad_normed, owned_grad[None])


def sum_sources(received):
    return jnp.sum(received, axis=0)


def body(x_in, gain, w_in, w_out, grad_out, block_cols, slots):
    whole_x, whole_grad = (
        lax.all_gather(x_in, "mp", axis=1, tiled=True),
        lax.all_gather(grad_out, "mp", axis=1, tiled=True),
    )
    tok_rows = whole_x.shape[0]
    feat_width = whole_x.shape[1]
    row_blocks = feat_width // BLK
    kept_count = w_in.shape[0]
    per_row = kept_count // row_blocks
    col_blocks = FF // lax.axis_size("mp") // BLK
    col_ids = block_cols[0]
    slot_ids = slots[0]
    x_float = whole_x.astype(jnp.float32)
    inv_rms = lax.rsqrt(jnp.mean(x_float * x_float, axis=-1, keepdims=True) + norm_eps)
    normed = (x_float * inv_rms * gain).astype(jnp.bfloat16)
    normed_cols = normed.reshape(tok_rows, row_blocks, BLK).transpose(1, 2, 0)
    grad_cols = whole_grad.reshape(tok_rows, row_blocks, BLK).transpose(1, 2, 0)
    in_blocks = w_in.reshape(row_blocks, per_row, BLK, BLK)
    out_blocks = w_out.reshape(row_blocks, per_row, BLK, BLK)
    col_onehot = (col_ids[None, :] == jnp.arange(col_blocks, dtype=jnp.int32)[:, None]).astype(
        jnp.float32
    )
    pre_parts = jnp.einsum(
        "rkbc,rbt->rkct", in_blocks, normed_cols, preferred_element_type=jnp.float32
    )
    pre_act = jnp.dot(
        col_onehot,
        pre_parts.reshape(kept_count, BLK * tok_rows),
        precision=lax.Precision.HIGHEST,
        preferred_element_type=jnp.float32,
    )
    pre_act = pre_act.reshape(col_blocks, BLK, tok_rows)
    activation = gelu_value(pre_act).astype(jnp.bfloat16)
    act_blocks = jnp.take(activation, col_ids, axis=0).reshape(row_blocks, per_row, BLK, tok_rows)
    branch_cols = jnp.einsum(
        "rkcb,rkct->rbt", out_blocks, act_blocks, preferred_element_type=jnp.float32
    )
    branch_part = branch_cols.transpose(2, 0, 1).reshape(tok_rows, feat_width)
    branch = lax.psum_scatter(branch_part, "mp", scatter_dimension=1, tiled=True).astype(
        jnp.bfloat16
    )
    act_parts = jnp.einsum(
        "rkcb,rbt->rkct", out_blocks, grad_cols, preferred_element_type=jnp.float32
    )
    grad_act = jnp.dot(
        col_onehot,
        act_parts.reshape(kept_count, BLK * tok_rows),
        precision=lax.Precision.HIGHEST,
        preferred_element_type=jnp.float32,
    )
    grad_act = grad_act.reshape(col_blocks, BLK, tok_rows)
    grad_pre = (grad_act * gelu_slope(pre_act)).astype(jnp.bfloat16)
    pre_blocks = jnp.take(grad_pre, col_ids, axis=0).reshape(row_blocks, per_row, BLK, tok_rows)
    dp_count = lax.axis_size("dp")
    weight_scale = 1.0 / math.sqrt(tok_rows * dp_count)
    block_terms = jnp.einsum(
        "rkct,rbt->rkcb", pre_blocks, normed_cols, preferred_element_type=jnp.float32
    )
    block_partial = (block_terms * weight_scale).reshape(kept_count, BLK * BLK)
    capacity = 2 * kept_count // dp_count
    outgoing = (
        jnp.zeros((dp_count * capacity, BLK * BLK), jnp.float32).at[slot_ids].set(block_partial)
    )
    outgoing = outgoing.reshape(dp_count, capacity, BLK * BLK)
    owned_grad = sum_sources(
        lax.all_to_all(
            outgoing.astype(jnp.bfloat16), "dp", split_axis=0, concat_axis=0, tiled=True
        ).astype(outgoing.dtype)
    )
    normed_part = jnp.einsum(
        "rkbc,rkct->rbt", in_blocks, pre_blocks, preferred_element_type=jnp.float32
    )
    normed_part = normed_part.transpose(2, 0, 1).reshape(tok_rows, feat_width)
    grad_normed = lax.psum_scatter(normed_part, "mp", scatter_dimension=1, tiled=True).astype(
        jnp.bfloat16
    )
    return (branch, grad_normed, owned_grad[None])


def solution(mesh):
    placed = (
        P("dp", "mp"),
        P(),
        P("mp", None),
        P("mp", None),
        P("dp", "mp"),
        P("mp", None),
        P("mp", None),
    )
    fits = mesh.shape["dp"] == 8 and mesh.shape["mp"] == 4
    return jax.shard_map(
        fast_body if fits else body,
        mesh=mesh,
        in_specs=placed,
        out_specs=(P("dp", "mp"), P("dp", "mp"), P("mp", "dp", None)),
        check_vma=False,
    )
```

```python
import functools
import math

import jax
import jax.numpy as jnp
from jax import lax
from jax.experimental import pallas as pl
from jax.experimental.pallas import tpu as pltpu
from jax.sharding import PartitionSpec as P

FF = 32768
BLK = 64
HALF = BLK // 2
GROUP = 4
FIRST = 1024
BATCH = 10
BEND = 8


norm_eps = 1e-06
tanh_coef = 0.7978845608028654

F32 = jnp.float32
BF16 = jnp.bfloat16
MIB = 1024 * 1024


def gelu_value(pre_act):
    cubic = pre_act * pre_act * pre_act
    slope_arg = jnp.tanh(tanh_coef * (pre_act + 0.044715 * cubic))
    return 0.5 * pre_act * (1.0 + slope_arg)


def gelu_slope(pre_act):
    cubic = pre_act * pre_act * pre_act
    slope_arg = jnp.tanh(tanh_coef * (pre_act + 0.044715 * cubic))
    inner = tanh_coef * (1.0 + 0.134145 * pre_act * pre_act)
    return 0.5 * (1.0 + slope_arg) + 0.5 * pre_act * (1.0 - slope_arg * slope_arg) * inner


def gelu_both(v):
    square = v * v
    th = jnp.tanh(v * (tanh_coef + (tanh_coef * 0.044715) * square))
    gate = 0.5 + 0.5 * th
    inner = 2.0 * tanh_coef + (2.0 * tanh_coef * 0.134145) * square
    return v * gate, gate + v * (gate - gate * gate) * inner


def dot(a, b, dims=((1,), (0,))):
    return lax.dot_general(a, b, (dims, ((), ())), preferred_element_type=F32)


def iota(shape, axis):
    return lax.broadcasted_iota(jnp.int32, shape, axis)


def even_first(width):
    row, col = iota((width, width), 0), iota((width, width), 1)
    inside = row & (BLK - 1)
    target = (row - inside) + (inside & 1) * HALF + (inside >> 1)
    return jnp.where(col == target, 1.0, 0.0).astype(BF16)


def stack_kernel(x_ref, grad_ref, both_ref):
    tok = x_ref.shape[0]
    both_ref[:tok, :] = x_ref[...]
    both_ref[tok:, :] = grad_ref[...]


def plan_kernel(cap, col_blocks, row_blocks, cols_ref, slots_ref, out_ref):
    kept = cols_ref.shape[1]
    per_row = kept // row_blocks
    me = lax.axis_index("dp")
    cols, slots = cols_ref[...], slots_ref[...]
    owner = lax.div(slots, jnp.int32(cap))
    own = jnp.where(owner == me, 1.0, 0.0)
    peer = jnp.where(owner == (me ^ 1), 1.0, 0.0)
    needed = jnp.max(
        jnp.where(cols == iota((col_blocks, kept), 0), own + peer, 0.0), axis=1, keepdims=True
    )

    def to_column(row):
        size = row.shape[1]
        eye = iota((size, size), 0) == iota((size, size), 1)
        return jnp.sum(jnp.where(eye, row, 0.0), axis=1, keepdims=True)

    def to_row(column):
        size = column.shape[0]
        eye = iota((size, size), 0) == iota((size, size), 1)
        return jnp.sum(jnp.where(eye, column, 0.0), axis=0, keepdims=True)

    def listed(flags_r, flags_c):
        size = flags_r.shape[1]
        before = iota((size, size), 1) < iota((size, size), 0)
        place = jnp.sum(jnp.where(before, flags_r, 0.0), axis=1, keepdims=True)
        hit = (place == iota((size, kept), 1).astype(F32)) & (flags_c > 0)
        index = iota((size, 1), 0).astype(F32)
        return jnp.sum(jnp.where(hit, index, 0.0), axis=0, keepdims=True)

    cols_r = cols.astype(F32)
    cols_c = to_column(cols_r)
    earlier = iota((kept, kept), 1) < iota((kept, kept), 0)
    seen = jnp.max(jnp.where(earlier & (cols_r == cols_c), 1.0, 0.0), axis=1, keepdims=True)
    peer_c, own_c = to_column(peer), to_column(own)
    pair_end = iota((kept, kept), 0) < 2 * per_row * iota((kept, kept), 1)

    def starts(flags_c):
        return jnp.sum(jnp.where(pair_end, flags_c, 0.0), axis=0, keepdims=True)

    rows = [
        cols_r + FIRST * (1.0 - to_row(seen)),
        (slots - owner * cap).astype(F32),
        listed(peer, peer_c),
        starts(peer_c),
        listed(to_row(needed), needed),
        jnp.sum(needed, axis=0, keepdims=True),
        listed(own, own_c),
        starts(own_c),
    ]
    for index, row in enumerate(rows):
        out_ref[index : index + 1, :] = jnp.broadcast_to(row, (1, kept)).astype(jnp.int32)


def prepare_kernel(plan_ref, win_ref, wout_ref, a_in, b_in, p_out, a_out, order, both):
    count = a_in.shape[0]
    per_row, length = win_ref.shape[0] // count, win_ref.shape[1]
    lanes = 2 * BLK
    rows = per_row * HALF

    @pl.when(pl.program_id(0) == 0)
    def _():
        row, col = iota((rows, rows), 0), iota((rows, rows), 1)
        source = (row & (HALF - 1)) * per_row + lax.div(row, jnp.int32(HALF))
        order[...] = jnp.where(col == source, 1.0, 0.0).astype(BF16)
        row, col = iota((lanes, lanes), 0), iota((lanes, lanes), 1)
        swap = jnp.where(((col + BLK) & (lanes - 1)) == row, 1.0, 0.0).astype(BF16)
        perm = even_first(lanes)
        both[:, :lanes] = perm
        both[:, lanes:] = dot(perm, swap).astype(BF16)

    def by_block(ref):
        stacked = [
            jnp.concatenate(
                [
                    ref[n * per_row : (n + 1) * per_row, j * lanes : (j + 1) * lanes]
                    for j in range(length // lanes)
                ],
                axis=0,
            )
            for n in range(count)
        ]
        return dot(order[...], jnp.concatenate(stacked, axis=1)).astype(BF16)

    ordered_in, ordered_out = by_block(win_ref), by_block(wout_ref)
    left = iota((HALF, lanes), 1) < BLK
    left2 = iota((BLK, lanes), 1) < BLK
    for n in range(count):
        of_n = slice(n * lanes, (n + 1) * lanes)
        kept_in = dot(ordered_in[:, of_n], both[...])
        kept_out = ordered_out[:, of_n]
        p_out[n] = kept_out
        for pair in range(per_row // 2):
            first = kept_in[2 * pair * HALF : (2 * pair + 1) * HALF]
            second = kept_in[(2 * pair + 1) * HALF : (2 * pair + 2) * HALF]
            at = slice(pair * lanes, (pair + 1) * lanes)
            b_in[n, :HALF, at] = jnp.where(left, first[:, :lanes], second[:, lanes:]).astype(BF16)
            b_in[n, HALF:, at] = jnp.where(left, first[:, lanes:], second[:, :lanes]).astype(BF16)
        for quad in range(per_row // GROUP):
            rows_of = slice(quad * lanes, (quad + 1) * lanes)
            straight, swapped = kept_in[rows_of, :lanes], kept_in[rows_of, lanes:]
            pairs = jnp.concatenate(
                [
                    jnp.where(left2, straight[:BLK], swapped[BLK:]),
                    jnp.where(left2, swapped[:BLK], straight[BLK:]),
                ],
                axis=0,
            )
            a_in[n, rows_of, :] = pairs.astype(BF16).T
            turned = kept_out[rows_of].T
            a_out[n, :, rows_of] = turned[:BLK]
            a_out[n, :, rows + quad * lanes : rows + (quad + 1) * lanes] = turned[BLK:]


def load_tokens(pieces, tok, gain_ref, perm, n_s, nt_s, gt_s, base):
    mine = lax.axis_index("mp")
    width = pieces[0][0].shape[1]
    values, total = [], 0.0
    for ref, first in pieces:
        value = ref[first : first + tok, :].astype(F32)
        values.append(value)
        total = total + jnp.sum(value * value, axis=-1, keepdims=True)
    inv_rms = lax.rsqrt(total / (width * len(pieces)) + norm_eps)
    for q, (ref, first) in enumerate(pieces):
        at = pl.ds(pl.multiple_of((mine ^ q) * width, width), width)
        normed = (values[q] * inv_rms * gain_ref[:, at]).astype(BF16)
        n_s[base : base + tok, at] = normed
        nt_s[at, :] = dot(normed, perm).astype(BF16).T
        gt_s[at, :] = ref[first + tok : first + 2 * tok, :].T


def expand(plan, a_in, p_out, nt_s, gt_s, acc_v, acc_a):
    row_blocks = a_in.shape[0]
    tok = nt_s.shape[1]
    per_row = p_out.shape[1] // HALF
    gap = jnp.zeros((HALF, tok), BF16)
    gap2 = jnp.zeros((BLK, tok), BF16)

    def step(r, carry):
        at = pl.ds(pl.multiple_of(r * BLK, BLK), BLK)
        normed, cot = nt_s[at, :], gt_s[at, :]
        spread = []
        for a in (0, 1):
            part = normed[a * HALF : (a + 1) * HALF]
            spread.append(jnp.concatenate([part, gap], axis=1))
            spread.append(jnp.concatenate([gap, part], axis=1))
        terms_v = dot(a_in[r], jnp.concatenate(spread, axis=0))
        cots = jnp.concatenate(
            [jnp.concatenate([cot, gap2], axis=1), jnp.concatenate([gap2, cot], axis=1)], axis=0
        )
        terms_a = dot(p_out[r], cots)
        for quad in range(per_row // GROUP):
            new = []
            for u in range(GROUP):
                k = quad * GROUP + u
                code = plan[0, r * per_row + k]
                c, first = code & (FIRST - 1), code >= FIRST
                rows = terms_v[(k // 2) * BLK : (k // 2 + 1) * BLK]
                v = rows[:, (k % 2) * tok : (k % 2 + 1) * tok]
                rows = terms_a[k * HALF : (k + 1) * HALF]
                a = jnp.concatenate([rows[:, :tok], rows[:, tok:]], axis=0)
                v = jnp.where(first, v, acc_v[c] + v)
                a = jnp.where(first, a, acc_a[c] + a)
                new.append((c, v, a))
            for c, v, a in new:
                acc_v[c] = v
                acc_a[c] = a
        return carry

    lax.fori_loop(0, row_blocks, step, 0, unroll=16)


def local_kernel(
    plan, gain_ref, s0, s1, s2, s3, a_in, p_out, act_ref, gp_ref, n_ref, nt_s, gt_s, acc_v, acc_a
):
    tok = n_ref.shape[0]
    perm = even_first(s0.shape[1])
    load_tokens([(ref, 0) for ref in (s0, s1, s2, s3)], tok, gain_ref, perm, n_ref, nt_s, gt_s, 0)
    expand(plan, a_in, p_out, nt_s, gt_s, acc_v, acc_a)

    def bend(c, carry):
        value, slope = gelu_both(acc_v[c])
        act_ref[c] = value.astype(BF16)
        gp_ref[c] = (acc_a[c] * slope).astype(BF16)
        return carry

    lax.fori_loop(0, gp_ref.shape[0], bend, 0, unroll=8)


def contract_kernel(plan, act_ref, gp_ref, b_in, a_out, o0, o1, o2, o3, br_s, gn_s):
    tok, width = o0.shape[0] // 2, o0.shape[1]
    row_blocks, per_row = b_in.shape[0], b_in.shape[2] // BLK
    perm = even_first(width)

    def contract(r, carry):
        at = pl.ds(pl.multiple_of(r * BLK, BLK), BLK)
        ids = [plan[0, r * per_row + k] & (FIRST - 1) for k in range(per_row)]
        acts = [act_ref[c, a * HALF : (a + 1) * HALF, :] for a in (0, 1) for c in ids]
        br_s[at, :] = dot(a_out[r], jnp.concatenate(acts, axis=0)).astype(BF16)
        grads = [gp_ref[c] for c in ids]
        gn_s[at, :] = dot(b_in[r], jnp.concatenate(grads, axis=0)).astype(BF16)
        return carry

    lax.fori_loop(0, row_blocks, contract, 0, unroll=16)
    mine = lax.axis_index("mp")
    for q, out in enumerate((o0, o1, o2, o3)):
        at = pl.ds(pl.multiple_of((mine ^ q) * width, width), width)
        out[:tok, :] = br_s[at, :].T
        out[tok:, :] = dot(gn_s[at, :].T, perm, ((1,), (1,))).astype(BF16)


def chunk_kernel(
    plan, gain_ref, s0, s1, s2, s3, a_in, p_out, gp_ref, n_ref, nt_s, gt_s, acc_v, acc_a
):
    chunks = gp_ref.shape[0]
    tok = n_ref.shape[0] // chunks
    perm = even_first(s0.shape[1])
    count = plan[5, 0]
    for j in range(chunks):
        pieces = [(ref, 2 * tok * j) for ref in (s0, s1, s2, s3)]
        load_tokens(pieces, tok, gain_ref, perm, n_ref, nt_s.at[j], gt_s.at[j], j * tok)
    for j in range(chunks):
        expand(plan, a_in, p_out, nt_s.at[j], gt_s.at[j], acc_v, acc_a)

        def bend(i, carry):
            for u in range(BEND):
                c = plan[4, jnp.minimum(i * BEND + u, count - 1)]
                _, slope = gelu_both(acc_v[c])
                gp_ref[j, c] = (acc_a[c] * slope).astype(BF16)
            return carry

        lax.fori_loop(0, (count + BEND - 1) // BEND, bend, 0)


def block_kernel(
    list_row, scale, plan, gp0, gp1, gp2, n0, n1, n2, p_out, found
):
    per_row = p_out.shape[1] // HALF
    lanes = 2 * BLK
    pairs = p_out.shape[0] // 2
    cap = found.shape[0] - 1
    left = iota((HALF, lanes), 1) < BLK
    found[...] = jnp.zeros_like(found)

    def form(pair, first):
        end = plan[list_row + 1, pair + 1]
        at_lane = pl.ds(pl.multiple_of(pair * lanes, lanes), lanes)
        ids = [
            plan[list_row, jnp.maximum(jnp.minimum(first + u, end - 1), 0)] for u in range(BATCH)
        ]
        grads = []
        for k in ids:
            c = plan[0, k] & (FIRST - 1)
            chunks = [gp0[c]] + [ref[j, c] for ref in (gp1, gp2) for j in range(ref.shape[0])]
            grads.append(jnp.concatenate(chunks, axis=1))
        normed = jnp.concatenate([ref[:, at_lane] for ref in (n0, n1, n2)], axis=0)
        blocks = dot(jnp.concatenate(grads, axis=0), normed) * scale
        done = []
        for u, k in enumerate(ids):
            odd = (lax.div(k, jnp.int32(per_row)) & 1) == 1
            top = blocks[u * BLK : u * BLK + HALF]
            low = blocks[u * BLK + HALF : (u + 1) * BLK]
            top = jnp.where(odd, pltpu.roll(top, BLK, 1), top)
            low = jnp.where(odd, low, pltpu.roll(low, BLK, 1))
            slot = jnp.where(first < end, plan[1, k], cap)
            done.append((slot, jnp.where(left, top, low).astype(found.dtype)))
        for slot, value in done:
            found[slot] = value

    def begin(pair, carry):
        form(pair, plan[list_row + 1, pair])
        return carry

    lax.fori_loop(0, pairs, begin, 0, unroll=8)

    def finish(pair, carry):
        begin, end = plan[list_row + 1, pair], plan[list_row + 1, pair + 1]

        def more(i, carry):
            form(pair, begin + i * BATCH)
            return carry

        return lax.fori_loop(1, (end - begin + BATCH - 1) // BATCH, more, carry)

    lax.fori_loop(0, pairs, finish, 0)


def finish_kernel(own_ref, arrived_ref, s0, s1, s2, s3, branch_ref, normed_ref, out_ref):
    lanes = own_ref.shape[2]
    rows = 8
    for first in range(0, own_ref.shape[0], rows):
        at = slice(first, first + rows)
        blocks = own_ref[at] + arrived_ref[at].astype(F32)
        turned = jnp.swapaxes(blocks, 0, 1)
        for j in range(turned.shape[0]):
            out_ref[at, j * lanes : (j + 1) * lanes] = turned[j]

    @pl.when(pl.program_id(0) == 0)
    def _():
        tok = branch_ref.shape[0]
        for out, base in ((branch_ref, 0), (normed_ref, tok)):
            total = sum(ref[base : base + tok, :].astype(F32) for ref in (s0, s1, s2, s3))
            out[...] = total.astype(BF16)


def fast_body(x_in, gain, w_in, w_out, grad_out, block_cols, slots):
    dp_count, mp_count = lax.axis_size("dp"), lax.axis_size("mp")
    tok, width = x_in.shape
    feat = width * mp_count
    kept = w_in.shape[0]
    row_blocks = feat // BLK
    per_row = kept // row_blocks
    hidden = FF // mp_count
    col_blocks = hidden // BLK
    lanes = 2 * BLK
    cap = 2 * kept // dp_count
    scale = 1.0 / math.sqrt(tok * dp_count)
    across_x = [(i, i ^ 1) for i in range(dp_count)]
    near = [[(i, i ^ q) for i in range(mp_count)] for q in range(mp_count)]
    z_count = dp_count // 2
    along_z = [[(i, i ^ (2 * j)) for i in range(dp_count)] for j in (1, 3, 2)]

    whole = pl.BlockSpec(memory_space=pltpu.VMEM)
    mm = 2 * tok * kept * BLK * BLK

    own = pl.pallas_call(
        stack_kernel,
        out_shape=jax.ShapeDtypeStruct((2 * tok, width), BF16),
        cost_estimate=pl.CostEstimate(flops=0, bytes_accessed=8 * tok * width, transcendentals=0),
        name="stack",
    )(x_in, grad_out)
    pieces = [lax.ppermute(own, "dp", along_z[0])]
    over_core, own_late = lax.optimization_barrier((lax.ppermute(own, "mp", near[1]), own))
    over_y = lax.ppermute(own_late, "mp", near[2])
    gathered = [own, over_core, over_y, lax.ppermute(own_late, "mp", near[3])]
    pieces += [lax.ppermute(own_late, "dp", hop) for hop in along_z[1:]]
    pieces[0], cols_late, slots_late = lax.optimization_barrier((pieces[0], block_cols, slots))
    plan = pl.pallas_call(
        functools.partial(plan_kernel, cap, col_blocks, row_blocks),
        out_shape=jax.ShapeDtypeStruct((8, kept), jnp.int32),
        cost_estimate=pl.CostEstimate(flops=4_000_000, bytes_accessed=16384, transcendentals=0),
        name="plan",
    )(cols_late, slots_late)
    near_piece = [pieces[0], lax.ppermute(pieces[0], "mp", near[2])]
    gain_row = gain.reshape(1, feat)

    step = min(4, row_blocks)
    shapes = [
        (per_row // 2 * BLK, lanes),
        (BLK, per_row * BLK),
        (per_row * HALF, lanes),
        (BLK, per_row * BLK),
    ]
    a_in, b_in, p_out, a_out = pl.pallas_call(
        prepare_kernel,
        out_shape=[jax.ShapeDtypeStruct((row_blocks, *shape), BF16) for shape in shapes],
        grid=(row_blocks // step,),
        in_specs=[pl.BlockSpec(memory_space=pltpu.SMEM)]
        + [pl.BlockSpec((step * per_row, BLK * BLK), lambda r: (r, 0))] * 2,
        out_specs=[pl.BlockSpec((step, *shape), lambda r: (r, 0, 0)) for shape in shapes],
        scratch_shapes=[
            pltpu.VMEM((per_row * HALF, per_row * HALF), BF16),
            pltpu.VMEM((lanes, 2 * lanes), BF16),
        ],
        compiler_params=pltpu.CompilerParams(vmem_limit_bytes=24 * MIB),
        cost_estimate=pl.CostEstimate(
            flops=8 * mm, bytes_accessed=12 * kept * BLK * BLK, transcendentals=0
        ),
        name="prepare",
    )(
        plan,
        pltpu.with_memory_space_constraint(w_in, pltpu.HBM),
        pltpu.with_memory_space_constraint(w_out, pltpu.HBM),
    )

    late, near_piece, gathered, p_out = lax.optimization_barrier(
        (pieces[1:], near_piece, gathered, p_out)
    )
    column = jnp.concatenate(late, axis=0)
    far_pieces = [column] + [lax.ppermute(column, "mp", near[q]) for q in (1, 2)]
    near_piece = [
        near_piece[0],
        lax.ppermute(near_piece[0], "mp", near[1]),
        near_piece[1],
        lax.ppermute(near_piece[1], "mp", near[1]),
    ]

    hidden_f32 = pltpu.VMEM((col_blocks, BLK, tok), F32)
    turned = pltpu.VMEM((feat, tok), BF16)

    def hidden_bf16(*chunks):
        return jax.ShapeDtypeStruct((*chunks, col_blocks, BLK, tok), BF16)

    def flat(chunks):
        return jax.ShapeDtypeStruct((chunks * tok, feat), BF16)

    def call(kernel, out_shape, scratch, limit, flops, transcendentals, *args):
        return pl.pallas_call(
            kernel,
            out_shape=out_shape,
            grid_spec=pltpu.PrefetchScalarGridSpec(
                num_scalar_prefetch=1,
                grid=(),
                in_specs=[whole] * (len(args) - 1),
                out_specs=[whole] * len(out_shape),
                scratch_shapes=scratch,
            ),
            compiler_params=pltpu.CompilerParams(vmem_limit_bytes=limit * MIB),
            cost_estimate=pl.CostEstimate(
                flops=flops, bytes_accessed=flops // (4 * tok), transcendentals=transcendentals
            ),
            name=(kernel.func if isinstance(kernel, functools.partial) else kernel).__name__,
        )(*args)

    scratch = [turned, turned, hidden_f32, hidden_f32]

    def chunk_scratch(chunks):
        return [pltpu.VMEM((chunks, feat, tok), BF16)] * 2 + [hidden_f32] * 2

    act, gp_own, n_own = call(
        local_kernel, [hidden_bf16(), hidden_bf16(), flat(1)], scratch, 32, 8 * mm, tok * hidden,
        plan, gain_row, *gathered, a_in, p_out,
    )
    far_pieces[2], n_own = lax.optimization_barrier((far_pieces[2], n_own))
    far_pieces.append(lax.ppermute(far_pieces[2], "mp", near[1]))
    gp_near, n_near = call(
        chunk_kernel, [hidden_bf16(1), flat(1)], chunk_scratch(1), 32, 8 * mm, tok * hidden // 2,
        plan, gain_row, *near_piece, a_in, p_out,
    )
    gp_far, n_far = call(
        chunk_kernel, [hidden_bf16(z_count - 2), flat(z_count - 2)], chunk_scratch(z_count - 2), 32, 16 * mm, tok * hidden,
        plan, gain_row, *far_pieces, a_in, p_out,
    )

    def blocks(list_row, dtype, flops, plan):
        return call(
            functools.partial(block_kernel, list_row, scale),
            [jax.ShapeDtypeStruct((cap + 1, HALF, lanes), dtype)],
            [],
            16, flops, 0,
            plan, gp_own, gp_near, gp_far, n_own, n_near, n_far, p_out,
        )[0]

    for_peer = blocks(2, BF16, 2 * mm, plan)
    for_peer, plan_later, act = lax.optimization_barrier((for_peer, plan, act))
    arrived = lax.ppermute(for_peer, "dp", across_x)
    parts = call(
        contract_kernel,
        [jax.ShapeDtypeStruct((2 * tok, width), BF16)] * mp_count,
        [turned, turned],
        16, 0, 0,
        plan_later, act, gp_own, b_in, a_out,
    )
    for_own = blocks(6, F32, 0, plan_later)
    summed = [parts[0]] + [lax.ppermute(parts[q], "mp", near[q]) for q in range(1, mp_count)]
    steps = 2
    own_rows = pl.BlockSpec((cap // steps, HALF, lanes), lambda i: (i, 0, 0))
    token_rows = pl.BlockSpec((2 * tok, width), lambda i: (0, 0))
    result = pl.BlockSpec((tok, width), lambda i: (0, 0))
    branch, grad_normed, owned_grad = pl.pallas_call(
        finish_kernel,
        out_shape=[
            jax.ShapeDtypeStruct((tok, width), BF16),
            jax.ShapeDtypeStruct((tok, width), BF16),
            jax.ShapeDtypeStruct((cap, BLK * BLK), F32),
        ],
        grid=(steps,),
        in_specs=[own_rows] * 2 + [token_rows] * mp_count,
        out_specs=[result, result, pl.BlockSpec((cap // steps, BLK * BLK), lambda i: (i, 0))],
        compiler_params=pltpu.CompilerParams(vmem_limit_bytes=16 * MIB),
        cost_estimate=pl.CostEstimate(flops=0, bytes_accessed=0, transcendentals=0),
        name="finish",
    )(for_own, arrived, *summed)
    return (branch, grad_normed, owned_grad[None])


def sum_sources(received):
    return jnp.sum(received, axis=0)


def body(x_in, gain, w_in, w_out, grad_out, block_cols, slots):
    whole_x, whole_grad = (
        lax.all_gather(x_in, "mp", axis=1, tiled=True),
        lax.all_gather(grad_out, "mp", axis=1, tiled=True),
    )
    tok_rows = whole_x.shape[0]
    feat_width = whole_x.shape[1]
    row_blocks = feat_width // BLK
    kept_count = w_in.shape[0]
    per_row = kept_count // row_blocks
    col_blocks = FF // lax.axis_size("mp") // BLK
    col_ids = block_cols[0]
    slot_ids = slots[0]
    x_float = whole_x.astype(jnp.float32)
    inv_rms = lax.rsqrt(jnp.mean(x_float * x_float, axis=-1, keepdims=True) + norm_eps)
    normed = (x_float * inv_rms * gain).astype(jnp.bfloat16)
    normed_cols = normed.reshape(tok_rows, row_blocks, BLK).transpose(1, 2, 0)
    grad_cols = whole_grad.reshape(tok_rows, row_blocks, BLK).transpose(1, 2, 0)
    in_blocks = w_in.reshape(row_blocks, per_row, BLK, BLK)
    out_blocks = w_out.reshape(row_blocks, per_row, BLK, BLK)
    col_onehot = (col_ids[None, :] == jnp.arange(col_blocks, dtype=jnp.int32)[:, None]).astype(
        jnp.float32
    )
    pre_parts = jnp.einsum(
        "rkbc,rbt->rkct", in_blocks, normed_cols, preferred_element_type=jnp.float32
    )
    pre_act = jnp.dot(
        col_onehot,
        pre_parts.reshape(kept_count, BLK * tok_rows),
        precision=lax.Precision.HIGHEST,
        preferred_element_type=jnp.float32,
    )
    pre_act = pre_act.reshape(col_blocks, BLK, tok_rows)
    activation = gelu_value(pre_act).astype(jnp.bfloat16)
    act_blocks = jnp.take(activation, col_ids, axis=0).reshape(row_blocks, per_row, BLK, tok_rows)
    branch_cols = jnp.einsum(
        "rkcb,rkct->rbt", out_blocks, act_blocks, preferred_element_type=jnp.float32
    )
    branch_part = branch_cols.transpose(2, 0, 1).reshape(tok_rows, feat_width)
    branch = lax.psum_scatter(branch_part, "mp", scatter_dimension=1, tiled=True).astype(
        jnp.bfloat16
    )
    act_parts = jnp.einsum(
        "rkcb,rbt->rkct", out_blocks, grad_cols, preferred_element_type=jnp.float32
    )
    grad_act = jnp.dot(
        col_onehot,
        act_parts.reshape(kept_count, BLK * tok_rows),
        precision=lax.Precision.HIGHEST,
        preferred_element_type=jnp.float32,
    )
    grad_act = grad_act.reshape(col_blocks, BLK, tok_rows)
    grad_pre = (grad_act * gelu_slope(pre_act)).astype(jnp.bfloat16)
    pre_blocks = jnp.take(grad_pre, col_ids, axis=0).reshape(row_blocks, per_row, BLK, tok_rows)
    dp_count = lax.axis_size("dp")
    weight_scale = 1.0 / math.sqrt(tok_rows * dp_count)
    block_terms = jnp.einsum(
        "rkct,rbt->rkcb", pre_blocks, normed_cols, preferred_element_type=jnp.float32
    )
    block_partial = (block_terms * weight_scale).reshape(kept_count, BLK * BLK)
    capacity = 2 * kept_count // dp_count
    outgoing = (
        jnp.zeros((dp_count * capacity, BLK * BLK), jnp.float32).at[slot_ids].set(block_partial)
    )
    outgoing = outgoing.reshape(dp_count, capacity, BLK * BLK)
    owned_grad = sum_sources(
        lax.all_to_all(
            outgoing.astype(jnp.bfloat16), "dp", split_axis=0, concat_axis=0, tiled=True
        ).astype(outgoing.dtype)
    )
    normed_part = jnp.einsum(
        "rkbc,rkct->rbt", in_blocks, pre_blocks, preferred_element_type=jnp.float32
    )
    normed_part = normed_part.transpose(2, 0, 1).reshape(tok_rows, feat_width)
    grad_normed = lax.psum_scatter(normed_part, "mp", scatter_dimension=1, tiled=True).astype(
        jnp.bfloat16
    )
    return (branch, grad_normed, owned_grad[None])


def solution(mesh):
    placed = (
        P("dp", "mp"),
        P(),
        P("mp", None),
        P("mp", None),
        P("dp", "mp"),
        P("mp", None),
        P("mp", None),
    )
    fits = mesh.shape["dp"] == 8 and mesh.shape["mp"] == 4
    return jax.shard_map(
        fast_body if fits else body,
        mesh=mesh,
        in_specs=placed,
        out_specs=(P("dp", "mp"), P("dp", "mp"), P("mp", "dp", None)),
        check_vma=False,
    )
```

```python
import functools
import math

import jax
import jax.numpy as jnp
from jax import lax
from jax.experimental import pallas as pl
from jax.experimental.pallas import tpu as pltpu
from jax.sharding import PartitionSpec as P

FF = 32768
BLK = 64
HALF = BLK // 2
GROUP = 4
FIRST = 1024
BATCH = 10
BEND = 16


norm_eps = 1e-06
tanh_coef = 0.7978845608028654

F32 = jnp.float32
BF16 = jnp.bfloat16
MIB = 1024 * 1024


def gelu_value(pre_act):
    cubic = pre_act * pre_act * pre_act
    slope_arg = jnp.tanh(tanh_coef * (pre_act + 0.044715 * cubic))
    return 0.5 * pre_act * (1.0 + slope_arg)


def gelu_slope(pre_act):
    cubic = pre_act * pre_act * pre_act
    slope_arg = jnp.tanh(tanh_coef * (pre_act + 0.044715 * cubic))
    inner = tanh_coef * (1.0 + 0.134145 * pre_act * pre_act)
    return 0.5 * (1.0 + slope_arg) + 0.5 * pre_act * (1.0 - slope_arg * slope_arg) * inner


def gelu_both(v):
    square = v * v
    th = jnp.tanh(v * (tanh_coef + (tanh_coef * 0.044715) * square))
    gate = 0.5 + 0.5 * th
    inner = 2.0 * tanh_coef + (2.0 * tanh_coef * 0.134145) * square
    return v * gate, gate + v * (gate - gate * gate) * inner


def dot(a, b, dims=((1,), (0,))):
    return lax.dot_general(a, b, (dims, ((), ())), preferred_element_type=F32)


def iota(shape, axis):
    return lax.broadcasted_iota(jnp.int32, shape, axis)


def even_first(width):
    row, col = iota((width, width), 0), iota((width, width), 1)
    inside = row & (BLK - 1)
    target = (row - inside) + (inside & 1) * HALF + (inside >> 1)
    return jnp.where(col == target, 1.0, 0.0).astype(BF16)


def stack_kernel(x_ref, grad_ref, both_ref):
    tok = x_ref.shape[0]
    both_ref[:tok, :] = x_ref[...]
    both_ref[tok:, :] = grad_ref[...]


def plan_kernel(cap, col_blocks, row_blocks, cols_ref, slots_ref, out_ref):
    kept = cols_ref.shape[1]
    per_row = kept // row_blocks
    me = lax.axis_index("dp")
    cols, slots = cols_ref[...], slots_ref[...]
    owner = lax.div(slots, jnp.int32(cap))
    own = jnp.where(owner == me, 1.0, 0.0)
    peer = jnp.where(owner == (me ^ 1), 1.0, 0.0)
    needed = jnp.max(
        jnp.where(cols == iota((col_blocks, kept), 0), own + peer, 0.0), axis=1, keepdims=True
    )

    def to_column(row):
        size = row.shape[1]
        eye = iota((size, size), 0) == iota((size, size), 1)
        return jnp.sum(jnp.where(eye, row, 0.0), axis=1, keepdims=True)

    def to_row(column):
        size = column.shape[0]
        eye = iota((size, size), 0) == iota((size, size), 1)
        return jnp.sum(jnp.where(eye, column, 0.0), axis=0, keepdims=True)

    def listed(flags_r, flags_c):
        size = flags_r.shape[1]
        before = iota((size, size), 1) < iota((size, size), 0)
        place = jnp.sum(jnp.where(before, flags_r, 0.0), axis=1, keepdims=True)
        hit = (place == iota((size, kept), 1).astype(F32)) & (flags_c > 0)
        index = iota((size, 1), 0).astype(F32)
        return jnp.sum(jnp.where(hit, index, 0.0), axis=0, keepdims=True)

    cols_r = cols.astype(F32)
    cols_c = to_column(cols_r)
    earlier = iota((kept, kept), 1) < iota((kept, kept), 0)
    seen = jnp.max(jnp.where(earlier & (cols_r == cols_c), 1.0, 0.0), axis=1, keepdims=True)
    peer_c, own_c = to_column(peer), to_column(own)
    pair_end = iota((kept, kept), 0) < 2 * per_row * iota((kept, kept), 1)

    def starts(flags_c):
        return jnp.sum(jnp.where(pair_end, flags_c, 0.0), axis=0, keepdims=True)

    rows = [
        cols_r + FIRST * (1.0 - to_row(seen)),
        (slots - owner * cap).astype(F32),
        listed(peer, peer_c),
        starts(peer_c),
        listed(to_row(needed), needed),
        jnp.sum(needed, axis=0, keepdims=True),
        listed(own, own_c),
        starts(own_c),
    ]
    for index, row in enumerate(rows):
        out_ref[index : index + 1, :] = jnp.broadcast_to(row, (1, kept)).astype(jnp.int32)


def prepare_kernel(plan_ref, win_ref, wout_ref, a_in, b_in, p_out, a_out, order, both):
    count = a_in.shape[0]
    per_row, length = win_ref.shape[0] // count, win_ref.shape[1]
    lanes = 2 * BLK
    rows = per_row * HALF

    @pl.when(pl.program_id(0) == 0)
    def _():
        row, col = iota((rows, rows), 0), iota((rows, rows), 1)
        source = (row & (HALF - 1)) * per_row + lax.div(row, jnp.int32(HALF))
        order[...] = jnp.where(col == source, 1.0, 0.0).astype(BF16)
        row, col = iota((lanes, lanes), 0), iota((lanes, lanes), 1)
        swap = jnp.where(((col + BLK) & (lanes - 1)) == row, 1.0, 0.0).astype(BF16)
        perm = even_first(lanes)
        both[:, :lanes] = perm
        both[:, lanes:] = dot(perm, swap).astype(BF16)

    def by_block(ref):
        stacked = [
            jnp.concatenate(
                [
                    ref[n * per_row : (n + 1) * per_row, j * lanes : (j + 1) * lanes]
                    for j in range(length // lanes)
                ],
                axis=0,
            )
            for n in range(count)
        ]
        return dot(order[...], jnp.concatenate(stacked, axis=1)).astype(BF16)

    ordered_in, ordered_out = by_block(win_ref), by_block(wout_ref)
    left = iota((HALF, lanes), 1) < BLK
    left2 = iota((BLK, lanes), 1) < BLK
    for n in range(count):
        of_n = slice(n * lanes, (n + 1) * lanes)
        kept_in = dot(ordered_in[:, of_n], both[...])
        kept_out = ordered_out[:, of_n]
        p_out[n] = kept_out
        for pair in range(per_row // 2):
            first = kept_in[2 * pair * HALF : (2 * pair + 1) * HALF]
            second = kept_in[(2 * pair + 1) * HALF : (2 * pair + 2) * HALF]
            at = slice(pair * lanes, (pair + 1) * lanes)
            b_in[n, :HALF, at] = jnp.where(left, first[:, :lanes], second[:, lanes:]).astype(BF16)
            b_in[n, HALF:, at] = jnp.where(left, first[:, lanes:], second[:, :lanes]).astype(BF16)
        for quad in range(per_row // GROUP):
            rows_of = slice(quad * lanes, (quad + 1) * lanes)
            straight, swapped = kept_in[rows_of, :lanes], kept_in[rows_of, lanes:]
            pairs = jnp.concatenate(
                [
                    jnp.where(left2, straight[:BLK], swapped[BLK:]),
                    jnp.where(left2, swapped[:BLK], straight[BLK:]),
                ],
                axis=0,
            )
            a_in[n, rows_of, :] = pairs.astype(BF16).T
            turned = kept_out[rows_of].T
            a_out[n, :, rows_of] = turned[:BLK]
            a_out[n, :, rows + quad * lanes : rows + (quad + 1) * lanes] = turned[BLK:]


def load_tokens(pieces, tok, gain_ref, perm, n_s, nt_s, gt_s, base):
    mine = lax.axis_index("mp")
    width = pieces[0][0].shape[1]
    values, total = [], 0.0
    for ref, first in pieces:
        value = ref[first : first + tok, :].astype(F32)
        values.append(value)
        total = total + jnp.sum(value * value, axis=-1, keepdims=True)
    inv_rms = lax.rsqrt(total / (width * len(pieces)) + norm_eps)
    for q, (ref, first) in enumerate(pieces):
        at = pl.ds(pl.multiple_of((mine ^ q) * width, width), width)
        normed = (values[q] * inv_rms * gain_ref[:, at]).astype(BF16)
        n_s[base : base + tok, at] = normed
        nt_s[at, :] = dot(normed, perm).astype(BF16).T
        gt_s[at, :] = ref[first + tok : first + 2 * tok, :].T


def expand(plan, a_in, p_out, nt_s, gt_s, acc_v, acc_a):
    row_blocks = a_in.shape[0]
    tok = nt_s.shape[1]
    per_row = p_out.shape[1] // HALF
    gap = jnp.zeros((HALF, tok), BF16)
    gap2 = jnp.zeros((BLK, tok), BF16)

    def step(r, carry):
        at = pl.ds(pl.multiple_of(r * BLK, BLK), BLK)
        normed, cot = nt_s[at, :], gt_s[at, :]
        spread = []
        for a in (0, 1):
            part = normed[a * HALF : (a + 1) * HALF]
            spread.append(jnp.concatenate([part, gap], axis=1))
            spread.append(jnp.concatenate([gap, part], axis=1))
        terms_v = dot(a_in[r], jnp.concatenate(spread, axis=0))
        cots = jnp.concatenate(
            [jnp.concatenate([cot, gap2], axis=1), jnp.concatenate([gap2, cot], axis=1)], axis=0
        )
        terms_a = dot(p_out[r], cots)
        for quad in range(per_row // GROUP):
            new = []
            for u in range(GROUP):
                k = quad * GROUP + u
                code = plan[0, r * per_row + k]
                c, first = code & (FIRST - 1), code >= FIRST
                rows = terms_v[(k // 2) * BLK : (k // 2 + 1) * BLK]
                v = rows[:, (k % 2) * tok : (k % 2 + 1) * tok]
                rows = terms_a[k * HALF : (k + 1) * HALF]
                a = jnp.concatenate([rows[:, :tok], rows[:, tok:]], axis=0)
                v = jnp.where(first, v, acc_v[c] + v)
                a = jnp.where(first, a, acc_a[c] + a)
                new.append((c, v, a))
            for c, v, a in new:
                acc_v[c] = v
                acc_a[c] = a
        return carry

    lax.fori_loop(0, row_blocks, step, 0, unroll=16)


def local_kernel(
    plan, gain_ref, s0, s1, s2, s3, a_in, p_out, act_ref, gp_ref, n_ref, nt_s, gt_s, acc_v, acc_a
):
    tok = n_ref.shape[0]
    perm = even_first(s0.shape[1])
    load_tokens([(ref, 0) for ref in (s0, s1, s2, s3)], tok, gain_ref, perm, n_ref, nt_s, gt_s, 0)
    expand(plan, a_in, p_out, nt_s, gt_s, acc_v, acc_a)

    def bend(c, carry):
        value, slope = gelu_both(acc_v[c])
        act_ref[c] = value.astype(BF16)
        gp_ref[c] = (acc_a[c] * slope).astype(BF16)
        return carry

    lax.fori_loop(0, gp_ref.shape[0], bend, 0, unroll=8)


def contract_kernel(plan, act_ref, gp_ref, b_in, a_out, o0, o1, o2, o3, br_s, gn_s):
    tok, width = o0.shape[0] // 2, o0.shape[1]
    row_blocks, per_row = b_in.shape[0], b_in.shape[2] // BLK
    perm = even_first(width)

    def contract(r, carry):
        at = pl.ds(pl.multiple_of(r * BLK, BLK), BLK)
        ids = [plan[0, r * per_row + k] & (FIRST - 1) for k in range(per_row)]
        acts = [act_ref[c, a * HALF : (a + 1) * HALF, :] for a in (0, 1) for c in ids]
        br_s[at, :] = dot(a_out[r], jnp.concatenate(acts, axis=0)).astype(BF16)
        grads = [gp_ref[c] for c in ids]
        gn_s[at, :] = dot(b_in[r], jnp.concatenate(grads, axis=0)).astype(BF16)
        return carry

    lax.fori_loop(0, row_blocks, contract, 0, unroll=16)
    mine = lax.axis_index("mp")
    for q, out in enumerate((o0, o1, o2, o3)):
        at = pl.ds(pl.multiple_of((mine ^ q) * width, width), width)
        out[:tok, :] = br_s[at, :].T
        out[tok:, :] = dot(gn_s[at, :].T, perm, ((1,), (1,))).astype(BF16)


def chunk_kernel(
    plan, gain_ref, s0, s1, s2, s3, a_in, p_out, gp_ref, n_ref, nt_s, gt_s, acc_v, acc_a
):
    chunks = gp_ref.shape[0]
    tok = n_ref.shape[0] // chunks
    perm = even_first(s0.shape[1])
    count = plan[5, 0]
    for j in range(chunks):
        pieces = [(ref, 2 * tok * j) for ref in (s0, s1, s2, s3)]
        load_tokens(pieces, tok, gain_ref, perm, n_ref, nt_s.at[j], gt_s.at[j], j * tok)
    for j in range(chunks):
        expand(plan, a_in, p_out, nt_s.at[j], gt_s.at[j], acc_v, acc_a)

        def bend(i, carry):
            for u in range(BEND):
                c = plan[4, jnp.minimum(i * BEND + u, count - 1)]
                _, slope = gelu_both(acc_v[c])
                gp_ref[j, c] = (acc_a[c] * slope).astype(BF16)
            return carry

        lax.fori_loop(0, (count + BEND - 1) // BEND, bend, 0)


def block_kernel(
    list_row, scale, plan, gp0, gp1, gp2, n0, n1, n2, p_out, found
):
    per_row = p_out.shape[1] // HALF
    lanes = 2 * BLK
    pairs = p_out.shape[0] // 2
    cap = found.shape[0] - 1
    left = iota((HALF, lanes), 1) < BLK
    found[...] = jnp.zeros_like(found)

    def form(pair, first):
        end = plan[list_row + 1, pair + 1]
        at_lane = pl.ds(pl.multiple_of(pair * lanes, lanes), lanes)
        ids = [
            plan[list_row, jnp.maximum(jnp.minimum(first + u, end - 1), 0)] for u in range(BATCH)
        ]
        grads = []
        for k in ids:
            c = plan[0, k] & (FIRST - 1)
            chunks = [gp0[c]] + [ref[j, c] for ref in (gp1, gp2) for j in range(ref.shape[0])]
            grads.append(jnp.concatenate(chunks, axis=1))
        normed = jnp.concatenate([ref[:, at_lane] for ref in (n0, n1, n2)], axis=0)
        blocks = dot(jnp.concatenate(grads, axis=0), normed) * scale
        done = []
        for u, k in enumerate(ids):
            odd = (lax.div(k, jnp.int32(per_row)) & 1) == 1
            top = blocks[u * BLK : u * BLK + HALF]
            low = blocks[u * BLK + HALF : (u + 1) * BLK]
            top = jnp.where(odd, pltpu.roll(top, BLK, 1), top)
            low = jnp.where(odd, low, pltpu.roll(low, BLK, 1))
            slot = jnp.where(first < end, plan[1, k], cap)
            done.append((slot, jnp.where(left, top, low).astype(found.dtype)))
        for slot, value in done:
            found[slot] = value

    def begin(pair, carry):
        form(pair, plan[list_row + 1, pair])
        return carry

    lax.fori_loop(0, pairs, begin, 0, unroll=8)

    def finish(pair, carry):
        begin, end = plan[list_row + 1, pair], plan[list_row + 1, pair + 1]

        def more(i, carry):
            form(pair, begin + i * BATCH)
            return carry

        return lax.fori_loop(1, (end - begin + BATCH - 1) // BATCH, more, carry)

    lax.fori_loop(0, pairs, finish, 0)


def finish_kernel(own_ref, arrived_ref, s0, s1, s2, s3, branch_ref, normed_ref, out_ref):
    lanes = own_ref.shape[2]
    rows = 8
    for first in range(0, own_ref.shape[0], rows):
        at = slice(first, first + rows)
        blocks = own_ref[at] + arrived_ref[at].astype(F32)
        turned = jnp.swapaxes(blocks, 0, 1)
        for j in range(turned.shape[0]):
            out_ref[at, j * lanes : (j + 1) * lanes] = turned[j]

    @pl.when(pl.program_id(0) == 0)
    def _():
        tok = branch_ref.shape[0]
        for out, base in ((branch_ref, 0), (normed_ref, tok)):
            total = sum(ref[base : base + tok, :].astype(F32) for ref in (s0, s1, s2, s3))
            out[...] = total.astype(BF16)


def fast_body(x_in, gain, w_in, w_out, grad_out, block_cols, slots):
    dp_count, mp_count = lax.axis_size("dp"), lax.axis_size("mp")
    tok, width = x_in.shape
    feat = width * mp_count
    kept = w_in.shape[0]
    row_blocks = feat // BLK
    per_row = kept // row_blocks
    hidden = FF // mp_count
    col_blocks = hidden // BLK
    lanes = 2 * BLK
    cap = 2 * kept // dp_count
    scale = 1.0 / math.sqrt(tok * dp_count)
    across_x = [(i, i ^ 1) for i in range(dp_count)]
    near = [[(i, i ^ q) for i in range(mp_count)] for q in range(mp_count)]
    z_count = dp_count // 2
    along_z = [[(i, i ^ (2 * j)) for i in range(dp_count)] for j in (1, 3, 2)]

    whole = pl.BlockSpec(memory_space=pltpu.VMEM)
    mm = 2 * tok * kept * BLK * BLK

    own = pl.pallas_call(
        stack_kernel,
        out_shape=jax.ShapeDtypeStruct((2 * tok, width), BF16),
        cost_estimate=pl.CostEstimate(flops=0, bytes_accessed=8 * tok * width, transcendentals=0),
        name="stack",
    )(x_in, grad_out)
    pieces = [lax.ppermute(own, "dp", along_z[0])]
    over_core, own_late = lax.optimization_barrier((lax.ppermute(own, "mp", near[1]), own))
    over_y = lax.ppermute(own_late, "mp", near[2])
    gathered = [own, over_core, over_y, lax.ppermute(own_late, "mp", near[3])]
    pieces += [lax.ppermute(own_late, "dp", hop) for hop in along_z[1:]]
    pieces[0], cols_late, slots_late = lax.optimization_barrier((pieces[0], block_cols, slots))
    plan = pl.pallas_call(
        functools.partial(plan_kernel, cap, col_blocks, row_blocks),
        out_shape=jax.ShapeDtypeStruct((8, kept), jnp.int32),
        cost_estimate=pl.CostEstimate(flops=4_000_000, bytes_accessed=16384, transcendentals=0),
        name="plan",
    )(cols_late, slots_late)
    near_piece = [pieces[0], lax.ppermute(pieces[0], "mp", near[2])]
    gain_row = gain.reshape(1, feat)

    step = min(4, row_blocks)
    shapes = [
        (per_row // 2 * BLK, lanes),
        (BLK, per_row * BLK),
        (per_row * HALF, lanes),
        (BLK, per_row * BLK),
    ]
    a_in, b_in, p_out, a_out = pl.pallas_call(
        prepare_kernel,
        out_shape=[jax.ShapeDtypeStruct((row_blocks, *shape), BF16) for shape in shapes],
        grid=(row_blocks // step,),
        in_specs=[pl.BlockSpec(memory_space=pltpu.SMEM)]
        + [pl.BlockSpec((step * per_row, BLK * BLK), lambda r: (r, 0))] * 2,
        out_specs=[pl.BlockSpec((step, *shape), lambda r: (r, 0, 0)) for shape in shapes],
        scratch_shapes=[
            pltpu.VMEM((per_row * HALF, per_row * HALF), BF16),
            pltpu.VMEM((lanes, 2 * lanes), BF16),
        ],
        compiler_params=pltpu.CompilerParams(vmem_limit_bytes=24 * MIB),
        cost_estimate=pl.CostEstimate(
            flops=8 * mm, bytes_accessed=12 * kept * BLK * BLK, transcendentals=0
        ),
        name="prepare",
    )(
        plan,
        pltpu.with_memory_space_constraint(w_in, pltpu.HBM),
        pltpu.with_memory_space_constraint(w_out, pltpu.HBM),
    )

    late, near_piece, gathered, p_out = lax.optimization_barrier(
        (pieces[1:], near_piece, gathered, p_out)
    )
    column = jnp.concatenate(late, axis=0)
    far_pieces = [column] + [lax.ppermute(column, "mp", near[q]) for q in (1, 2)]
    near_piece = [
        near_piece[0],
        lax.ppermute(near_piece[0], "mp", near[1]),
        near_piece[1],
        lax.ppermute(near_piece[1], "mp", near[1]),
    ]

    hidden_f32 = pltpu.VMEM((col_blocks, BLK, tok), F32)
    turned = pltpu.VMEM((feat, tok), BF16)

    def hidden_bf16(*chunks):
        return jax.ShapeDtypeStruct((*chunks, col_blocks, BLK, tok), BF16)

    def flat(chunks):
        return jax.ShapeDtypeStruct((chunks * tok, feat), BF16)

    def call(kernel, out_shape, scratch, limit, flops, transcendentals, *args):
        return pl.pallas_call(
            kernel,
            out_shape=out_shape,
            grid_spec=pltpu.PrefetchScalarGridSpec(
                num_scalar_prefetch=1,
                grid=(),
                in_specs=[whole] * (len(args) - 1),
                out_specs=[whole] * len(out_shape),
                scratch_shapes=scratch,
            ),
            compiler_params=pltpu.CompilerParams(vmem_limit_bytes=limit * MIB),
            cost_estimate=pl.CostEstimate(
                flops=flops, bytes_accessed=flops // (4 * tok), transcendentals=transcendentals
            ),
            name=(kernel.func if isinstance(kernel, functools.partial) else kernel).__name__,
        )(*args)

    scratch = [turned, turned, hidden_f32, hidden_f32]

    def chunk_scratch(chunks):
        return [pltpu.VMEM((chunks, feat, tok), BF16)] * 2 + [hidden_f32] * 2

    act, gp_own, n_own = call(
        local_kernel, [hidden_bf16(), hidden_bf16(), flat(1)], scratch, 32, 8 * mm, tok * hidden,
        plan, gain_row, *gathered, a_in, p_out,
    )
    far_pieces[2], n_own = lax.optimization_barrier((far_pieces[2], n_own))
    far_pieces.append(lax.ppermute(far_pieces[2], "mp", near[1]))
    gp_near, n_near = call(
        chunk_kernel, [hidden_bf16(1), flat(1)], chunk_scratch(1), 32, 8 * mm, tok * hidden // 2,
        plan, gain_row, *near_piece, a_in, p_out,
    )
    gp_far, n_far = call(
        chunk_kernel, [hidden_bf16(z_count - 2), flat(z_count - 2)], chunk_scratch(z_count - 2), 32, 16 * mm, tok * hidden,
        plan, gain_row, *far_pieces, a_in, p_out,
    )

    def blocks(list_row, dtype, flops, plan):
        return call(
            functools.partial(block_kernel, list_row, scale),
            [jax.ShapeDtypeStruct((cap + 1, HALF, lanes), dtype)],
            [],
            16, flops, 0,
            plan, gp_own, gp_near, gp_far, n_own, n_near, n_far, p_out,
        )[0]

    for_peer = blocks(2, BF16, 2 * mm, plan)
    for_peer, plan_later, act = lax.optimization_barrier((for_peer, plan, act))
    arrived = lax.ppermute(for_peer, "dp", across_x)
    parts = call(
        contract_kernel,
        [jax.ShapeDtypeStruct((2 * tok, width), BF16)] * mp_count,
        [turned, turned],
        16, 0, 0,
        plan_later, act, gp_own, b_in, a_out,
    )
    for_own = blocks(6, F32, 0, plan_later)
    summed = [parts[0]] + [lax.ppermute(parts[q], "mp", near[q]) for q in range(1, mp_count)]
    steps = 2
    own_rows = pl.BlockSpec((cap // steps, HALF, lanes), lambda i: (i, 0, 0))
    token_rows = pl.BlockSpec((2 * tok, width), lambda i: (0, 0))
    result = pl.BlockSpec((tok, width), lambda i: (0, 0))
    branch, grad_normed, owned_grad = pl.pallas_call(
        finish_kernel,
        out_shape=[
            jax.ShapeDtypeStruct((tok, width), BF16),
            jax.ShapeDtypeStruct((tok, width), BF16),
            jax.ShapeDtypeStruct((cap, BLK * BLK), F32),
        ],
        grid=(steps,),
        in_specs=[own_rows] * 2 + [token_rows] * mp_count,
        out_specs=[result, result, pl.BlockSpec((cap // steps, BLK * BLK), lambda i: (i, 0))],
        compiler_params=pltpu.CompilerParams(vmem_limit_bytes=16 * MIB),
        cost_estimate=pl.CostEstimate(flops=0, bytes_accessed=0, transcendentals=0),
        name="finish",
    )(for_own, arrived, *summed)
    return (branch, grad_normed, owned_grad[None])


def sum_sources(received):
    return jnp.sum(received, axis=0)


def body(x_in, gain, w_in, w_out, grad_out, block_cols, slots):
    whole_x, whole_grad = (
        lax.all_gather(x_in, "mp", axis=1, tiled=True),
        lax.all_gather(grad_out, "mp", axis=1, tiled=True),
    )
    tok_rows = whole_x.shape[0]
    feat_width = whole_x.shape[1]
    row_blocks = feat_width // BLK
    kept_count = w_in.shape[0]
    per_row = kept_count // row_blocks
    col_blocks = FF // lax.axis_size("mp") // BLK
    col_ids = block_cols[0]
    slot_ids = slots[0]
    x_float = whole_x.astype(jnp.float32)
    inv_rms = lax.rsqrt(jnp.mean(x_float * x_float, axis=-1, keepdims=True) + norm_eps)
    normed = (x_float * inv_rms * gain).astype(jnp.bfloat16)
    normed_cols = normed.reshape(tok_rows, row_blocks, BLK).transpose(1, 2, 0)
    grad_cols = whole_grad.reshape(tok_rows, row_blocks, BLK).transpose(1, 2, 0)
    in_blocks = w_in.reshape(row_blocks, per_row, BLK, BLK)
    out_blocks = w_out.reshape(row_blocks, per_row, BLK, BLK)
    col_onehot = (col_ids[None, :] == jnp.arange(col_blocks, dtype=jnp.int32)[:, None]).astype(
        jnp.float32
    )
    pre_parts = jnp.einsum(
        "rkbc,rbt->rkct", in_blocks, normed_cols, preferred_element_type=jnp.float32
    )
    pre_act = jnp.dot(
        col_onehot,
        pre_parts.reshape(kept_count, BLK * tok_rows),
        precision=lax.Precision.HIGHEST,
        preferred_element_type=jnp.float32,
    )
    pre_act = pre_act.reshape(col_blocks, BLK, tok_rows)
    activation = gelu_value(pre_act).astype(jnp.bfloat16)
    act_blocks = jnp.take(activation, col_ids, axis=0).reshape(row_blocks, per_row, BLK, tok_rows)
    branch_cols = jnp.einsum(
        "rkcb,rkct->rbt", out_blocks, act_blocks, preferred_element_type=jnp.float32
    )
    branch_part = branch_cols.transpose(2, 0, 1).reshape(tok_rows, feat_width)
    branch = lax.psum_scatter(branch_part, "mp", scatter_dimension=1, tiled=True).astype(
        jnp.bfloat16
    )
    act_parts = jnp.einsum(
        "rkcb,rbt->rkct", out_blocks, grad_cols, preferred_element_type=jnp.float32
    )
    grad_act = jnp.dot(
        col_onehot,
        act_parts.reshape(kept_count, BLK * tok_rows),
        precision=lax.Precision.HIGHEST,
        preferred_element_type=jnp.float32,
    )
    grad_act = grad_act.reshape(col_blocks, BLK, tok_rows)
    grad_pre = (grad_act * gelu_slope(pre_act)).astype(jnp.bfloat16)
    pre_blocks = jnp.take(grad_pre, col_ids, axis=0).reshape(row_blocks, per_row, BLK, tok_rows)
    dp_count = lax.axis_size("dp")
    weight_scale = 1.0 / math.sqrt(tok_rows * dp_count)
    block_terms = jnp.einsum(
        "rkct,rbt->rkcb", pre_blocks, normed_cols, preferred_element_type=jnp.float32
    )
    block_partial = (block_terms * weight_scale).reshape(kept_count, BLK * BLK)
    capacity = 2 * kept_count // dp_count
    outgoing = (
        jnp.zeros((dp_count * capacity, BLK * BLK), jnp.float32).at[slot_ids].set(block_partial)
    )
    outgoing = outgoing.reshape(dp_count, capacity, BLK * BLK)
    owned_grad = sum_sources(
        lax.all_to_all(
            outgoing.astype(jnp.bfloat16), "dp", split_axis=0, concat_axis=0, tiled=True
        ).astype(outgoing.dtype)
    )
    normed_part = jnp.einsum(
        "rkbc,rkct->rbt", in_blocks, pre_blocks, preferred_element_type=jnp.float32
    )
    normed_part = normed_part.transpose(2, 0, 1).reshape(tok_rows, feat_width)
    grad_normed = lax.psum_scatter(normed_part, "mp", scatter_dimension=1, tiled=True).astype(
        jnp.bfloat16
    )
    return (branch, grad_normed, owned_grad[None])


def solution(mesh):
    placed = (
        P("dp", "mp"),
        P(),
        P("mp", None),
        P("mp", None),
        P("dp", "mp"),
        P("mp", None),
        P("mp", None),
    )
    fits = mesh.shape["dp"] == 8 and mesh.shape["mp"] == 4
    return jax.shard_map(
        fast_body if fits else body,
        mesh=mesh,
        in_specs=placed,
        out_specs=(P("dp", "mp"), P("dp", "mp"), P("mp", "dp", None)),
        check_vma=False,
    )
```
